256 devices in a mesh: pipe: 8 (over z), expert: 16 (over y, x), dp: 2 (over core).
Axes of the slice: x: 4, y: 4, z: 8, core: 2. Of those that a mesh axis runs over, the one named last changes fastest.
Arguments:
- sent_down: bfloat16 [8, 512, 3584], P('pipe', 'expert'), may hold values from -6 to 6
- sent_up: bfloat16 [8, 512, 3584], P('pipe', 'expert'), may hold values from -6 to 6
- expert_ids: int32 [2, 8, 512, 2], P(None, 'pipe', 'expert'), may hold values from 0 to 7, all different within a row; in each aligned block of 32 rows (0 to 31, 32 to 63, ..., all dimensions but the last counted through in order) at most 16 rows name the same one
- router_logits: float32 [2, 8, 512, 2], P(None, 'pipe', 'expert'), may hold values from -6 to 6
- saved_gate_up: bfloat16 [2, 8, 16, 2, 256, 512], P(None, 'pipe', 'expert', None, None, 'dp'), may hold values from -6 to 6
- down_weight: bfloat16 [8, 16, 512, 3584], P('pipe', 'expert', 'dp'), may hold values from -0.09375 to 0.09375
Outputs:
- grad_gate_up: bfloat16 [2, 8, 16, 2, 256, 512], P(None, 'pipe', 'expert', None, None, 'dp')
- grad_down: bfloat16 [8, 16, 512, 3584], P('pipe', 'expert', 'dp')
- grad_logits: float32 [2, 8, 512, 2], P(None, 'pipe', 'expert')
The draws below stay inside these ranges and needn't reach their ends.
Inputs may be any that keep to these rules, and one draw needn't show every extreme that they name: `expert_ids`: in each aligned block of 32 tokens of a span and segment no expert is named by more than 16 tokens, a bound that some block reaches.
All inputs are finite; a program needn't handle non-finite values.
Results may differ from the reference program's by a relative error of at most 0.015.
Values may be sent and summed in bfloat16 or wider, within the bound.
No kernel may reach another device: no remote copies, remote signals or barrier semaphores. Data moves between devices by JAX's collectives and lax.ppermute only.
A program may use at most 64 MiB of HBM per device.

```python
import math
import jax
import jax.numpy as jnp
import numpy as np
from jax import lax

D = 3584
TOP = 2
TOK_C = 32
SEGMENTS = 8
GROUP = 2
EXPERTS = 8
HID_PART = 512
TOK_SEGMENT = 512
CAP = 16
ROWS = 256
N_EXPERT = 16


def shard_levels(stream_key, shape, split, smallest, high):
    factor_of, own = 1.0, jax.random.fold_in(stream_key, 6)
    for position, shards_of in split:
        steps = jnp.exp(jax.random.uniform(jax.random.fold_in(own, position), (shards_of,), jnp.float32, smallest / len(split), high / len(split)))
        factor_of = factor_of * jnp.repeat(steps, shape[position] // shards_of).reshape([-1 if axis == position else 1 for axis in range(len(shape))])
    return factor_of


def assign_block(key, own, number, rows, count, top, most, lean):
    order = jax.random.permutation(key, count)
    crowded, ordinary = portions_of(count, rows * top, most, lean, True), portions_of(count, rows * top, most, lean, False)
    places = jnp.arange(count)

    def named(sizes, rotation):
        used = int((sizes > 0).sum())
        fixed = max(1, used // 4)
        passed = fixed + (places - fixed + rotation * (used - fixed)) % max(1, count - fixed)
        return jnp.zeros((count,), jnp.int32).at[order[jnp.where(places < fixed, places, passed)]].set(jnp.asarray(sizes, jnp.int32))

    sizes = jnp.where(number % 4 == 0, named(crowded, number // 4), named(ordinary, number - number // 4 - 1))
    mixed = jax.random.permutation(jax.random.fold_in(own, 3), count)
    donor, taker = mixed[0:count // 2 * 2:2], mixed[1:count // 2 * 2:2]
    slack = jnp.minimum(sizes[donor] - 1, most - sizes[taker]) // 2
    slack = jnp.where((donor == order[0]) | (taker == order[0]) | (sizes[taker] == 0), 0, jnp.maximum(slack, 0))
    passed = jax.random.randint(jax.random.fold_in(own, 4), (count // 2,), 0, 1 << 20) % (slack + 1)
    sizes = sizes.at[donor].add(-passed).at[taker].add(passed)
    labels = jnp.searchsorted(jnp.cumsum(sizes), jnp.arange(rows * top), side="right").astype(jnp.int32)
    table = labels.reshape(top, rows).T
    table = table[jax.random.permutation(jax.random.fold_in(own, 1), rows)]
    rotation = jax.random.randint(jax.random.fold_in(own, 2), (rows, 1), 0, top)
    return jnp.take_along_axis(table, (jnp.arange(top)[None, :] + rotation) % top, axis=1)


def portions_of(count, total, reach, skew, full):
    loads = [(1 << 20) // math.isqrt(standing ** skew) + 1 for standing in range(1, count + 1)]
    largest = reach if full else min(reach, max(-(-total // count), total * loads[0] // sum(loads)))
    least = 1 if total - largest >= count - 1 else 0
    holding, surplus = [largest] + [least] * (count - 1), total - largest - least * (count - 1)
    while surplus > 0:
        candidates = [i for i in range(1, count) if holding[i] < largest] or [i for i in range(1, count) if holding[i] < reach]
        mass, left = sum([loads[i] for i in candidates]), surplus
        for i in candidates:
            addition = min(reach - holding[i], max(1, left * loads[i] // mass), surplus)
            holding[i] = holding[i] + addition
            surplus = surplus - addition
    return np.array(holding)


def centred(key, shape, scale, bound, cuts=(), kind=jnp.bfloat16):
    entries = scale * jax.random.normal(key, shape, jnp.float32)
    if cuts:
        entries = entries * shard_levels(key, shape, cuts, -0.22, 0.18)
    return jnp.clip(entries, -bound, bound).astype(kind)


def setup_inputs(seed: int = 0) -> dict:
    streams_of = jax.random.split(jax.random.key(seed), 7)
    sent_down = centred(streams_of[0], (SEGMENTS, TOK_SEGMENT, D), 1.0, 6.0, ((0, 8), (1, 16)))
    sent_up = centred(streams_of[1], (SEGMENTS, TOK_SEGMENT, D), 1.0, 6.0, ((0, 8), (1, 16)))
    expert_ids_keys = jax.random.split(jax.random.fold_in(streams_of[2], 1), 2 * SEGMENTS * TOK_SEGMENT // TOK_C)
    expert_ids_turns = jax.random.permutation(jax.random.fold_in(streams_of[2], 3), 2 * SEGMENTS * TOK_SEGMENT // TOK_C)
    expert_ids = jax.vmap(lambda own, number: assign_block(jax.random.fold_in(streams_of[2], 2), own, number, TOK_C, EXPERTS, TOP, CAP, 2))(expert_ids_keys, expert_ids_turns).reshape((2, SEGMENTS, TOK_SEGMENT, TOP))
    router_logits = centred(streams_of[3], (2, SEGMENTS, TOK_SEGMENT, TOP), 1.5, 6.0, ((1, 8), (2, 16)), jnp.float32)
    saved_gate_up = centred(streams_of[4], (2, SEGMENTS, EXPERTS * GROUP, 2, ROWS, HID_PART), 1.0, 6.0, ((1, 8), (2, 16), (5, 2)))
    down_weight = centred(streams_of[5], (SEGMENTS, EXPERTS * GROUP, HID_PART, D), D ** -0.5, 0.09375, ((0, 8), (1, 16), (2, 2)))
    return {"sent_down": sent_down, "sent_up": sent_up, "expert_ids": expert_ids, "router_logits": router_logits, "saved_gate_up": saved_gate_up, "down_weight": down_weight}


route_scale = 2.5


def slot_table(expert_list, experts, capacity):
    flat_ids = expert_list.reshape(-1)
    marks = (flat_ids[:, None] == jnp.arange(experts, dtype=jnp.int32)[None, :]).astype(jnp.int32)
    before = jnp.cumsum(marks, axis=0) - marks
    place = jnp.sum(before * marks, axis=1)
    slot_index = flat_ids * capacity + place
    filler = flat_ids.shape[0]
    owner = jnp.full((experts * capacity,), filler, jnp.int32).at[slot_index].set(jnp.arange(filler, dtype=jnp.int32))
    return slot_index, owner


def segment_backward(packed):
    down_in, up_in, expert_list, logits, saved, weight = packed
    sections = weight.shape[0]
    experts = sections // GROUP
    tok_segment, width = down_in.shape
    top_count = expert_list.shape[2]
    blocks = N_EXPERT
    tok_block = tok_segment // blocks
    rows_all = saved.shape[3]
    capacity = rows_all // blocks
    incoming = jnp.stack([down_in, up_in])
    scores = jax.nn.sigmoid(logits)
    total = jnp.sum(scores, axis=-1, keepdims=True)
    combine = (route_scale * scores / total).astype(jnp.bfloat16)
    weight_full = weight.astype(jnp.float32)
    weight_grad = jnp.zeros(weight.shape, jnp.float32)
    pair_grads = []
    logit_grads = []
    for span_idx in range(2):
        slot_index, owner = jax.vmap(lambda block_ids: slot_table(block_ids, experts, capacity))(
            expert_list[span_idx].reshape(blocks, tok_block, top_count))
        filler = tok_block * top_count
        offsets = (jnp.arange(blocks, dtype=jnp.int32) * filler)[:, None]
        global_slot = jnp.where(owner < filler, owner + offsets, tok_segment * top_count).astype(jnp.int32)
        global_slot = global_slot.reshape(blocks, experts, capacity).transpose(1, 0, 2).reshape(experts, rows_all)
        padded_rows = jnp.concatenate([incoming[span_idx], jnp.zeros((1, width), jnp.bfloat16)], axis=0)
        slot_rows = jnp.repeat(padded_rows[global_slot // top_count], GROUP, axis=0)
        padded_weights = jnp.concatenate([combine[span_idx].reshape(-1), jnp.zeros((1,), jnp.bfloat16)])
        slot_weight = jnp.repeat(padded_weights[global_slot].astype(jnp.float32)[..., None], GROUP, axis=0)
        gate_pre = saved[span_idx, :, 0].astype(jnp.float32)
        up_pre = saved[span_idx, :, 1].astype(jnp.float32)
        sigma = jax.nn.sigmoid(gate_pre)
        silu_val = gate_pre * sigma
        hidden_b = lax.optimization_barrier((silu_val * up_pre).astype(jnp.bfloat16))
        hidden_f = hidden_b.astype(jnp.float32)
        rows_f = slot_rows.astype(jnp.float32)
        raw_grad = jnp.einsum("erd,ehd->erh", rows_f, weight_full)
        partial_dot = jnp.sum(hidden_f * raw_grad, axis=-1)
        partial_dot = jnp.sum(partial_dot.reshape(experts, GROUP, rows_all), axis=1)
        hidden_grad = slot_weight * raw_grad
        gate_grad = hidden_grad * up_pre * sigma * (1.0 + gate_pre * (1.0 - sigma))
        up_grad = hidden_grad * silu_val
        pair_grads.append(jnp.stack([gate_grad, up_grad], axis=1).astype(jnp.bfloat16))
        scaled_b = lax.optimization_barrier((slot_weight * hidden_f).astype(jnp.bfloat16))
        weight_grad = weight_grad + jnp.einsum("erh,erd->ehd", scaled_b.astype(jnp.float32), rows_f)
        dots = partial_dot.reshape(experts, blocks, capacity).transpose(1, 0, 2).reshape(blocks, experts * capacity)
        route_grad = jnp.take_along_axis(dots, slot_index, axis=1).reshape(tok_segment, top_count)
        score_now = scores[span_idx]
        total_now = total[span_idx]
        score_grad = route_scale / total_now * (route_grad - jnp.sum(route_grad * score_now, axis=-1, keepdims=True) / total_now)
        logit_grads.append(score_grad * score_now * (1.0 - score_now))
    return jnp.stack(pair_grads), weight_grad.astype(jnp.bfloat16), jnp.stack(logit_grads)


def reference(sent_down, sent_up, expert_ids, router_logits, saved_gate_up, down_weight):
    empty = jnp.zeros_like(sent_down[:1])
    from_above = jnp.concatenate([sent_down[1:], empty], axis=0)
    from_below = jnp.concatenate([empty, sent_up[:-1]], axis=0)
    pair_grads, weight_grads, logit_grads = lax.map(
        segment_backward,
        (from_above, from_below, jnp.moveaxis(expert_ids, 1, 0), jnp.moveaxis(router_logits, 1, 0),
         jnp.moveaxis(saved_gate_up, 1, 0), down_weight))
    return jnp.moveaxis(pair_grads, 0, 1), weight_grads, jnp.moveaxis(logit_grads, 0, 1)
```

```python
import functools

import jax
import jax.numpy as jnp
from jax import lax
from jax.experimental import pallas as pl
from jax.experimental.pallas import tpu as pltpu
from jax.sharding import PartitionSpec as P

route_scale = 2.5
side = 4
shifts = (1, -1, 2)
extra = 128
bf16, f32 = jnp.bfloat16, jnp.float32
params = pltpu.CompilerParams(vmem_limit_bytes=48 * 2**20)
whole = pl.BlockSpec(memory_space=pltpu.VMEM)
scalars = pl.BlockSpec(memory_space=pltpu.SMEM)


def moved(place, step, along_x):
    y, x = place // side, place % side
    return y * side + (x + step) % side if along_x else (y + step) % side * side + x


def plane_shift(value, step, first_along_x):
    pairs = [
        (place * 2 + core, moved(place, step, first_along_x == (core == 0)) * 2 + core)
        for place in range(side * side)
        for core in range(2)
    ]
    return lax.ppermute(value, ("expert", "dp"), pairs)


def swapped(value):
    return lax.ppermute(value, "dp", [(0, 1), (1, 0)])


def select_kernel(info, *refs):
    blocks, outs = refs[:4], refs[4:]
    tokens, width = blocks[0].shape
    width -= extra
    slots = outs[0].shape[0] // 4
    rows, columns = 4 * tokens, 4 * outs[0].shape[0]

    def pick(index, base):
        return jnp.where(
            index < 2,
            jnp.where(index == 0, info[base], info[base + 1]),
            jnp.where(index == 2, info[base + 2], info[base + 3]),
        )

    notes = jnp.concatenate([ref[:, width:] for ref in blocks], axis=0).astype(f32)
    id0, id1 = notes[:, 0:1], notes[:, 1:2]
    row = lax.broadcasted_iota(jnp.int32, (rows, columns), 0)
    column = lax.broadcasted_iota(jnp.int32, (rows, columns), 1)
    expert = pick(column // (4 * slots), 4).astype(f32)
    same = pick(row // tokens, 0) == column // slots % 4
    named0 = same & (id0 == expert)
    named = named0 | (same & (id1 == expert))
    i = lax.broadcasted_iota(jnp.int32, (rows, rows), 0)
    j = lax.broadcasted_iota(jnp.int32, (rows, rows), 1)
    earlier = ((j < i) & (i // tokens == j // tokens)).astype(f32).astype(bf16)
    place = jnp.dot(earlier, named.astype(f32).astype(bf16), preferred_element_type=f32)
    taken = jnp.where(named & (place == (column % slots).astype(f32)), 1.0, 0.0)
    weights = (taken * jnp.where(named0, notes[:, 2:3], notes[:, 3:4])).astype(bf16)
    taken = taken.astype(bf16)
    across = (((0,), (0,)), ((), ()))

    def put(start, size, value):
        for out_index, out in enumerate(outs):
            out[:, start : start + size] = value[
                out_index * 4 * slots : (out_index + 1) * 4 * slots
            ].astype(bf16)

    put(
        width,
        extra,
        lax.dot_general(
            weights, jnp.ones((rows, extra), bf16), across, preferred_element_type=f32
        ),
    )
    step = 512 if width % 512 == 0 else width
    for start in range(0, width, step):
        chunk = jnp.concatenate([ref[:, start : start + step] for ref in blocks], axis=0)
        put(start, step, lax.dot_general(taken, chunk, across, preferred_element_type=f32))


def select_rows(info, blocks, slots):
    shape = jax.ShapeDtypeStruct((4 * slots, blocks[0].shape[1]), bf16)
    return pl.pallas_call(
        select_kernel,
        out_shape=(shape,) * 4,
        in_specs=[scalars] + [whole] * 4,
        out_specs=(whole,) * 4,
        compiler_params=params,
        name="select_rows",
    )(info, *blocks)


def hidden_of(saved, block):
    gate, up = saved[0, block, :].astype(f32), saved[1, block, :].astype(f32)
    sigma = jax.nn.sigmoid(gate)
    silu = gate * sigma
    return gate, up, sigma, silu, (silu * up).astype(bf16).astype(f32)


def raw_kernel(order, rows, mine, other, saved_mine, saved_other, g_mine, g_other, dots):
    count = rows.shape[0]
    width = rows.shape[1] - extra
    slots = count // 16
    slot_weight = rows[:, width : width + 1].astype(f32)
    total = jnp.zeros((count, 1), f32)
    for weight, saved, out in ((other, saved_other, g_other), (mine, saved_mine, g_mine)):
        raw = lax.dot_general(
            rows[:, :width], weight[...], (((1,), (1,)), ((), ())), preferred_element_type=f32
        )
        for chunk in range(16):
            at = pl.ds(pl.multiple_of(order[chunk] * slots, slots), slots)
            gate, up, sigma, silu, hidden = hidden_of(saved, at)
            raw_chunk = raw[chunk * slots : (chunk + 1) * slots]
            lane = lax.broadcasted_iota(jnp.int32, (slots, 128), 1)
            row = lax.broadcasted_iota(jnp.int32, (slots, 128), 0)
            dot = jnp.sum(hidden * raw_chunk, axis=1, keepdims=True)
            dot = jnp.sum(jnp.where(lane == row, dot, 0.0), axis=0, keepdims=True)
            spot = pl.ds(order[chunk] * 2, 1)
            if weight is other:
                dots[spot, :] = dot
            else:
                dot = dots[spot, :] + dot
                dots[spot, :] = dot
                dots[pl.ds(order[chunk] * 2 + 1, 1), :] = dot
            grad = slot_weight[chunk * slots : (chunk + 1) * slots] * raw_chunk
            out[0, at, :] = (grad * up * sigma * (1.0 + gate * (1.0 - sigma))).astype(bf16)
            out[1, at, :] = (grad * silu).astype(bf16)


def raw_grads(order, rows, mine, other, saved_mine, saved_other):
    return pl.pallas_call(
        raw_kernel,
        out_shape=(
            jax.ShapeDtypeStruct(saved_mine.shape, bf16),
            jax.ShapeDtypeStruct(saved_mine.shape, bf16),
            jax.ShapeDtypeStruct((32, 128), f32),
        ),
        in_specs=[scalars] + [whole] * 5,
        out_specs=(whole,) * 3,
        compiler_params=params,
        name="raw_grads",
    )(order, rows, mine, other, saved_mine, saved_other)


def down_kernel(order, rows, saved, *refs):
    out, scaled = refs[-2:]
    count = rows.shape[0]
    width = rows.shape[1] - extra
    slots = count // 16
    for chunk in range(16):
        at = pl.ds(pl.multiple_of(order[chunk] * slots, slots), slots)
        here = slice(chunk * slots, (chunk + 1) * slots)
        weight = rows[here, width : width + 1].astype(f32)
        scaled[here, :] = (weight * hidden_of(saved, at)[4]).astype(bf16)
    step = 512 if width % 512 == 0 else width
    for start in range(0, width, step):
        here = slice(start, start + step)
        value = lax.dot_general(
            scaled[...], rows[:, here], (((0,), (0,)), ((), ())), preferred_element_type=f32
        )
        if len(refs) == 3:
            value = value + refs[0][:, here].astype(f32)
        out[:, here] = value.astype(bf16)


def down_grads(order, rows, saved, *added):
    hidden_units = saved.shape[2]
    return pl.pallas_call(
        down_kernel,
        out_shape=jax.ShapeDtypeStruct((hidden_units, rows.shape[1] - extra), bf16),
        in_specs=[scalars] + [whole] * (2 + len(added)),
        out_specs=whole,
        scratch_shapes=[pltpu.VMEM((rows.shape[0], hidden_units), bf16)],
        compiler_params=params,
        name="down_grads",
    )(order, rows, saved, *added)


def logit_kernel(returned, experts, places, scores, out):
    half = scores.shape[0]
    spread = jnp.dot(
        experts[...], returned[...], preferred_element_type=f32, precision=lax.Precision.HIGHEST
    )
    route = jnp.sum(spread * places[...], axis=1, keepdims=True)
    route0, route1 = route[:half], route[half:]
    score0, score1 = scores[:, 0:1], scores[:, 1:2]
    total = score0 + score1
    mean = (route0 * score0 + route1 * score1) / total
    scale = route_scale / total
    grad0 = scale * (route0 - mean) * score0 * (1.0 - score0)
    grad1 = scale * (route1 - mean) * score1 * (1.0 - score1)
    lane = lax.broadcasted_iota(jnp.int32, (half, 2), 1)
    out[...] = jnp.where(lane == 0, grad0, grad1)


def local(sent_down, sent_up, expert_ids, router_logits, saved_gate_up, down_weight):
    core = lax.axis_index("dp")
    spot = lax.axis_index("expert")
    y, x = spot >> 2, spot & 3
    first = core == 0
    segments = lax.axis_size("pipe")
    ids = expert_ids[:, 0]
    scores = jax.nn.sigmoid(router_logits[:, 0])
    saved = saved_gate_up[:, 0, 0]
    mine = down_weight[0, 0]
    slots = saved.shape[2] // 16
    tokens, top = ids.shape[1:]

    pairs = [(2 * z, 2 * (z - 1)) for z in range(1, segments)]
    pairs += [(2 * z + 1, 2 * (z + 1) + 1) for z in range(segments - 1)]
    incoming = lax.ppermute(
        jnp.where(first, sent_down[0], sent_up[0]), ("pipe", "dp"), pairs
    )
    other = swapped(mine)
    saved_mine = jnp.where(first, saved[0], saved[1])
    saved_other = swapped(jnp.where(first, saved[1], saved[0]))

    combine = (route_scale * scores / jnp.sum(scores, axis=-1, keepdims=True)).astype(bf16)
    my_ids = jnp.where(first, ids[0], ids[1]).astype(bf16)
    my_combine = jnp.where(first, combine[0], combine[1])
    notes = jnp.concatenate(
        [my_ids, my_combine, jnp.zeros((tokens, extra - 2 * top), bf16)], axis=1
    )
    block = jnp.concatenate([incoming, notes], axis=1)

    near, far = jnp.where(first, x, y), jnp.where(first, y, x)
    blocks = [block] + [plane_shift(block, step, True) for step in shifts]
    held = [near] + [(near + side - step) & 3 for step in shifts]
    targets = [far] + [(far + side + step) & 3 for step in shifts]
    wanted = [jnp.where(first, t * 2 + (x >> 1), y * 2 + (t >> 1)) for t in targets]
    pieces = select_rows(jnp.stack(held + wanted).astype(jnp.int32), blocks, slots)
    pieces = [pieces[0]] + [
        plane_shift(piece, step, False) for piece, step in zip(pieces[1:], shifts, strict=True)
    ]
    rows = jnp.zeros((16 * slots, pieces[0].shape[1]), bf16)
    for piece, step in zip(pieces, (0,) + shifts, strict=True):
        rows = lax.dynamic_update_slice(
            rows, piece, (((far + side - step) & 3) * (4 * slots), jnp.int32(0))
        )
    number = jnp.arange(16, dtype=jnp.int32)
    order = jnp.where(first, number, (number & 3) * 4 + (number >> 2))

    g_mine, g_other, dots = raw_grads(order, rows, mine, other, saved_mine, saved_other)
    returned = lax.all_to_all(dots, ("expert", "dp"), split_axis=0, concat_axis=0, tiled=True)
    g_other = swapped(g_other)
    down_other = swapped(down_grads(order, rows, saved_other))
    weight_grad = down_grads(order, rows, saved_mine, down_other)
    pair_grads = jnp.where(
        first, jnp.stack([g_mine, g_other]), jnp.stack([g_other, g_mine])
    )

    marks = jnp.sum(
        (ids[..., None] == jnp.arange(8, dtype=jnp.int32)).astype(jnp.int32), axis=2
    )
    before = jnp.cumsum(marks, axis=1) - marks
    span = jnp.arange(2, dtype=jnp.int32)[:, None]
    source = jnp.arange(32, dtype=jnp.int32)
    lanes = jnp.arange(128, dtype=jnp.int32)
    experts, places = [], []
    for k in range(top):
        own = ids[..., k]
        experts.append(
            (source // 4 == own[..., None]) & (source % 2 == span[..., None])
        )
        place = jnp.sum(
            jnp.where(own[..., None] == jnp.arange(8, dtype=jnp.int32), before, 0), axis=-1
        )
        places.append(lanes == place[..., None])
    logit_grads = pl.pallas_call(
        logit_kernel,
        out_shape=jax.ShapeDtypeStruct((2 * tokens, top), f32),
        in_specs=[whole] * 4,
        out_specs=whole,
        compiler_params=params,
        name="logit_grads",
    )(
        returned,
        jnp.stack(experts).astype(f32).reshape(2 * top * tokens, 32),
        jnp.stack(places).astype(f32).reshape(2 * top * tokens, 128),
        scores.reshape(2 * tokens, top),
    )
    return (
        pair_grads[:, None, None],
        weight_grad[None, None],
        logit_grads.reshape(2, 1, tokens, top),
    )


def solution(mesh):
    placed = (
        P("pipe", "expert", None),
        P("pipe", "expert", None),
        P(None, "pipe", "expert", None),
        P(None, "pipe", "expert", None),
        P(None, "pipe", "expert", None, None, "dp"),
        P("pipe", "expert", "dp", None),
    )
    return jax.shard_map(
        local,
        mesh=mesh,
        in_specs=placed,
        out_specs=(
            P(None, "pipe", "expert", None, None, "dp"),
            P("pipe", "expert", "dp", None),
            P(None, "pipe", "expert", None),
        ),
        check_vma=False,
    )
```

```python
import jax
import jax.numpy as jnp
from jax import lax
from jax.experimental import pallas as pl
from jax.experimental.pallas import tpu as pltpu
from jax.sharding import PartitionSpec as P

route_scale = 2.5
side = 4
shifts = (2, 1, -1)
extra = 128
bf16, f32 = jnp.bfloat16, jnp.float32
params = pltpu.CompilerParams(vmem_limit_bytes=16 * 2**20)
whole = pl.BlockSpec(memory_space=pltpu.VMEM)
scalars = pl.BlockSpec(memory_space=pltpu.SMEM)


def moved(place, step, along_x):
    y, x = place // side, place % side
    return y * side + (x + step) % side if along_x else (y + step) % side * side + x


def plane_shift(value, step, first_along_x):
    pairs = [
        (place * 2 + core, moved(place, step, first_along_x == (core == 0)) * 2 + core)
        for place in range(side * side)
        for core in range(2)
    ]
    return lax.ppermute(value, ("expert", "dp"), pairs)


def swapped(value):
    return lax.ppermute(value, "dp", [(0, 1), (1, 0)])


def select_kernel(info, *refs):
    blocks, outs = refs[:4], refs[4:]
    tokens, width = blocks[0].shape
    width -= extra
    slots = outs[0].shape[0] // 4
    rows, columns = 4 * outs[0].shape[0], 4 * tokens

    def pick(index, base):
        return jnp.where(
            index < 2,
            jnp.where(index == 0, info[base], info[base + 1]),
            jnp.where(index == 2, info[base + 2], info[base + 3]),
        )

    notes = jnp.concatenate([ref[:, width:] for ref in blocks], axis=0).astype(f32).T
    row = lax.broadcasted_iota(jnp.int32, (rows, 1), 0)
    column = lax.broadcasted_iota(jnp.int32, (1, columns), 1)
    expert = pick(row >> 6, 4).astype(f32)
    same = ((row >> 4) & 3) == pick(column >> 5, 0)
    named0 = same & (notes[0:1] == expert)
    named = named0 | (same & (notes[1:2] == expert))
    i = lax.broadcasted_iota(jnp.int32, (columns, columns), 0)
    j = lax.broadcasted_iota(jnp.int32, (columns, columns), 1)
    earlier = jnp.where((i < j) & ((i >> 5) == (j >> 5)), 1.0, 0.0).astype(bf16)
    marked = jnp.where(named, 1.0, 0.0).astype(bf16)
    place = jnp.dot(marked, earlier, preferred_element_type=f32)
    taken = jnp.where(named & (place == (row & 15).astype(f32)), 1.0, 0.0)
    weight = jnp.sum(
        taken * jnp.where(named0, notes[2:3], notes[3:4]), axis=1, keepdims=True
    )
    taken = taken.astype(bf16)

    def put(start, size, value):
        for index, out in enumerate(outs):
            out[:, start : start + size] = value[index * 4 * slots : (index + 1) * 4 * slots]

    put(width, extra, jnp.broadcast_to(weight, (rows, extra)).astype(bf16))
    step = 512 if width % 512 == 0 else width
    for start in range(0, width, step):
        chunk = jnp.concatenate([ref[:, start : start + step] for ref in blocks], axis=0)
        put(start, step, jnp.dot(taken, chunk, preferred_element_type=f32).astype(bf16))


def select_rows(info, blocks, slots):
    shape = jax.ShapeDtypeStruct((4 * slots, blocks[0].shape[1]), bf16)
    return pl.pallas_call(
        select_kernel,
        out_shape=(shape,) * 4,
        in_specs=[scalars] + [whole] * 4,
        out_specs=(whole,) * 4,
        compiler_params=params,
        name="select_rows",
    )(info, *blocks)


def factor_kernel(order, saved, swapped_saved, factors):
    slots = saved.shape[2] // 16
    span = order[16]
    for index, ref in enumerate((swapped_saved, saved)):
        for chunk in range(16):
            at = pl.ds(pl.multiple_of(order[chunk] * slots, slots), slots)
            here = slice(chunk * slots, (chunk + 1) * slots)
            gate, up = ref[span, 0, at, :].astype(f32), ref[span, 1, at, :].astype(f32)
            sigma = jax.nn.sigmoid(gate)
            silu = gate * sigma
            factors[index, 0, here, :] = (silu * up).astype(bf16).astype(f32)
            factors[index, 1, here, :] = up * sigma * (1.0 + gate * (1.0 - sigma))
            factors[index, 2, here, :] = silu


def saved_factors(order, saved, swapped_saved):
    return pl.pallas_call(
        factor_kernel,
        out_shape=jax.ShapeDtypeStruct((2, 3) + saved.shape[2:], f32),
        in_specs=[scalars] + [whole] * 2,
        out_specs=whole,
        compiler_params=params,
        name="saved_factors",
    )(order, saved, swapped_saved)


def down_product(scaled, rows, out, added=None):
    width = out.shape[1]
    step = 512 if width % 512 == 0 else width
    for start in range(0, width, step):
        here = slice(start, start + step)
        value = lax.dot_general(
            scaled, rows[:, here], (((0,), (0,)), ((), ())), preferred_element_type=f32
        )
        if added is not None:
            value = value + added[:, here].astype(f32)
        out[:, here] = value.astype(bf16)


def slot_weights(rows, like):
    weights = rows[:, rows.shape[1] - extra :].astype(f32)
    return jnp.concatenate([weights] * (like.shape[-1] // extra), axis=1)


def raw_kernel(order, rows, mine, other, factors, g_mine, g_other, dots, down_other):
    count = rows.shape[0]
    width = rows.shape[1] - extra
    slots = count // 16
    weights = slot_weights(rows, factors)
    dot = jnp.zeros((count, 1), f32)
    for index, (weight, out) in enumerate(((other, g_other), (mine, g_mine))):
        raw = lax.dot_general(
            rows[:, :width], weight[...], (((1,), (1,)), ((), ())), preferred_element_type=f32
        )
        dot = dot + jnp.sum(factors[index, 0] * raw, axis=1, keepdims=True)
        grad = weights * raw
        for part in range(2):
            value = (grad * factors[index, part + 1]).astype(bf16)
            for chunk in range(16):
                at = pl.ds(pl.multiple_of(order[chunk] * slots, slots), slots)
                out[part, at, :] = value[chunk * slots : (chunk + 1) * slots]
    lane = lax.broadcasted_iota(jnp.int32, (count, 128), 1)
    row = lax.broadcasted_iota(jnp.int32, (count, 128), 0)
    spread = jnp.where(lane == (row & 15), dot, 0.0)
    for chunk in range(16):
        line = jnp.sum(spread[chunk * slots : (chunk + 1) * slots], axis=0, keepdims=True)
        for core in range(2):
            dots[pl.ds(order[chunk] * 2 + core, 1), :] = line
    down_product((weights * factors[0, 0]).astype(bf16), rows, down_other)


def raw_grads(order, rows, mine, other, factors):
    grads = jax.ShapeDtypeStruct((2,) + factors.shape[2:], bf16)
    return pl.pallas_call(
        raw_kernel,
        out_shape=(
            grads,
            grads,
            jax.ShapeDtypeStruct((32, 128), f32),
            jax.ShapeDtypeStruct(mine.shape, bf16),
        ),
        in_specs=[scalars] + [whole] * 4,
        out_specs=(whole,) * 4,
        compiler_params=params,
        name="raw_grads",
    )(order, rows, mine, other, factors)


def finish_kernel(order, rows, factors, g_mine, g_other, down_other, pair_grads, weight_grad):
    span = order[16]
    pair_grads[span] = g_mine[...]
    pair_grads[1 - span] = g_other[...]
    scaled = (slot_weights(rows, factors) * factors[1, 0]).astype(bf16)
    down_product(scaled, rows, weight_grad, down_other)


def finished(order, rows, factors, g_mine, g_other, down_other):
    return pl.pallas_call(
        finish_kernel,
        out_shape=(
            jax.ShapeDtypeStruct((2,) + g_mine.shape, bf16),
            jax.ShapeDtypeStruct(down_other.shape, bf16),
        ),
        in_specs=[scalars] + [whole] * 5,
        out_specs=(whole,) * 2,
        compiler_params=params,
        name="finished",
    )(order, rows, factors, g_mine, g_other, down_other)


def logit_kernel(returned, experts, places, scores, out):
    tokens = scores.shape[1]
    spread = lax.dot_general(
        returned[...],
        experts[...],
        (((0,), (0,)), ((), ())),
        preferred_element_type=f32,
        precision=lax.Precision.HIGHEST,
    )
    route = jnp.sum(spread * places[...], axis=0, keepdims=True)
    for span in range(2):
        first, second = 2 * span, 2 * span + 1
        route0 = route[:, first * tokens : (first + 1) * tokens]
        route1 = route[:, second * tokens : (second + 1) * tokens]
        score0, score1 = scores[first : first + 1], scores[second : second + 1]
        total = score0 + score1
        mean = (route0 * score0 + route1 * score1) / total
        scale = route_scale / total
        out[first : first + 1] = scale * (route0 - mean) * score0 * (1.0 - score0)
        out[second : second + 1] = scale * (route1 - mean) * score1 * (1.0 - score1)


def note_kernel(ids, logits, notes, experts, places, scores):
    tokens = ids.shape[1]
    score = jax.nn.sigmoid(logits[...])
    scores[...] = score
    number = ids[...]
    line = jnp.concatenate([number[row : row + 1] for row in range(4)], axis=1)
    lane = lax.broadcasted_iota(jnp.int32, (1, 4 * tokens), 1)
    source = lax.broadcasted_iota(jnp.int32, (32, 4 * tokens), 0)
    span = lane >> 6
    experts[...] = jnp.where(((source >> 2) == line) & ((source & 1) == span), 1.0, 0.0)
    expert = lax.broadcasted_iota(jnp.int32, (8, 4 * tokens), 0)
    marked = jnp.where(expert == line, 1.0, 0.0)
    i = lax.broadcasted_iota(jnp.int32, (4 * tokens, 4 * tokens), 0)
    j = lax.broadcasted_iota(jnp.int32, (4 * tokens, 4 * tokens), 1)
    earlier = jnp.where(((i >> 6) == (j >> 6)) & ((i & 31) < (j & 31)), 1.0, 0.0)
    before = jnp.dot(marked.astype(bf16), earlier.astype(bf16), preferred_element_type=f32)
    place = jnp.sum(before * marked, axis=0, keepdims=True)
    slot = lax.broadcasted_iota(jnp.int32, (128, 4 * tokens), 0).astype(f32)
    places[...] = jnp.where(slot == place, 1.0, 0.0)
    for span in range(2):
        pair = score[2 * span : 2 * span + 2]
        combine = route_scale * pair / (pair[0:1] + pair[1:2])
        lines = [
            number[2 * span : 2 * span + 2].astype(f32),
            combine,
            jnp.zeros((extra - 4, tokens), f32),
        ]
        table = jnp.concatenate(lines, axis=0)
        table = jnp.concatenate([table, jnp.zeros((extra, extra - tokens), f32)], axis=1)
        notes[span] = table.T[:tokens].astype(bf16)


def slot_notes(ids, logits):
    tokens = ids.shape[1]
    return pl.pallas_call(
        note_kernel,
        out_shape=(
            jax.ShapeDtypeStruct((2, tokens, extra), bf16),
            jax.ShapeDtypeStruct((32, 4 * tokens), f32),
            jax.ShapeDtypeStruct((128, 4 * tokens), f32),
            jax.ShapeDtypeStruct((4, tokens), f32),
        ),
        in_specs=[whole] * 2,
        out_specs=(whole,) * 4,
        compiler_params=params,
        name="slot_notes",
    )(ids, logits)


def local(sent_down, sent_up, expert_ids, router_logits, saved_gate_up, down_weight):
    core = lax.axis_index("dp")
    spot = lax.axis_index("expert")
    y, x = spot >> 2, spot & 3
    first = core == 0
    segments = lax.axis_size("pipe")
    saved = saved_gate_up[:, 0, 0]
    mine = down_weight[0, 0]
    slots = saved.shape[2] // 16
    tokens, top = expert_ids.shape[2:]

    def by_slot(value):
        return jnp.swapaxes(value[:, 0], 1, 2).reshape(2 * top, tokens)

    pairs = [(2 * z, 2 * (z - 1)) for z in range(1, segments)]
    pairs += [(2 * z + 1, 2 * (z + 1) + 1) for z in range(segments - 1)]
    incoming = lax.ppermute(
        jnp.where(first, sent_down[0], sent_up[0]), ("pipe", "dp"), pairs
    )
    other = swapped(mine)
    swapped_saved = swapped(saved)
    notes, experts, places, scores = slot_notes(by_slot(expert_ids), by_slot(router_logits))
    block = jnp.concatenate([incoming, jnp.where(first, notes[0], notes[1])], axis=1)

    near, far = jnp.where(first, x, y), jnp.where(first, y, x)
    blocks = [block] + [plane_shift(block, step, True) for step in shifts]
    held = [near] + [(near + side - step) & 3 for step in shifts]
    targets = [far] + [(far + side + step) & 3 for step in shifts]
    wanted = [jnp.where(first, t * 2 + (x >> 1), y * 2 + (t >> 1)) for t in targets]
    pieces = select_rows(jnp.stack(held + wanted).astype(jnp.int32), blocks, slots)
    pieces = [pieces[0]] + [
        plane_shift(piece, step, False) for piece, step in zip(pieces[1:], shifts, strict=True)
    ]
    rows = jnp.zeros((16 * slots, pieces[0].shape[1]), bf16)
    for piece, step in zip(pieces, (0,) + shifts, strict=True):
        rows = lax.dynamic_update_slice(
            rows, piece, (((far + side - step) & 3) * (4 * slots), jnp.int32(0))
        )
    number = jnp.arange(16, dtype=jnp.int32)
    order = jnp.where(first, number, (number & 3) * 4 + (number >> 2))
    order = jnp.concatenate([order, core[None].astype(jnp.int32)])

    factors = saved_factors(order, saved, swapped_saved)
    g_mine, g_other, dots, down_other = raw_grads(order, rows, mine, other, factors)
    returned = lax.all_to_all(dots, ("expert", "dp"), split_axis=0, concat_axis=0, tiled=True)
    pair_grads, weight_grad = finished(
        order, rows, factors, g_mine, swapped(g_other), swapped(down_other)
    )
    returned, pair_grads, weight_grad = lax.optimization_barrier(
        (returned, pair_grads, weight_grad)
    )
    logit_grads = pl.pallas_call(
        logit_kernel,
        out_shape=jax.ShapeDtypeStruct((2 * top, tokens), f32),
        in_specs=[whole] * 4,
        out_specs=whole,
        compiler_params=params,
        name="logit_grads",
    )(returned, experts, places, scores)
    return (
        pair_grads[:, None, None],
        weight_grad[None, None],
        jnp.swapaxes(logit_grads.reshape(2, 1, top, tokens), 2, 3),
    )


def solution(mesh):
    placed = (
        P("pipe", "expert", None),
        P("pipe", "expert", None),
        P(None, "pipe", "expert", None),
        P(None, "pipe", "expert", None),
        P(None, "pipe", "expert", None, None, "dp"),
        P("pipe", "expert", "dp", None),
    )
    return jax.shard_map(
        local,
        mesh=mesh,
        in_specs=placed,
        out_specs=(
            P(None, "pipe", "expert", None, None, "dp"),
            P("pipe", "expert", "dp", None),
            P(None, "pipe", "expert", None),
        ),
        check_vma=False,
    )
```

```python
import jax
import jax.numpy as jnp
from jax import lax
from jax.experimental import pallas as pl
from jax.experimental.pallas import tpu as pltpu
from jax.sharding import PartitionSpec as P

route_scale = 2.5
side = 4
shifts = (2, 1, -1)
extra = 128
bf16, f32 = jnp.bfloat16, jnp.float32
params = pltpu.CompilerParams(vmem_limit_bytes=16 * 2**20)
whole = pl.BlockSpec(memory_space=pltpu.VMEM)


def moved(place, step, along_x):
    y, x = place // side, place % side
    return y * side + (x + step) % side if along_x else (y + step) % side * side + x


def plane_shift(value, step, first_along_x):
    pairs = [
        (place * 2 + core, moved(place, step, first_along_x == (core == 0)) * 2 + core)
        for place in range(side * side)
        for core in range(2)
    ]
    return lax.ppermute(value, ("expert", "dp"), pairs)


def swapped(value):
    return lax.ppermute(value, "dp", [(0, 1), (1, 0)])


def position():
    core, spot = lax.axis_index("dp"), lax.axis_index("expert")
    y, x = spot >> 2, spot & 3
    return core, jnp.where(core == 0, x, y), jnp.where(core == 0, y, x)


def token_blocks(core, far):
    places = [(far + side - step) & 3 for step in (0,) + shifts]
    return [
        jnp.where(core == 0, place * 4 + chunk, chunk * 4 + place)
        for place in places
        for chunk in range(side)
    ]


def select_kernel(*refs):
    blocks, outs = refs[:4], refs[4:]
    core, near, far = position()
    held = [(near + side - step) & 3 for step in (0,) + shifts]
    targets = [(far + side + step) & 3 for step in (0,) + shifts]
    wanted = [jnp.where(core == 0, t * 2 + (near >> 1), near * 2 + (t >> 1)) for t in targets]
    tokens, width = blocks[0].shape
    width -= extra
    slots = outs[0].shape[0] // 4
    rows, columns = 4 * outs[0].shape[0], 4 * tokens

    def pick(index, values):
        return jnp.where(
            index < 2,
            jnp.where(index == 0, values[0], values[1]),
            jnp.where(index == 2, values[2], values[3]),
        )

    notes = jnp.concatenate([ref[:, width:] for ref in blocks], axis=0).astype(f32).T
    row = lax.broadcasted_iota(jnp.int32, (rows, 1), 0)
    column = lax.broadcasted_iota(jnp.int32, (1, columns), 1)
    expert = pick(row >> 6, wanted).astype(f32)
    same = ((row >> 4) & 3) == pick(column >> 5, held)
    named0 = same & (notes[0:1] == expert)
    named = named0 | (same & (notes[1:2] == expert))
    i = lax.broadcasted_iota(jnp.int32, (columns, columns), 0)
    j = lax.broadcasted_iota(jnp.int32, (columns, columns), 1)
    earlier = jnp.where((i < j) & ((i >> 5) == (j >> 5)), 1.0, 0.0).astype(bf16)
    marked = jnp.where(named, 1.0, 0.0).astype(bf16)
    place = jnp.dot(marked, earlier, preferred_element_type=f32)
    taken = jnp.where(named & (place == (row & 15).astype(f32)), 1.0, 0.0)
    weight = jnp.sum(
        taken * jnp.where(named0, notes[2:3], notes[3:4]), axis=1, keepdims=True
    )
    taken = taken.astype(bf16)

    def put(start, size, value):
        for index, out in enumerate(outs):
            out[:, start : start + size] = value[index * 4 * slots : (index + 1) * 4 * slots]

    put(width, extra, jnp.broadcast_to(weight, (rows, extra)).astype(bf16))
    step = 512 if width % 512 == 0 else width
    for start in range(0, width, step):
        chunk = jnp.concatenate([ref[:, start : start + step] for ref in blocks], axis=0)
        put(start, step, jnp.dot(taken, chunk, preferred_element_type=f32).astype(bf16))


def select_rows(blocks, slots):
    shape = jax.ShapeDtypeStruct((4 * slots, blocks[0].shape[1]), bf16)
    return pl.pallas_call(
        select_kernel,
        out_shape=(shape,) * 4,
        in_specs=[whole] * 4,
        out_specs=(whole,) * 4,
        compiler_params=params,
        name="select_rows",
    )(*blocks)


def factor_kernel(saved, swapped_saved, mine, factors, hidden, kept, arrived):
    fetch = pltpu.make_async_copy(mine, kept, arrived)
    fetch.start()
    slots = saved.shape[2] // 16
    span, near, far = position()
    order = token_blocks(span, far) + token_blocks(1 - span, near)

    def at(chunk):
        return pl.ds(pl.multiple_of(order[chunk] * slots, slots), slots)

    for chunk in range(16):
        here = slice(chunk * slots, (chunk + 1) * slots)
        for index, ref in enumerate((swapped_saved, saved)):
            gate = ref[span, 0, at(chunk), :].astype(f32)
            up = ref[span, 1, at(chunk), :].astype(f32)
            sigma = jax.nn.sigmoid(gate)
            silu = gate * sigma
            product = (silu * up).astype(bf16)
            factors[index, 0, here, :] = product.astype(f32)
            factors[index, 1, here, :] = up * sigma * (1.0 + gate * (1.0 - sigma))
            factors[index, 2, here, :] = silu
        hidden[0, here, :] = product
        gate = saved[1 - span, 0, at(16 + chunk), :].astype(f32)
        up = saved[1 - span, 1, at(16 + chunk), :].astype(f32)
        hidden[1, here, :] = (gate * jax.nn.sigmoid(gate) * up).astype(bf16)
    fetch.wait()


def saved_factors(saved, swapped_saved, mine):
    return pl.pallas_call(
        factor_kernel,
        out_shape=(
            jax.ShapeDtypeStruct((2, 3) + saved.shape[2:], f32),
            jax.ShapeDtypeStruct((2,) + saved.shape[2:], bf16),
            jax.ShapeDtypeStruct(mine.shape, bf16),
        ),
        in_specs=[whole, whole, pl.BlockSpec(memory_space=pl.ANY)],
        out_specs=(whole,) * 3,
        scratch_shapes=[pltpu.SemaphoreType.DMA],
        compiler_params=params,
        name="saved_factors",
    )(saved, swapped_saved, mine)


def slot_weights(notes, wide):
    return jnp.concatenate([notes.astype(f32)] * (wide // extra), axis=1)


def raw_kernel(rows, mine, other, factors, g_mine, g_other, dots):
    count = rows.shape[0]
    width = rows.shape[1] - extra
    slots = count // 16
    core, _, far = position()
    order = token_blocks(core, far)
    weights = slot_weights(rows[:, width:], factors.shape[3])
    dot = jnp.zeros((count, 1), f32)
    for index, (weight, out) in ((1, (mine, g_mine)), (0, (other, g_other))):
        raw = lax.dot_general(
            rows[:, :width], weight[...], (((1,), (1,)), ((), ())), preferred_element_type=f32
        )
        dot = dot + jnp.sum(factors[index, 0] * raw, axis=1, keepdims=True)
        grad = weights * raw
        for part in range(2):
            value = (grad * factors[index, part + 1]).astype(bf16)
            for chunk in range(16):
                at = pl.ds(pl.multiple_of(order[chunk] * slots, slots), slots)
                out[part, at, :] = value[chunk * slots : (chunk + 1) * slots]
    lane = lax.broadcasted_iota(jnp.int32, (count, 128), 1)
    row = lax.broadcasted_iota(jnp.int32, (count, 128), 0)
    spread = jnp.where(lane == (row & 15), dot, 0.0)
    for chunk in range(16):
        line = jnp.sum(spread[chunk * slots : (chunk + 1) * slots], axis=0, keepdims=True)
        for core in range(2):
            dots[pl.ds(order[chunk] * 2 + core, 1), :] = line


def raw_grads(rows, mine, other, factors):
    grads = jax.ShapeDtypeStruct((2,) + factors.shape[2:], bf16)
    return pl.pallas_call(
        raw_kernel,
        out_shape=(grads, grads, jax.ShapeDtypeStruct((32, 128), f32)),
        in_specs=[whole] * 4,
        out_specs=(whole,) * 3,
        compiler_params=params,
        name="raw_grads",
    )(rows, mine, other, factors)


def finish_kernel(
    rows, notes, rows_other, notes_other, hidden, g_mine, g_other, *refs
):
    tables, (pair_grads, weight_grad), passed, scaled = refs[:3], refs[3:5], refs[5:8], refs[8]
    count, wide = hidden.shape[1:]

    @pl.when(pl.program_id(0) == 0)
    def _():
        span = lax.axis_index("dp")
        pair_grads[span] = g_mine[...]
        pair_grads[1 - span] = g_other[...]
        for table, out in zip(tables, passed, strict=True):
            out[...] = table[...]
        for index, ref in enumerate((notes, notes_other)):
            value = slot_weights(ref[...], wide) * hidden[index].astype(f32)
            scaled[:, index * count : (index + 1) * count] = value.T.astype(bf16)

    total = jnp.dot(scaled[:, :count], rows[...], preferred_element_type=f32)
    total = total + jnp.dot(scaled[:, count:], rows_other[...], preferred_element_type=f32)
    weight_grad[...] = total.astype(bf16)


def finished(rows, rows_other, hidden, g_mine, g_other, tables):
    count, wide = hidden.shape[1:]
    width = rows.shape[1] - extra
    step = 512 if width % 512 == 0 else width

    def kept(shape):
        return pl.BlockSpec(shape, lambda i: (0,) * len(shape))

    block = pl.BlockSpec((count, step), lambda i: (0, i))
    note = pl.BlockSpec((count, extra), lambda i: (0, width // extra))
    return pl.pallas_call(
        finish_kernel,
        grid=(width // step,),
        out_shape=(
            jax.ShapeDtypeStruct((2,) + g_mine.shape, bf16),
            jax.ShapeDtypeStruct((wide, width), bf16),
            *(jax.ShapeDtypeStruct(table.shape, table.dtype) for table in tables),
        ),
        in_specs=[
            block,
            note,
            block,
            note,
            kept(hidden.shape),
            kept(g_mine.shape),
            kept(g_other.shape),
            *(kept(table.shape) for table in tables),
        ],
        out_specs=(
            kept((2,) + g_mine.shape),
            pl.BlockSpec((wide, step), lambda i: (0, i)),
            *(kept(table.shape) for table in tables),
        ),
        scratch_shapes=[pltpu.VMEM((wide, 2 * count), bf16)],
        compiler_params=params,
        name="finished",
    )(rows, rows, rows_other, rows_other, hidden, g_mine, g_other, *tables)


def logit_kernel(returned, experts, places, scores, out):
    tokens = scores.shape[1]
    spread = lax.dot_general(
        returned[...],
        experts[...],
        (((0,), (0,)), ((), ())),
        preferred_element_type=f32,
        precision=lax.Precision.HIGHEST,
    )
    route = jnp.sum(spread * places[...], axis=0, keepdims=True)
    for span in range(2):
        first, second = 2 * span, 2 * span + 1
        route0 = route[:, first * tokens : (first + 1) * tokens]
        route1 = route[:, second * tokens : (second + 1) * tokens]
        score0, score1 = scores[first : first + 1], scores[second : second + 1]
        total = score0 + score1
        mean = (route0 * score0 + route1 * score1) / total
        scale = route_scale / total
        out[first : first + 1] = scale * (route0 - mean) * score0 * (1.0 - score0)
        out[second : second + 1] = scale * (route1 - mean) * score1 * (1.0 - score1)


def note_kernel(ids, logits, notes, experts, places, scores):
    tokens = ids.shape[1]
    score = jax.nn.sigmoid(logits[...])
    scores[...] = score
    number = ids[...]
    line = jnp.concatenate([number[row : row + 1] for row in range(4)], axis=1)
    lane = lax.broadcasted_iota(jnp.int32, (1, 4 * tokens), 1)
    source = lax.broadcasted_iota(jnp.int32, (32, 4 * tokens), 0)
    span = lane >> 6
    experts[...] = jnp.where(((source >> 2) == line) & ((source & 1) == span), 1.0, 0.0)
    expert = lax.broadcasted_iota(jnp.int32, (8, 4 * tokens), 0)
    marked = jnp.where(expert == line, 1.0, 0.0)
    i = lax.broadcasted_iota(jnp.int32, (4 * tokens, 4 * tokens), 0)
    j = lax.broadcasted_iota(jnp.int32, (4 * tokens, 4 * tokens), 1)
    earlier = jnp.where(((i >> 6) == (j >> 6)) & ((i & 31) < (j & 31)), 1.0, 0.0)
    before = jnp.dot(marked.astype(bf16), earlier.astype(bf16), preferred_element_type=f32)
    place = jnp.sum(before * marked, axis=0, keepdims=True)
    slot = lax.broadcasted_iota(jnp.int32, (128, 4 * tokens), 0).astype(f32)
    places[...] = jnp.where(slot == place, 1.0, 0.0)
    first = lax.axis_index("dp") == 0
    pair = jnp.where(first, score[0:2], score[2:4])
    lines = [
        jnp.where(first, number[0:2], number[2:4]).astype(f32),
        route_scale * pair / (pair[0:1] + pair[1:2]),
        jnp.zeros((extra - 4, tokens), f32),
    ]
    table = jnp.concatenate(lines, axis=0)
    table = jnp.concatenate([table, jnp.zeros((extra, extra - tokens), f32)], axis=1)
    notes[...] = table.T[:tokens].astype(bf16)


def slot_notes(ids, logits):
    tokens = ids.shape[1]
    return pl.pallas_call(
        note_kernel,
        out_shape=(
            jax.ShapeDtypeStruct((tokens, extra), bf16),
            jax.ShapeDtypeStruct((32, 4 * tokens), f32),
            jax.ShapeDtypeStruct((128, 4 * tokens), f32),
            jax.ShapeDtypeStruct((4, tokens), f32),
        ),
        in_specs=[whole] * 2,
        out_specs=(whole,) * 4,
        compiler_params=params,
        name="slot_notes",
    )(ids, logits)


def local(sent_down, sent_up, expert_ids, router_logits, saved_gate_up, down_weight):
    first = lax.axis_index("dp") == 0
    segments = lax.axis_size("pipe")
    saved = saved_gate_up[:, 0, 0]
    mine = down_weight[0, 0]
    slots = saved.shape[2] // 16
    tokens, top = expert_ids.shape[2:]

    def by_slot(value):
        return jnp.swapaxes(value[:, 0], 1, 2).reshape(2 * top, tokens)

    pairs = [(2 * z, 2 * (z - 1)) for z in range(1, segments)]
    pairs += [(2 * z + 1, 2 * (z + 1) + 1) for z in range(segments - 1)]
    outgoing, expert_ids, router_logits = lax.optimization_barrier(
        (jnp.where(first, sent_down[0], sent_up[0]), expert_ids, router_logits)
    )
    incoming = lax.ppermute(outgoing, ("pipe", "dp"), pairs)
    notes, experts, places, scores = slot_notes(by_slot(expert_ids), by_slot(router_logits))
    block = jnp.concatenate([incoming, notes], axis=1)
    swapped_saved = swapped(saved)
    block, held, swapped_saved = lax.optimization_barrier((block, mine, swapped_saved))
    other = swapped(held)

    blocks = [block] + [plane_shift(block, step, True) for step in shifts]
    factors, hidden, mine = saved_factors(saved, swapped_saved, mine)
    blocks[1], other, mine, factors, hidden = lax.optimization_barrier(
        (blocks[1], other, mine, factors, hidden)
    )
    pieces = select_rows(blocks, slots)
    pieces = [pieces[0]] + [
        plane_shift(piece, step, False) for piece, step in zip(pieces[1:], shifts, strict=True)
    ]
    rows = jnp.zeros((16 * slots, pieces[0].shape[1]), bf16)
    for index, piece in enumerate(pieces):
        rows = lax.dynamic_update_slice(rows, piece, (index * 4 * slots, 0))
    g_mine, g_other, dots = raw_grads(rows, mine, other, factors)
    returned = lax.all_to_all(dots, ("expert", "dp"), split_axis=0, concat_axis=0, tiled=True)
    pair_grads, weight_grad, experts, places, scores = finished(
        rows, swapped(rows), hidden, g_mine, swapped(g_other), (experts, places, scores)
    )
    returned, pair_grads, weight_grad = lax.optimization_barrier(
        (returned, pair_grads, weight_grad)
    )
    logit_grads = pl.pallas_call(
        logit_kernel,
        out_shape=jax.ShapeDtypeStruct((2 * top, tokens), f32),
        in_specs=[whole] * 4,
        out_specs=whole,
        compiler_params=params,
        name="logit_grads",
    )(returned, experts, places, scores)
    return (
        pair_grads[:, None, None],
        weight_grad[None, None],
        jnp.swapaxes(logit_grads.reshape(2, 1, top, tokens), 2, 3),
    )


def solution(mesh):
    placed = (
        P("pipe", "expert", None),
        P("pipe", "expert", None),
        P(None, "pipe", "expert", None),
        P(None, "pipe", "expert", None),
        P(None, "pipe", "expert", None, None, "dp"),
        P("pipe", "expert", "dp", None),
    )
    return jax.shard_map(
        local,
        mesh=mesh,
        in_specs=placed,
        out_specs=(
            P(None, "pipe", "expert", None, None, "dp"),
            P("pipe", "expert", "dp", None),
            P(None, "pipe", "expert", None),
        ),
        check_vma=False,
    )
```

```python
import jax
import jax.numpy as jnp
from jax import lax
from jax.experimental import pallas as pl
from jax.experimental.pallas import tpu as pltpu
from jax.sharding import PartitionSpec as P

route_scale = 2.5
side = 4
shifts = (2, 1, -1)
extra = 128
bf16, f32 = jnp.bfloat16, jnp.float32
params = pltpu.CompilerParams(vmem_limit_bytes=16 * 2**20)
whole = pl.BlockSpec(memory_space=pltpu.VMEM)
in_hbm = pl.BlockSpec(memory_space=pltpu.HBM)


def moved(place, step, along_x):
    y, x = place // side, place % side
    return y * side + (x + step) % side if along_x else (y + step) % side * side + x


def plane_shift(value, step, first_along_x):
    pairs = [
        (place * 2 + core, moved(place, step, first_along_x == (core == 0)) * 2 + core)
        for place in range(side * side)
        for core in range(2)
    ]
    return lax.ppermute(value, ("expert", "dp"), pairs)


def swapped(value):
    return lax.ppermute(value, "dp", [(0, 1), (1, 0)])


def position():
    core, spot = lax.axis_index("dp"), lax.axis_index("expert")
    y, x = spot >> 2, spot & 3
    return core, jnp.where(core == 0, x, y), jnp.where(core == 0, y, x)


def token_blocks(core, far):
    places = [(far + side - step) & 3 for step in (0,) + shifts]
    return [
        jnp.where(core == 0, place * 4 + chunk, chunk * 4 + place)
        for place in places
        for chunk in range(side)
    ]


def select_kernel(*refs):
    blocks, outs = refs[:4], refs[4:]
    core, near, far = position()
    held = [(near + side - step) & 3 for step in (0,) + shifts]
    targets = [(far + side + step) & 3 for step in (0,) + shifts]
    wanted = [jnp.where(core == 0, t * 2 + (near >> 1), near * 2 + (t >> 1)) for t in targets]
    tokens, width = blocks[0].shape
    width -= extra
    slots = outs[0].shape[0] // 4
    rows, columns = 4 * outs[0].shape[0], 4 * tokens

    def pick(index, values):
        return jnp.where(
            index < 2,
            jnp.where(index == 0, values[0], values[1]),
            jnp.where(index == 2, values[2], values[3]),
        )

    notes = jnp.concatenate([ref[:, width:] for ref in blocks], axis=0).astype(f32).T
    row = lax.broadcasted_iota(jnp.int32, (rows, 1), 0)
    column = lax.broadcasted_iota(jnp.int32, (1, columns), 1)
    expert = pick(row >> 6, wanted).astype(f32)
    same = ((row >> 4) & 3) == pick(column >> 5, held)
    named0 = same & (notes[0:1] == expert)
    named = named0 | (same & (notes[1:2] == expert))
    i = lax.broadcasted_iota(jnp.int32, (columns, columns), 0)
    j = lax.broadcasted_iota(jnp.int32, (columns, columns), 1)
    earlier = jnp.where((i < j) & ((i >> 5) == (j >> 5)), 1.0, 0.0).astype(bf16)
    marked = jnp.where(named, 1.0, 0.0).astype(bf16)
    place = jnp.dot(marked, earlier, preferred_element_type=f32)
    taken = jnp.where(named & (place == (row & 15).astype(f32)), 1.0, 0.0)
    weight = jnp.sum(
        taken * jnp.where(named0, notes[2:3], notes[3:4]), axis=1, keepdims=True
    )
    taken = taken.astype(bf16)

    def put(start, size, value):
        for index, out in enumerate(outs):
            out[:, start : start + size] = value[index * 4 * slots : (index + 1) * 4 * slots]

    put(width, extra, jnp.broadcast_to(weight, (rows, extra)).astype(bf16))
    step = 512 if width % 512 == 0 else width
    for start in range(0, width, step):
        chunk = jnp.concatenate([ref[:, start : start + step] for ref in blocks], axis=0)
        put(start, step, jnp.dot(taken, chunk, preferred_element_type=f32).astype(bf16))


def select_rows(blocks, slots):
    shape = jax.ShapeDtypeStruct((4 * slots, blocks[0].shape[1]), bf16)
    return pl.pallas_call(
        select_kernel,
        out_shape=(shape,) * 4,
        in_specs=[whole] * 4,
        out_specs=(whole,) * 4,
        compiler_params=params,
        name="select_rows",
    )(*blocks)


def factor_kernel(saved, swapped_saved, mine, factors, later, hidden, kept, arrived):
    fetch = pltpu.make_async_copy(mine, kept, arrived)
    fetch.start()
    slots = saved.shape[2] // 16
    span, near, far = position()
    order, order_other = token_blocks(span, far), token_blocks(1 - span, near)

    def loaded(ref, which, block):
        at = pl.ds(pl.multiple_of(block * slots, slots), slots)
        gate, up = ref[which, 0, at, :].astype(f32), ref[which, 1, at, :].astype(f32)
        sigma = jax.nn.sigmoid(gate)
        silu = gate * sigma
        return up * sigma * (1.0 + gate * (1.0 - sigma)), silu, (silu * up).astype(bf16)

    for chunk in range(16):
        here = slice(chunk * slots, (chunk + 1) * slots)
        factors[0, here, :] = loaded(swapped_saved, span, order[chunk])[2].astype(f32)
        gate, up, product = loaded(saved, span, order[chunk])
        factors[1, here, :] = product.astype(f32)
        factors[2, here, :] = gate
        factors[3, here, :] = up
        hidden[0, here, :] = product
        later[0, here, :], later[1, here, :], hidden[1, here, :] = loaded(
            saved, 1 - span, order_other[chunk]
        )
    fetch.wait()


def saved_factors(saved, swapped_saved, mine):
    shape = saved.shape[2:]
    return pl.pallas_call(
        factor_kernel,
        out_shape=(
            jax.ShapeDtypeStruct((4,) + shape, f32),
            jax.ShapeDtypeStruct((2,) + shape, f32),
            jax.ShapeDtypeStruct((2,) + shape, bf16),
            jax.ShapeDtypeStruct(mine.shape, bf16),
        ),
        in_specs=[whole, whole, in_hbm],
        out_specs=(whole,) * 4,
        scratch_shapes=[pltpu.SemaphoreType.DMA],
        compiler_params=params,
        name="saved_factors",
    )(saved, swapped_saved, mine)


def slot_weights(notes, wide):
    return jnp.concatenate([notes.astype(f32)] * (wide // extra), axis=1)


def product_with(rows, weight):
    return lax.dot_general(
        rows, weight, (((1,), (1,)), ((), ())), preferred_element_type=f32
    )


def store_grads(out, raw, weights, gate, up, order):
    slots = raw.shape[0] // 16
    grad = weights * raw
    for part, factor in enumerate((gate, up)):
        value = (grad * factor).astype(bf16)
        for chunk in range(16):
            at = pl.ds(pl.multiple_of(order[chunk] * slots, slots), slots)
            out[part, at, :] = value[chunk * slots : (chunk + 1) * slots]


def raw_kernel(rows, mine, other, factors, grads, dots):
    count = rows.shape[0]
    width = rows.shape[1] - extra
    slots = count // 16
    core, _, far = position()
    order = token_blocks(core, far)
    raw_other = product_with(rows[:, :width], other[...])
    raw = product_with(rows[:, :width], mine[...])
    dot = jnp.sum(factors[0] * raw_other + factors[1] * raw, axis=1, keepdims=True)
    lane = lax.broadcasted_iota(jnp.int32, (count, 128), 1)
    row = lax.broadcasted_iota(jnp.int32, (count, 128), 0)
    spread = jnp.where(lane == (row & 15), dot, 0.0)
    for chunk in range(16):
        line = jnp.sum(spread[chunk * slots : (chunk + 1) * slots], axis=0, keepdims=True)
        for target in range(2):
            dots[pl.ds(order[chunk] * 2 + target, 1), :] = line
    weights = slot_weights(rows[:, width:], raw.shape[1])
    store_grads(grads, raw, weights, factors[2], factors[3], order)


def raw_grads(rows, mine, other, factors):
    return pl.pallas_call(
        raw_kernel,
        out_shape=(
            jax.ShapeDtypeStruct((2,) + factors.shape[1:], bf16),
            jax.ShapeDtypeStruct((32, 128), f32),
        ),
        in_specs=[whole] * 4,
        out_specs=(whole,) * 2,
        compiler_params=params,
        name="raw_grads",
    )(rows, mine, other, factors)


def finish_kernel(
    rows, notes, rows_other, notes_other, mine, hidden, later, grads, *refs
):
    tables, (pair_grads, weight_grad), passed = refs[:3], refs[3:5], refs[5:8]
    scaled, raw = refs[8:]
    count, wide = hidden.shape[1:]
    step = pl.program_id(0)
    span, near, _ = position()

    @pl.when(step == 0)
    def _():
        pair_grads[span] = grads[...]
        for table, out in zip(tables, passed, strict=True):
            out[...] = table[...]
        for index, ref in enumerate((notes, notes_other)):
            value = slot_weights(ref[...], wide) * hidden[index].astype(f32)
            scaled[:, index * count : (index + 1) * count] = value.T.astype(bf16)
        raw[...] = jnp.zeros_like(raw)

    total = jnp.dot(scaled[:, :count], rows[...], preferred_element_type=f32)
    total = total + jnp.dot(scaled[:, count:], rows_other[...], preferred_element_type=f32)
    weight_grad[...] = total.astype(bf16)
    columns = rows.shape[1]
    here = pl.ds(pl.multiple_of(step * columns, 128), columns)
    raw[...] += product_with(rows_other[...], mine[:, here])

    @pl.when(step == pl.num_programs(0) - 1)
    def _():
        store_grads(
            pair_grads.at[1 - span],
            raw[...],
            slot_weights(notes_other[...], wide),
            later[0],
            later[1],
            token_blocks(1 - span, near),
        )


def finished(rows, rows_other, mine, hidden, later, grads, tables):
    count, wide = hidden.shape[1:]
    width = rows.shape[1] - extra
    step = width // 2 if width % 256 == 0 else width

    def kept(value):
        return pl.BlockSpec(value.shape, lambda i: (0,) * len(value.shape))

    block = pl.BlockSpec((count, step), lambda i: (0, i))
    note = pl.BlockSpec((count, extra), lambda i: (0, width // extra))
    weight = pl.BlockSpec((wide, step), lambda i: (0, i))
    shapes = (
        jax.ShapeDtypeStruct((2,) + grads.shape, bf16),
        jax.ShapeDtypeStruct((wide, width), bf16),
        *(jax.ShapeDtypeStruct(table.shape, table.dtype) for table in tables),
    )
    inputs = (hidden, later, grads, *tables)
    return pl.pallas_call(
        finish_kernel,
        grid=(width // step,),
        out_shape=shapes,
        in_specs=[block, note, block, note, whole, *(kept(value) for value in inputs)],
        out_specs=(kept(shapes[0]), weight, *(kept(value) for value in shapes[2:])),
        scratch_shapes=[
            pltpu.VMEM((wide, 2 * count), bf16),
            pltpu.VMEM((count, wide), f32),
        ],
        compiler_params=params,
        name="finished",
    )(rows, rows, rows_other, rows_other, mine, *inputs)


def logit_kernel(returned, experts, places, scores, out):
    tokens = scores.shape[1]
    spread = lax.dot_general(
        returned[...],
        experts[...],
        (((0,), (0,)), ((), ())),
        preferred_element_type=f32,
        precision=lax.Precision.HIGHEST,
    )
    route = jnp.sum(spread * places[...], axis=0, keepdims=True)
    for span in range(2):
        first, second = 2 * span, 2 * span + 1
        route0 = route[:, first * tokens : (first + 1) * tokens]
        route1 = route[:, second * tokens : (second + 1) * tokens]
        score0, score1 = scores[first : first + 1], scores[second : second + 1]
        total = score0 + score1
        mean = (route0 * score0 + route1 * score1) / total
        scale = route_scale / total
        out[first : first + 1] = scale * (route0 - mean) * score0 * (1.0 - score0)
        out[second : second + 1] = scale * (route1 - mean) * score1 * (1.0 - score1)


def note_kernel(ids, logits, notes, core, experts, places, scores):
    tokens = ids.shape[1]
    score = jax.nn.sigmoid(logits[...])
    scores[...] = score
    number = ids[...]
    line = jnp.concatenate([number[row : row + 1] for row in range(4)], axis=1)
    lane = lax.broadcasted_iota(jnp.int32, (1, 4 * tokens), 1)
    source = lax.broadcasted_iota(jnp.int32, (32, 4 * tokens), 0)
    span = lane >> 6
    experts[...] = jnp.where(((source >> 2) == line) & ((source & 1) == span), 1.0, 0.0)
    expert = lax.broadcasted_iota(jnp.int32, (8, 4 * tokens), 0)
    marked = jnp.where(expert == line, 1.0, 0.0)
    i = lax.broadcasted_iota(jnp.int32, (4 * tokens, 4 * tokens), 0)
    j = lax.broadcasted_iota(jnp.int32, (4 * tokens, 4 * tokens), 1)
    earlier = jnp.where(((i >> 6) == (j >> 6)) & ((i & 31) < (j & 31)), 1.0, 0.0)
    before = jnp.dot(marked.astype(bf16), earlier.astype(bf16), preferred_element_type=f32)
    place = jnp.sum(before * marked, axis=0, keepdims=True)
    slot = lax.broadcasted_iota(jnp.int32, (128, 4 * tokens), 0).astype(f32)
    places[...] = jnp.where(slot == place, 1.0, 0.0)
    core[...] = jnp.broadcast_to(lax.axis_index("dp"), core.shape)
    first = lax.axis_index("dp") == 0
    pair = jnp.where(first, score[0:2], score[2:4])
    lines = [
        jnp.where(first, number[0:2], number[2:4]).astype(f32),
        route_scale * pair / (pair[0:1] + pair[1:2]),
        jnp.zeros((extra - 4, tokens), f32),
    ]
    table = jnp.concatenate(lines, axis=0)
    table = jnp.concatenate([table, jnp.zeros((extra, extra - tokens), f32)], axis=1)
    notes[...] = table.T[:tokens].astype(bf16)


def slot_notes(ids, logits):
    tokens = ids.shape[1]
    return pl.pallas_call(
        note_kernel,
        out_shape=(
            jax.ShapeDtypeStruct((tokens, extra), bf16),
            jax.ShapeDtypeStruct((tokens, 1), jnp.int32),
            jax.ShapeDtypeStruct((32, 4 * tokens), f32),
            jax.ShapeDtypeStruct((128, 4 * tokens), f32),
            jax.ShapeDtypeStruct((4, tokens), f32),
        ),
        in_specs=[whole] * 2,
        out_specs=(whole,) * 5,
        compiler_params=params,
        name="slot_notes",
    )(ids, logits)


def local(sent_down, sent_up, expert_ids, router_logits, saved_gate_up, down_weight):
    saved = saved_gate_up[:, 0, 0]
    mine = down_weight[0, 0]
    slots = saved.shape[2] // 16
    tokens, top = expert_ids.shape[2:]

    def by_slot(value):
        return jnp.swapaxes(value[:, 0], 1, 2).reshape(2 * top, tokens)

    count = lax.axis_size("pipe")
    from_above = lax.ppermute(
        sent_down[0], ("pipe", "dp"), [(2 * z, 2 * z - 2) for z in range(1, count)]
    )
    from_below = lax.ppermute(
        sent_up[0], ("pipe", "dp"), [(2 * z + 1, 2 * z + 3) for z in range(count - 1)]
    )
    notes, core, experts, places, scores = slot_notes(
        by_slot(expert_ids), by_slot(router_logits)
    )
    incoming = jnp.where(core == 0, from_above, from_below)
    block = jnp.concatenate([incoming, notes], axis=1)
    swapped_saved = swapped(saved)
    held, swapped_saved = lax.optimization_barrier((mine, swapped_saved))
    other = swapped(held)
    block, swapped_saved = lax.optimization_barrier((block, swapped_saved))

    blocks = [block] + [plane_shift(block, step, True) for step in shifts]
    factors, later, hidden, kept = saved_factors(saved, swapped_saved, mine)
    blocks[1], other, kept, factors, later, hidden = lax.optimization_barrier(
        (blocks[1], other, kept, factors, later, hidden)
    )
    pieces = select_rows(blocks, slots)
    pieces = [pieces[0]] + [
        plane_shift(piece, step, False) for piece, step in zip(pieces[1:], shifts, strict=True)
    ]
    rows = jnp.zeros((16 * slots, pieces[0].shape[1]), bf16)
    for index, piece in enumerate(pieces):
        rows = lax.dynamic_update_slice(rows, piece, (index * 4 * slots, 0))
    grads, dots = raw_grads(rows, kept, other, factors)
    returned = lax.all_to_all(dots, ("expert", "dp"), split_axis=0, concat_axis=0, tiled=True)
    pair_grads, weight_grad, experts, places, scores = finished(
        rows, swapped(rows), mine, hidden, later, grads, (experts, places, scores)
    )
    returned, pair_grads, weight_grad = lax.optimization_barrier(
        (returned, pair_grads, weight_grad)
    )
    logit_grads = pl.pallas_call(
        logit_kernel,
        out_shape=jax.ShapeDtypeStruct((2 * top, tokens), f32),
        in_specs=[whole] * 4,
        out_specs=whole,
        compiler_params=params,
        name="logit_grads",
    )(returned, experts, places, scores)
    return (
        pair_grads[:, None, None],
        weight_grad[None, None],
        jnp.swapaxes(logit_grads.reshape(2, 1, top, tokens), 2, 3),
    )


def solution(mesh):
    placed = (
        P("pipe", "expert", None),
        P("pipe", "expert", None),
        P(None, "pipe", "expert", None),
        P(None, "pipe", "expert", None),
        P(None, "pipe", "expert", None, None, "dp"),
        P("pipe", "expert", "dp", None),
    )
    return jax.shard_map(
        local,
        mesh=mesh,
        in_specs=placed,
        out_specs=(
            P(None, "pipe", "expert", None, None, "dp"),
            P("pipe", "expert", "dp", None),
            P(None, "pipe", "expert", None),
        ),
        check_vma=False,
    )
```

```python
import jax
import jax.numpy as jnp
from jax import lax
from jax.experimental import pallas as pl
from jax.experimental.pallas import tpu as pltpu
from jax.sharding import PartitionSpec as P

route_scale = 2.5
side = 4
shifts = (2, 1, -1)
extra = 128
bf16, f32 = jnp.bfloat16, jnp.float32
params = pltpu.CompilerParams(vmem_limit_bytes=16 * 2**20)
whole = pl.BlockSpec(memory_space=pltpu.VMEM)
in_hbm = pl.BlockSpec(memory_space=pltpu.HBM)


def moved(place, step, along_x):
    y, x = place // side, place % side
    return y * side + (x + step) % side if along_x else (y + step) % side * side + x


def plane_shift(value, step, first_along_x):
    pairs = [
        (place * 2 + core, moved(place, step, first_along_x == (core == 0)) * 2 + core)
        for place in range(side * side)
        for core in range(2)
    ]
    return lax.ppermute(value, ("expert", "dp"), pairs)


def swapped(value):
    return lax.ppermute(value, "dp", [(0, 1), (1, 0)])


def position():
    core, spot = lax.axis_index("dp"), lax.axis_index("expert")
    y, x = spot >> 2, spot & 3
    return core, jnp.where(core == 0, x, y), jnp.where(core == 0, y, x)


def token_blocks(core, far):
    places = [(far + side - step) & 3 for step in (0,) + shifts]
    return [
        jnp.where(core == 0, place * 4 + chunk, chunk * 4 + place)
        for place in places
        for chunk in range(side)
    ]


def select_kernel(*refs):
    blocks, outs = refs[:4], refs[4:]
    core, near, far = position()
    held = [(near + side - step) & 3 for step in (0,) + shifts]
    targets = [(far + side + step) & 3 for step in (0,) + shifts]
    wanted = [jnp.where(core == 0, t * 2 + (near >> 1), near * 2 + (t >> 1)) for t in targets]
    tokens, width = blocks[0].shape
    width -= extra
    slots = outs[0].shape[0] // 4
    rows, columns = 4 * outs[0].shape[0], 4 * tokens

    def pick(index, values):
        return jnp.where(
            index < 2,
            jnp.where(index == 0, values[0], values[1]),
            jnp.where(index == 2, values[2], values[3]),
        )

    notes = jnp.concatenate([ref[:, width:] for ref in blocks], axis=0).astype(f32).T
    row = lax.broadcasted_iota(jnp.int32, (rows, 1), 0)
    column = lax.broadcasted_iota(jnp.int32, (1, columns), 1)
    expert = pick(row >> 6, wanted).astype(f32)
    same = ((row >> 4) & 3) == pick(column >> 5, held)
    named0 = same & (notes[0:1] == expert)
    named = named0 | (same & (notes[1:2] == expert))
    i = lax.broadcasted_iota(jnp.int32, (columns, columns), 0)
    j = lax.broadcasted_iota(jnp.int32, (columns, columns), 1)
    earlier = jnp.where((i < j) & ((i >> 5) == (j >> 5)), 1.0, 0.0).astype(bf16)
    marked = jnp.where(named, 1.0, 0.0).astype(bf16)
    place = jnp.dot(marked, earlier, preferred_element_type=f32)
    taken = jnp.where(named & (place == (row & 15).astype(f32)), 1.0, 0.0)
    weight = jnp.sum(
        taken * jnp.where(named0, notes[2:3], notes[3:4]), axis=1, keepdims=True
    )
    taken = taken.astype(bf16)

    def put(start, size, value):
        for index, out in enumerate(outs):
            out[:, start : start + size] = value[index * 4 * slots : (index + 1) * 4 * slots]

    put(width, extra, jnp.broadcast_to(weight, (rows, extra)).astype(bf16))
    step = 512 if width % 512 == 0 else width
    for start in range(0, width, step):
        chunk = jnp.concatenate([ref[:, start : start + step] for ref in blocks], axis=0)
        put(start, step, jnp.dot(taken, chunk, preferred_element_type=f32).astype(bf16))


def select_rows(blocks, slots):
    shape = jax.ShapeDtypeStruct((4 * slots, blocks[0].shape[1]), bf16)
    return pl.pallas_call(
        select_kernel,
        out_shape=(shape,) * 4,
        in_specs=[whole] * 4,
        out_specs=(whole,) * 4,
        compiler_params=params,
        name="select_rows",
    )(*blocks)


def factor_kernel(saved, swapped_saved, mine, factors, hidden, kept, arrived):
    fetch = pltpu.make_async_copy(mine, kept, arrived)
    fetch.start()
    slots = saved.shape[2] // 16
    span, near, far = position()
    order, order_other = token_blocks(span, far), token_blocks(1 - span, near)

    def loaded(ref, which, block):
        at = pl.ds(pl.multiple_of(block * slots, slots), slots)
        gate, up = ref[which, 0, at, :].astype(f32), ref[which, 1, at, :].astype(f32)
        sigma = jax.nn.sigmoid(gate)
        silu = gate * sigma
        return (silu * up).astype(bf16), up * sigma * (1.0 + gate * (1.0 - sigma)), silu

    for chunk in range(16):
        here = slice(chunk * slots, (chunk + 1) * slots)
        for base, ref in ((0, swapped_saved), (3, saved)):
            product, gate, up = loaded(ref, span, order[chunk])
            factors[base, here, :] = product.astype(f32)
            factors[base + 1, here, :] = gate
            factors[base + 2, here, :] = up
        hidden[0, here, :] = product
        hidden[1, here, :] = loaded(saved, 1 - span, order_other[chunk])[0]
    fetch.wait()


def saved_factors(saved, swapped_saved, mine):
    shape = saved.shape[2:]
    return pl.pallas_call(
        factor_kernel,
        out_shape=(
            jax.ShapeDtypeStruct((6,) + shape, f32),
            jax.ShapeDtypeStruct((2,) + shape, bf16),
            jax.ShapeDtypeStruct(mine.shape, bf16),
        ),
        in_specs=[whole, whole, in_hbm],
        out_specs=(whole,) * 3,
        scratch_shapes=[pltpu.SemaphoreType.DMA],
        compiler_params=params,
        name="saved_factors",
    )(saved, swapped_saved, mine)


def slot_weights(notes, wide):
    return jnp.concatenate([notes.astype(f32)] * (wide // extra), axis=1)


def raw_values(pieces, mine, other, factors, start):
    width = pieces[0].shape[1] - extra
    rows = jnp.concatenate([piece[:, :width] for piece in pieces], axis=0)
    notes = jnp.concatenate([piece[:, width:] for piece in pieces], axis=0)
    count = rows.shape[0]
    here = slice(start, start + count)
    weights = slot_weights(notes, factors.shape[2])
    dot = jnp.zeros((count, 1), f32)
    values = []
    for base, weight in ((3, mine), (0, other)):
        raw = lax.dot_general(
            rows, weight[...], (((1,), (1,)), ((), ())), preferred_element_type=f32
        )
        dot = dot + jnp.sum(factors[base, here, :] * raw, axis=1, keepdims=True)
        grad = weights * raw
        for part in range(1, 3):
            values.append((grad * factors[base + part, here, :]).astype(bf16))
    lane = lax.broadcasted_iota(jnp.int32, (count, 128), 1)
    row = lax.broadcasted_iota(jnp.int32, (count, 128), 0)
    spread = jnp.where(lane == (row & 15), dot, 0.0)
    lines = [
        jnp.sum(spread[chunk : chunk + 16], axis=0, keepdims=True)
        for chunk in range(0, count, 16)
    ]
    return values, lines


def first_kernel(piece0, piece1, mine, other, factors, values, lines):
    results, sums = raw_values((piece0, piece1), mine, other, factors, 0)
    for index, value in enumerate(results):
        values[index] = value
    for index, line in enumerate(sums):
        lines[index : index + 1] = line


def first_grads(pieces, mine, other, factors):
    count = 2 * pieces[0].shape[0]
    return pl.pallas_call(
        first_kernel,
        out_shape=(
            jax.ShapeDtypeStruct((4, count, factors.shape[2]), bf16),
            jax.ShapeDtypeStruct((count // 16, 128), f32),
        ),
        in_specs=[whole] * 5,
        out_specs=(whole,) * 2,
        compiler_params=params,
        name="first_grads",
    )(*pieces, mine, other, factors)


def last_kernel(
    piece0, piece1, mine, other, factors, values, lines, g_mine, g_other, dots
):
    half = values.shape[1]
    core, _, far = position()
    order = token_blocks(core, far)
    results, sums = raw_values((piece0, piece1), mine, other, factors, half)
    for chunk in range(16):
        line = lines[chunk : chunk + 1] if chunk < 8 else sums[chunk - 8]
        for target in range(2):
            dots[pl.ds(order[chunk] * 2 + target, 1), :] = line
    for chunk in range(16):
        at = pl.ds(pl.multiple_of(order[chunk] * 16, 16), 16)
        start = chunk % 8 * 16
        for index in range(4):
            out = g_mine if index < 2 else g_other
            if chunk < 8:
                out[index % 2, at, :] = values[index, start : start + 16]
            else:
                out[index % 2, at, :] = results[index][start : start + 16]


def last_grads(pieces, mine, other, factors, values, lines):
    grads = jax.ShapeDtypeStruct((2,) + factors.shape[1:], bf16)
    return pl.pallas_call(
        last_kernel,
        out_shape=(grads, grads, jax.ShapeDtypeStruct((32, 128), f32)),
        in_specs=[whole] * 7,
        out_specs=(whole,) * 3,
        compiler_params=params,
        name="last_grads",
    )(*pieces, mine, other, factors, values, lines)


def finish_kernel(
    rows, notes, rows_other, notes_other, hidden, g_mine, g_other, *refs
):
    tables, (pair_grads, weight_grad), passed, scaled = refs[:3], refs[3:5], refs[5:8], refs[8]
    count, wide = hidden.shape[1:]

    @pl.when(pl.program_id(0) == 0)
    def _():
        span = lax.axis_index("dp")
        pair_grads[span] = g_mine[...]
        pair_grads[1 - span] = g_other[...]
        for table, out in zip(tables, passed, strict=True):
            out[...] = table[...]
        for index, ref in enumerate((notes, notes_other)):
            value = slot_weights(ref[...], wide) * hidden[index].astype(f32)
            scaled[:, index * count : (index + 1) * count] = value.T.astype(bf16)

    total = jnp.dot(scaled[:, :count], rows[...], preferred_element_type=f32)
    total = total + jnp.dot(scaled[:, count:], rows_other[...], preferred_element_type=f32)
    weight_grad[...] = total.astype(bf16)


def finished(rows, rows_other, hidden, g_mine, g_other, tables):
    count, wide = hidden.shape[1:]
    width = rows.shape[1] - extra
    step = width // 2 if width % 256 == 0 else width

    def kept(value):
        return pl.BlockSpec(value.shape, lambda i: (0,) * len(value.shape))

    block = pl.BlockSpec((count, step), lambda i: (0, i))
    note = pl.BlockSpec((count, extra), lambda i: (0, width // extra))
    shapes = (
        jax.ShapeDtypeStruct((2,) + g_mine.shape, bf16),
        jax.ShapeDtypeStruct((wide, width), bf16),
        *(jax.ShapeDtypeStruct(table.shape, table.dtype) for table in tables),
    )
    inputs = (hidden, g_mine, g_other, *tables)
    return pl.pallas_call(
        finish_kernel,
        grid=(width // step,),
        out_shape=shapes,
        in_specs=[block, note, block, note, *(kept(value) for value in inputs)],
        out_specs=(
            kept(shapes[0]),
            pl.BlockSpec((wide, step), lambda i: (0, i)),
            *(kept(value) for value in shapes[2:]),
        ),
        scratch_shapes=[pltpu.VMEM((wide, 2 * count), bf16)],
        compiler_params=params,
        name="finished",
    )(rows, rows, rows_other, rows_other, *inputs)


def logit_kernel(returned, experts, places, scores, out):
    tokens = scores.shape[1]
    left, parts = returned[...], []
    for _ in range(3):
        parts.append(left.astype(bf16))
        left = left - parts[-1].astype(f32)
    spread = lax.dot_general(
        jnp.concatenate(parts, axis=0),
        experts[...],
        (((0,), (0,)), ((), ())),
        preferred_element_type=f32,
    )
    slots = places.shape[0]
    route = jnp.sum(spread[:slots] * places[...], axis=0, keepdims=True)
    for span in range(2):
        first, second = 2 * span, 2 * span + 1
        route0 = route[:, first * tokens : (first + 1) * tokens]
        route1 = route[:, second * tokens : (second + 1) * tokens]
        score0, score1 = scores[first : first + 1], scores[second : second + 1]
        total = score0 + score1
        mean = (route0 * score0 + route1 * score1) / total
        scale = route_scale / total
        out[first : first + 1] = scale * (route0 - mean) * score0 * (1.0 - score0)
        out[second : second + 1] = scale * (route1 - mean) * score1 * (1.0 - score1)


def note_kernel(ids, logits, notes, core, experts, places, scores):
    tokens = ids.shape[1]
    score = jax.nn.sigmoid(logits[...])
    scores[...] = score
    number = ids[...]
    line = jnp.concatenate([number[row : row + 1] for row in range(4)], axis=1)
    lane = lax.broadcasted_iota(jnp.int32, (1, 4 * tokens), 1)
    source = lax.broadcasted_iota(jnp.int32, (32, 4 * tokens), 0)
    span = lane >> 6
    table = jnp.where(((source >> 2) == line) & ((source & 1) == span), 1.0, 0.0)
    experts[...] = jnp.concatenate([table] * 3, axis=0).astype(bf16)
    expert = lax.broadcasted_iota(jnp.int32, (8, 4 * tokens), 0)
    marked = jnp.where(expert == line, 1.0, 0.0)
    i = lax.broadcasted_iota(jnp.int32, (4 * tokens, 4 * tokens), 0)
    j = lax.broadcasted_iota(jnp.int32, (4 * tokens, 4 * tokens), 1)
    earlier = jnp.where(((i >> 6) == (j >> 6)) & ((i & 31) < (j & 31)), 1.0, 0.0)
    before = jnp.dot(marked.astype(bf16), earlier.astype(bf16), preferred_element_type=f32)
    place = jnp.sum(before * marked, axis=0, keepdims=True)
    slot = lax.broadcasted_iota(jnp.int32, places.shape, 0).astype(f32)
    places[...] = jnp.where(slot == place, 1.0, 0.0)
    core[...] = jnp.broadcast_to(lax.axis_index("dp"), core.shape)
    first = lax.axis_index("dp") == 0
    pair = jnp.where(first, score[0:2], score[2:4])
    lines = [
        jnp.where(first, number[0:2], number[2:4]).astype(f32),
        route_scale * pair / (pair[0:1] + pair[1:2]),
        jnp.zeros((extra - 4, tokens), f32),
    ]
    table = jnp.concatenate(lines, axis=0)
    table = jnp.concatenate([table, jnp.zeros((extra, extra - tokens), f32)], axis=1)
    notes[...] = table.T[:tokens].astype(bf16)


def slot_notes(ids, logits):
    tokens = ids.shape[1]
    return pl.pallas_call(
        note_kernel,
        out_shape=(
            jax.ShapeDtypeStruct((tokens, extra), bf16),
            jax.ShapeDtypeStruct((tokens, 1), jnp.int32),
            jax.ShapeDtypeStruct((96, 4 * tokens), bf16),
            jax.ShapeDtypeStruct((16, 4 * tokens), f32),
            jax.ShapeDtypeStruct((4, tokens), f32),
        ),
        in_specs=[whole] * 2,
        out_specs=(whole,) * 5,
        compiler_params=params,
        name="slot_notes",
    )(ids, logits)


def local(sent_down, sent_up, expert_ids, router_logits, saved_gate_up, down_weight):
    saved = saved_gate_up[:, 0, 0]
    mine = down_weight[0, 0]
    slots = saved.shape[2] // 16
    tokens, top = expert_ids.shape[2:]

    def by_slot(value):
        return jnp.swapaxes(value[:, 0], 1, 2).reshape(2 * top, tokens)

    count = lax.axis_size("pipe")
    from_above = lax.ppermute(
        sent_down[0], ("pipe", "dp"), [(2 * z, 2 * z - 2) for z in range(1, count)]
    )
    from_below = lax.ppermute(
        sent_up[0], ("pipe", "dp"), [(2 * z + 1, 2 * z + 3) for z in range(count - 1)]
    )
    notes, core, experts, places, scores = slot_notes(
        by_slot(expert_ids), by_slot(router_logits)
    )
    incoming = jnp.where(core == 0, from_above, from_below)
    block = jnp.concatenate([incoming, notes], axis=1)
    swapped_saved = swapped(saved)
    held, swapped_saved = lax.optimization_barrier((mine, swapped_saved))
    other = swapped(held)
    block, swapped_saved = lax.optimization_barrier((block, swapped_saved))

    blocks = [block] + [plane_shift(block, step, True) for step in shifts]
    factors, hidden, kept = saved_factors(saved, swapped_saved, mine)
    blocks[1], other, kept, factors, hidden = lax.optimization_barrier(
        (blocks[1], other, kept, factors, hidden)
    )
    pieces = select_rows(blocks, slots)
    pieces = [pieces[0]] + [
        plane_shift(piece, step, False) for piece, step in zip(pieces[1:], shifts, strict=True)
    ]
    values, lines = first_grads(pieces[:2], kept, other, factors)
    pieces[2], values, lines = lax.optimization_barrier((pieces[2], values, lines))
    rows = jnp.zeros((16 * slots, pieces[0].shape[1]), bf16)
    for index, piece in enumerate(pieces):
        rows = lax.dynamic_update_slice(rows, piece, (index * 4 * slots, 0))
    g_mine, g_other, dots = last_grads(pieces[2:], kept, other, factors, values, lines)
    returned = lax.all_to_all(dots, ("expert", "dp"), split_axis=0, concat_axis=0, tiled=True)
    pair_grads, weight_grad, experts, places, scores = finished(
        rows, swapped(rows), hidden, g_mine, swapped(g_other), (experts, places, scores)
    )
    returned, pair_grads, weight_grad = lax.optimization_barrier(
        (returned, pair_grads, weight_grad)
    )
    logit_grads = pl.pallas_call(
        logit_kernel,
        out_shape=jax.ShapeDtypeStruct((2 * top, tokens), f32),
        in_specs=[whole] * 4,
        out_specs=whole,
        compiler_params=params,
        name="logit_grads",
    )(returned, experts, places, scores)
    return (
        pair_grads[:, None, None],
        weight_grad[None, None],
        jnp.swapaxes(logit_grads.reshape(2, 1, top, tokens), 2, 3),
    )


def solution(mesh):
    placed = (
        P("pipe", "expert", None),
        P("pipe", "expert", None),
        P(None, "pipe", "expert", None),
        P(None, "pipe", "expert", None),
        P(None, "pipe", "expert", None, None, "dp"),
        P("pipe", "expert", "dp", None),
    )
    return jax.shard_map(
        local,
        mesh=mesh,
        in_specs=placed,
        out_specs=(
            P(None, "pipe", "expert", None, None, "dp"),
            P("pipe", "expert", "dp", None),
            P(None, "pipe", "expert", None),
        ),
        check_vma=False,
    )
```

```python
import jax
import jax.numpy as jnp
from jax import lax
from jax.experimental import pallas as pl
from jax.experimental.pallas import tpu as pltpu
from jax.sharding import PartitionSpec as P

route_scale = 2.5
side = 4
shifts = (2, 1, -1)
extra = 128
bf16, f32 = jnp.bfloat16, jnp.float32
params = pltpu.CompilerParams(vmem_limit_bytes=16 * 2**20)
whole = pl.BlockSpec(memory_space=pltpu.VMEM)
in_hbm = pl.BlockSpec(memory_space=pltpu.HBM)


def moved(place, step, along_x):
    y, x = place // side, place % side
    return y * side + (x + step) % side if along_x else (y + step) % side * side + x


def plane_shift(value, step, first_along_x):
    pairs = [
        (place * 2 + core, moved(place, step, first_along_x == (core == 0)) * 2 + core)
        for place in range(side * side)
        for core in range(2)
    ]
    return lax.ppermute(value, ("expert", "dp"), pairs)


def swapped(value):
    return lax.ppermute(value, "dp", [(0, 1), (1, 0)])


def position():
    core, spot = lax.axis_index("dp"), lax.axis_index("expert")
    y, x = spot >> 2, spot & 3
    return core, jnp.where(core == 0, x, y), jnp.where(core == 0, y, x)


def token_blocks(core, far):
    places = [(far + side - step) & 3 for step in (0,) + shifts]
    return [
        jnp.where(core == 0, place * 4 + chunk, chunk * 4 + place)
        for place in places
        for chunk in range(side)
    ]


def select_kernel(*refs):
    blocks, outs = refs[:4], refs[4:]
    core, near, far = position()
    held = [(near + side - step) & 3 for step in (0,) + shifts]
    targets = [(far + side + step) & 3 for step in (0,) + shifts]
    wanted = [jnp.where(core == 0, t * 2 + (near >> 1), near * 2 + (t >> 1)) for t in targets]
    tokens, width = blocks[0].shape
    width -= extra
    slots = outs[0].shape[0] // 4
    rows, columns = 4 * outs[0].shape[0], 4 * tokens

    def pick(index, values):
        return jnp.where(
            index < 2,
            jnp.where(index == 0, values[0], values[1]),
            jnp.where(index == 2, values[2], values[3]),
        )

    notes = jnp.concatenate([ref[:, width:] for ref in blocks], axis=0).astype(f32).T
    row = lax.broadcasted_iota(jnp.int32, (rows, 1), 0)
    column = lax.broadcasted_iota(jnp.int32, (1, columns), 1)
    expert = pick(row >> 6, wanted).astype(f32)
    same = ((row >> 4) & 3) == pick(column >> 5, held)
    named0 = same & (notes[0:1] == expert)
    named = named0 | (same & (notes[1:2] == expert))
    i = lax.broadcasted_iota(jnp.int32, (columns, columns), 0)
    j = lax.broadcasted_iota(jnp.int32, (columns, columns), 1)
    earlier = jnp.where((i < j) & ((i >> 5) == (j >> 5)), 1.0, 0.0).astype(bf16)
    marked = jnp.where(named, 1.0, 0.0).astype(bf16)
    place = jnp.dot(marked, earlier, preferred_element_type=f32)
    taken = jnp.where(named & (place == (row & 15).astype(f32)), 1.0, 0.0)
    weight = jnp.sum(
        taken * jnp.where(named0, notes[2:3], notes[3:4]), axis=1, keepdims=True
    )
    taken = taken.astype(bf16)

    def put(start, size, value):
        for index, out in enumerate(outs):
            out[:, start : start + size] = value[index * 4 * slots : (index + 1) * 4 * slots]

    put(width, extra, jnp.broadcast_to(weight, (rows, extra)).astype(bf16))
    step = 512 if width % 512 == 0 else width
    for start in range(0, width, step):
        chunk = jnp.concatenate([ref[:, start : start + step] for ref in blocks], axis=0)
        put(start, step, jnp.dot(taken, chunk, preferred_element_type=f32).astype(bf16))


def select_rows(blocks, slots):
    shape = jax.ShapeDtypeStruct((4 * slots, blocks[0].shape[1]), bf16)
    return pl.pallas_call(
        select_kernel,
        out_shape=(shape,) * 4,
        in_specs=[whole] * 4,
        out_specs=(whole,) * 4,
        compiler_params=params,
        name="select_rows",
    )(*blocks)


def factor_kernel(saved, swapped_saved, mine, factors, hidden, kept, arrived):
    fetch = pltpu.make_async_copy(mine, kept, arrived)
    fetch.start()
    slots = saved.shape[2] // 16
    span, near, far = position()
    order, order_other = token_blocks(span, far), token_blocks(1 - span, near)

    def loaded(ref, which, block):
        at = pl.ds(pl.multiple_of(block * slots, slots), slots)
        gate, up = ref[which, 0, at, :].astype(f32), ref[which, 1, at, :].astype(f32)
        sigma = jax.nn.sigmoid(gate)
        silu = gate * sigma
        return (silu * up).astype(bf16), up * sigma * (1.0 + gate * (1.0 - sigma)), silu

    for chunk in range(16):
        here = slice(chunk * slots, (chunk + 1) * slots)
        for base, ref in ((0, swapped_saved), (3, saved)):
            product, gate, up = loaded(ref, span, order[chunk])
            factors[base, here, :] = product.astype(f32)
            factors[base + 1, here, :] = gate
            factors[base + 2, here, :] = up
        hidden[0, here, :] = product
        hidden[1, here, :] = loaded(saved, 1 - span, order_other[chunk])[0]
    fetch.wait()


def saved_factors(saved, swapped_saved, mine):
    shape = saved.shape[2:]
    return pl.pallas_call(
        factor_kernel,
        out_shape=(
            jax.ShapeDtypeStruct((6,) + shape, f32),
            jax.ShapeDtypeStruct((2,) + shape, bf16),
            jax.ShapeDtypeStruct(mine.shape, bf16),
        ),
        in_specs=[whole, whole, in_hbm],
        out_specs=(whole,) * 3,
        scratch_shapes=[pltpu.SemaphoreType.DMA],
        compiler_params=params,
        name="saved_factors",
    )(saved, swapped_saved, mine)


def slot_weights(notes, wide):
    return jnp.concatenate([notes.astype(f32)] * (wide // extra), axis=1)


def raw_values(pieces, mine, other, factors, start):
    width = pieces[0].shape[1] - extra
    rows = jnp.concatenate([piece[:, :width] for piece in pieces], axis=0)
    notes = jnp.concatenate([piece[:, width:] for piece in pieces], axis=0)
    count = rows.shape[0]
    here = slice(start, start + count)
    weights = slot_weights(notes, factors.shape[2])
    dot = jnp.zeros((count, 1), f32)
    values = []
    for base, weight in ((3, mine), (0, other)):
        raw = lax.dot_general(
            rows, weight[...], (((1,), (1,)), ((), ())), preferred_element_type=f32
        )
        dot = dot + jnp.sum(factors[base, here, :] * raw, axis=1, keepdims=True)
        grad = weights * raw
        for part in range(1, 3):
            values.append((grad * factors[base + part, here, :]).astype(bf16))
    lane = lax.broadcasted_iota(jnp.int32, (count, 128), 1)
    row = lax.broadcasted_iota(jnp.int32, (count, 128), 0)
    spread = jnp.where(lane == (row & 15), dot, 0.0)
    lines = [
        jnp.sum(spread[chunk : chunk + 16], axis=0, keepdims=True)
        for chunk in range(0, count, 16)
    ]
    return values, lines


def first_kernel(piece0, piece1, mine, other, factors, g_mine, g_other, lines):
    results, sums = raw_values((piece0, piece1), mine, other, factors, 0)
    g_mine[0], g_mine[1], g_other[0], g_other[1] = results
    for index, line in enumerate(sums):
        lines[index : index + 1] = line


def first_grads(pieces, mine, other, factors):
    count = 2 * pieces[0].shape[0]
    grads = jax.ShapeDtypeStruct((2, count, factors.shape[2]), bf16)
    return pl.pallas_call(
        first_kernel,
        out_shape=(grads, grads, jax.ShapeDtypeStruct((count // 16, 128), f32)),
        in_specs=[whole] * 5,
        out_specs=(whole,) * 3,
        compiler_params=params,
        name="first_grads",
    )(*pieces, mine, other, factors)


def last_kernel(piece0, piece1, mine, other, factors, lines, g_mine, g_other, dots):
    core, _, far = position()
    order = token_blocks(core, far)
    for chunk in range(8):
        for target in range(2):
            dots[pl.ds(order[chunk] * 2 + target, 1), :] = lines[chunk : chunk + 1]
    start = 2 * piece0.shape[0]
    results, sums = raw_values((piece0, piece1), mine, other, factors, start)
    for chunk in range(8):
        for target in range(2):
            dots[pl.ds(order[8 + chunk] * 2 + target, 1), :] = sums[chunk]
    g_mine[0], g_mine[1], g_other[0], g_other[1] = results


def last_grads(pieces, mine, other, factors, lines):
    count = 2 * pieces[0].shape[0]
    grads = jax.ShapeDtypeStruct((2, count, factors.shape[2]), bf16)
    return pl.pallas_call(
        last_kernel,
        out_shape=(grads, grads, jax.ShapeDtypeStruct((32, 128), f32)),
        in_specs=[whole] * 6,
        out_specs=(whole,) * 3,
        compiler_params=params,
        name="last_grads",
    )(*pieces, mine, other, factors, lines)


def finish_kernel(
    rows, notes, rows_other, notes_other, hidden, mine0, mine1, other0, other1, *refs
):
    tables, (pair_grads, weight_grad), passed, scaled = refs[:3], refs[3:5], refs[5:8], refs[8]
    count, wide = hidden.shape[1:]

    @pl.when(pl.program_id(0) == 0)
    def _():
        span, near, far = position()
        for which, order, halves in (
            (span, token_blocks(span, far), (mine0, mine1)),
            (1 - span, token_blocks(1 - span, near), (other0, other1)),
        ):
            for chunk in range(16):
                at = pl.ds(pl.multiple_of(order[chunk] * 16, 16), 16)
                start = chunk % 8 * 16
                for part in range(2):
                    value = halves[chunk // 8][part, start : start + 16, :]
                    pair_grads[which, part, at, :] = value
        for table, out in zip(tables, passed, strict=True):
            out[...] = table[...]
        for index, ref in enumerate((notes, notes_other)):
            value = slot_weights(ref[...], wide) * hidden[index].astype(f32)
            scaled[:, index * count : (index + 1) * count] = value.T.astype(bf16)

    total = jnp.dot(scaled[:, :count], rows[...], preferred_element_type=f32)
    total = total + jnp.dot(scaled[:, count:], rows_other[...], preferred_element_type=f32)
    weight_grad[...] = total.astype(bf16)


def finished(rows, rows_other, hidden, grads, tables):
    count, wide = hidden.shape[1:]
    width = rows.shape[1] - extra
    step = width // 2 if width % 256 == 0 else width

    def kept(value):
        return pl.BlockSpec(value.shape, lambda i: (0,) * len(value.shape))

    block = pl.BlockSpec((count, step), lambda i: (0, i))
    note = pl.BlockSpec((count, extra), lambda i: (0, width // extra))
    shapes = (
        jax.ShapeDtypeStruct((2, 2, count, wide), bf16),
        jax.ShapeDtypeStruct((wide, width), bf16),
        *(jax.ShapeDtypeStruct(table.shape, table.dtype) for table in tables),
    )
    inputs = (hidden, *grads, *tables)
    return pl.pallas_call(
        finish_kernel,
        grid=(width // step,),
        out_shape=shapes,
        in_specs=[block, note, block, note, *(kept(value) for value in inputs)],
        out_specs=(
            kept(shapes[0]),
            pl.BlockSpec((wide, step), lambda i: (0, i)),
            *(kept(value) for value in shapes[2:]),
        ),
        scratch_shapes=[pltpu.VMEM((wide, 2 * count), bf16)],
        compiler_params=params,
        name="finished",
    )(rows, rows, rows_other, rows_other, *inputs)


def logit_kernel(returned, experts, places, scores, out):
    tokens = scores.shape[1]
    left, parts = returned[...], []
    for _ in range(3):
        parts.append(left.astype(bf16))
        left = left - parts[-1].astype(f32)
    spread = lax.dot_general(
        jnp.concatenate(parts, axis=0),
        experts[...],
        (((0,), (0,)), ((), ())),
        preferred_element_type=f32,
    )
    slots = places.shape[0]
    route = jnp.sum(spread[:slots] * places[...], axis=0, keepdims=True)
    for span in range(2):
        first, second = 2 * span, 2 * span + 1
        route0 = route[:, first * tokens : (first + 1) * tokens]
        route1 = route[:, second * tokens : (second + 1) * tokens]
        score0, score1 = scores[first : first + 1], scores[second : second + 1]
        total = score0 + score1
        mean = (route0 * score0 + route1 * score1) / total
        scale = route_scale / total
        out[first : first + 1] = scale * (route0 - mean) * score0 * (1.0 - score0)
        out[second : second + 1] = scale * (route1 - mean) * score1 * (1.0 - score1)


def note_kernel(ids, logits, notes, core, experts, places, scores):
    tokens = ids.shape[1]
    score = jax.nn.sigmoid(logits[...])
    scores[...] = score
    number = ids[...]
    line = jnp.concatenate([number[row : row + 1] for row in range(4)], axis=1)
    lane = lax.broadcasted_iota(jnp.int32, (1, 4 * tokens), 1)
    source = lax.broadcasted_iota(jnp.int32, (32, 4 * tokens), 0)
    span = lane >> 6
    table = jnp.where(((source >> 2) == line) & ((source & 1) == span), 1.0, 0.0)
    experts[...] = jnp.concatenate([table] * 3, axis=0).astype(bf16)
    expert = lax.broadcasted_iota(jnp.int32, (8, 4 * tokens), 0)
    marked = jnp.where(expert == line, 1.0, 0.0)
    i = lax.broadcasted_iota(jnp.int32, (4 * tokens, 4 * tokens), 0)
    j = lax.broadcasted_iota(jnp.int32, (4 * tokens, 4 * tokens), 1)
    earlier = jnp.where(((i >> 6) == (j >> 6)) & ((i & 31) < (j & 31)), 1.0, 0.0)
    before = jnp.dot(marked.astype(bf16), earlier.astype(bf16), preferred_element_type=f32)
    place = jnp.sum(before * marked, axis=0, keepdims=True)
    slot = lax.broadcasted_iota(jnp.int32, places.shape, 0).astype(f32)
    places[...] = jnp.where(slot == place, 1.0, 0.0)
    core[...] = jnp.broadcast_to(lax.axis_index("dp"), core.shape)
    first = lax.axis_index("dp") == 0
    pair = jnp.where(first, score[0:2], score[2:4])
    lines = [
        jnp.where(first, number[0:2], number[2:4]).astype(f32),
        route_scale * pair / (pair[0:1] + pair[1:2]),
        jnp.zeros((extra - 4, tokens), f32),
    ]
    table = jnp.concatenate(lines, axis=0)
    table = jnp.concatenate([table, jnp.zeros((extra, extra - tokens), f32)], axis=1)
    notes[...] = table.T[:tokens].astype(bf16)


def slot_notes(ids, logits):
    tokens = ids.shape[1]
    return pl.pallas_call(
        note_kernel,
        out_shape=(
            jax.ShapeDtypeStruct((tokens, extra), bf16),
            jax.ShapeDtypeStruct((tokens, 1), jnp.int32),
            jax.ShapeDtypeStruct((96, 4 * tokens), bf16),
            jax.ShapeDtypeStruct((16, 4 * tokens), f32),
            jax.ShapeDtypeStruct((4, tokens), f32),
        ),
        in_specs=[whole] * 2,
        out_specs=(whole,) * 5,
        compiler_params=params,
        name="slot_notes",
    )(ids, logits)


def local(sent_down, sent_up, expert_ids, router_logits, saved_gate_up, down_weight):
    saved = saved_gate_up[:, 0, 0]
    mine = down_weight[0, 0]
    slots = saved.shape[2] // 16
    tokens, top = expert_ids.shape[2:]

    def by_slot(value):
        return jnp.swapaxes(value[:, 0], 1, 2).reshape(2 * top, tokens)

    count = lax.axis_size("pipe")
    from_above = lax.ppermute(
        sent_down[0], ("pipe", "dp"), [(2 * z, 2 * z - 2) for z in range(1, count)]
    )
    from_below = lax.ppermute(
        sent_up[0], ("pipe", "dp"), [(2 * z + 1, 2 * z + 3) for z in range(count - 1)]
    )
    notes, core, experts, places, scores = slot_notes(
        by_slot(expert_ids), by_slot(router_logits)
    )
    notes, held = lax.optimization_barrier((notes, mine))
    other = swapped(held)
    incoming = jnp.where(core == 0, from_above, from_below)
    block = jnp.concatenate([incoming, notes], axis=1)
    block, swapped_saved = lax.optimization_barrier((block, swapped(saved)))

    blocks = [block] + [plane_shift(block, step, True) for step in shifts]
    factors, hidden, kept = saved_factors(saved, swapped_saved, mine)
    blocks[2], kept, factors, hidden = lax.optimization_barrier(
        (blocks[2], kept, factors, hidden)
    )
    pieces = select_rows(blocks, slots)
    pieces = [pieces[0]] + [
        plane_shift(piece, step, False) for piece, step in zip(pieces[1:], shifts, strict=True)
    ]
    mine0, other0, lines = first_grads(pieces[:2], kept, other, factors)
    pieces[2], mine0, other0, lines = lax.optimization_barrier(
        (pieces[2], mine0, other0, lines)
    )
    rows = jnp.zeros((16 * slots, pieces[0].shape[1]), bf16)
    for index, piece in enumerate(pieces):
        rows = lax.dynamic_update_slice(rows, piece, (index * 4 * slots, 0))
    mine1, other1, dots = last_grads(pieces[2:], kept, other, factors, lines)
    returned = lax.all_to_all(dots, ("expert", "dp"), split_axis=0, concat_axis=0, tiled=True)
    pair_grads, weight_grad, experts, places, scores = finished(
        rows,
        swapped(rows),
        hidden,
        (mine0, mine1, swapped(other0), swapped(other1)),
        (experts, places, scores),
    )
    returned, pair_grads, weight_grad = lax.optimization_barrier(
        (returned, pair_grads, weight_grad)
    )
    logit_grads = pl.pallas_call(
        logit_kernel,
        out_shape=jax.ShapeDtypeStruct((2 * top, tokens), f32),
        in_specs=[whole] * 4,
        out_specs=whole,
        compiler_params=params,
        name="logit_grads",
    )(returned, experts, places, scores)
    return (
        pair_grads[:, None, None],
        weight_grad[None, None],
        jnp.swapaxes(logit_grads.reshape(2, 1, top, tokens), 2, 3),
    )


def solution(mesh):
    placed = (
        P("pipe", "expert", None),
        P("pipe", "expert", None),
        P(None, "pipe", "expert", None),
        P(None, "pipe", "expert", None),
        P(None, "pipe", "expert", None, None, "dp"),
        P("pipe", "expert", "dp", None),
    )
    return jax.shard_map(
        local,
        mesh=mesh,
        in_specs=placed,
        out_specs=(
            P(None, "pipe", "expert", None, None, "dp"),
            P("pipe", "expert", "dp", None),
            P(None, "pipe", "expert", None),
        ),
        check_vma=False,
    )
```

```python
import jax
import jax.numpy as jnp
from jax import lax
from jax.experimental import pallas as pl
from jax.experimental.pallas import tpu as pltpu
from jax.sharding import PartitionSpec as P

route_scale = 2.5
side = 4
shifts = (2, 1, -1)
extra = 128
bf16, f32 = jnp.bfloat16, jnp.float32
params = pltpu.CompilerParams(vmem_limit_bytes=16 * 2**20)
whole = pl.BlockSpec(memory_space=pltpu.VMEM)


def moved(place, step, along_x):
    y, x = place // side, place % side
    return y * side + (x + step) % side if along_x else (y + step) % side * side + x


def plane_shift(value, step, first_along_x):
    pairs = [
        (place * 2 + core, moved(place, step, first_along_x == (core == 0)) * 2 + core)
        for place in range(side * side)
        for core in range(2)
    ]
    return lax.ppermute(value, ("expert", "dp"), pairs)


def swapped(value):
    return lax.ppermute(value, "dp", [(0, 1), (1, 0)])


def position():
    core, spot = lax.axis_index("dp"), lax.axis_index("expert")
    y, x = spot >> 2, spot & 3
    return core, jnp.where(core == 0, x, y), jnp.where(core == 0, y, x)


def token_blocks(core, near, far):
    steps = (0,) + shifts
    places = [(far + side - step) & 3 for step in steps]
    holders = [(near + side - step) & 3 for step in steps]
    return [
        jnp.where(core == 0, place * 4 + holder, holder * 4 + place)
        for place in places
        for holder in holders
    ]


def select_kernel(*refs):
    blocks, outs = refs[:-4], refs[-4:]
    core, near, far = position()
    targets = [(far + side + step) & 3 for step in (0,) + shifts]
    wanted = [jnp.where(core == 0, t * 2 + (near >> 1), near * 2 + (t >> 1)) for t in targets]
    tokens, width = blocks[0].shape
    width -= extra
    count, size = len(blocks), outs[0].shape[0]
    rows, columns = 4 * size, 128
    used = count * tokens

    notes = [ref[:, width:] for ref in blocks]
    if used < columns:
        notes.append(jnp.zeros((columns - used, extra), bf16))
    notes = jnp.concatenate(notes, axis=0).astype(f32).T
    row = lax.broadcasted_iota(jnp.int32, (rows, 1), 0)
    column = lax.broadcasted_iota(jnp.int32, (1, columns), 1)
    later = [row >= size * target for target in range(1, 4)]
    expert = jnp.where(later[0], wanted[1], wanted[0])
    expert = jnp.where(later[1], wanted[2], expert)
    expert = jnp.where(later[2], wanted[3], expert).astype(f32)
    target = sum(passed.astype(jnp.int32) for passed in later)
    same = ((row >> 4) - target * count) == (column >> 5)
    named0 = same & (notes[0:1] == expert)
    named = named0 | (same & (notes[1:2] == expert))
    i = lax.broadcasted_iota(jnp.int32, (columns, columns), 0)
    j = lax.broadcasted_iota(jnp.int32, (columns, columns), 1)
    earlier = jnp.where((i < j) & ((i >> 5) == (j >> 5)), 1.0, 0.0).astype(bf16)
    marked = jnp.where(named, 1.0, 0.0).astype(bf16)
    place = jnp.dot(marked, earlier, preferred_element_type=f32)
    taken = jnp.where(named & (place == (row & 15).astype(f32)), 1.0, 0.0)
    weight = jnp.sum(
        taken * jnp.where(named0, notes[2:3], notes[3:4]), axis=1, keepdims=True
    )
    taken = taken[:, :used].astype(bf16)

    def put(start, step, value):
        for index, out in enumerate(outs):
            out[:, start : start + step] = value[index * size : (index + 1) * size]

    put(width, extra, jnp.broadcast_to(weight, (rows, extra)).astype(bf16))
    step = 512 if width % 512 == 0 else width
    for start in range(0, width, step):
        chunk = jnp.concatenate([ref[:, start : start + step] for ref in blocks], axis=0)
        put(start, step, jnp.dot(taken, chunk, preferred_element_type=f32).astype(bf16))


def select_rows(blocks, slots):
    shape = jax.ShapeDtypeStruct((len(blocks) * slots, blocks[0].shape[1]), bf16)
    return pl.pallas_call(
        select_kernel,
        out_shape=(shape,) * 4,
        in_specs=[whole] * len(blocks),
        out_specs=(whole,) * 4,
        compiler_params=params,
        name="select_rows",
    )(*blocks)


def factor_kernel(saved, swapped_saved, factors, later, hidden):
    slots = saved.shape[2] // 16
    span, near, far = position()
    order, order_other = token_blocks(span, near, far), token_blocks(1 - span, far, near)

    def loaded(ref, which, block):
        at = pl.ds(pl.multiple_of(block * slots, slots), slots)
        gate, up = ref[which, 0, at, :].astype(f32), ref[which, 1, at, :].astype(f32)
        sigma = jax.nn.sigmoid(gate)
        silu = gate * sigma
        return up * sigma * (1.0 + gate * (1.0 - sigma)), silu, (silu * up).astype(bf16)

    for chunk in range(16):
        here = slice(chunk * slots, (chunk + 1) * slots)
        factors[0, here, :] = loaded(swapped_saved, span, order[chunk])[2].astype(f32)
        gate, up, product = loaded(saved, span, order[chunk])
        factors[1, here, :] = product.astype(f32)
        factors[2, here, :] = gate
        factors[3, here, :] = up
        hidden[0, here, :] = product
        later[0, here, :], later[1, here, :], hidden[1, here, :] = loaded(
            saved, 1 - span, order_other[chunk]
        )


def saved_factors(saved, swapped_saved):
    shape = saved.shape[2:]
    return pl.pallas_call(
        factor_kernel,
        out_shape=(
            jax.ShapeDtypeStruct((4,) + shape, f32),
            jax.ShapeDtypeStruct((2,) + shape, f32),
            jax.ShapeDtypeStruct((2,) + shape, bf16),
        ),
        in_specs=[whole] * 2,
        out_specs=(whole,) * 3,
        compiler_params=params,
        name="saved_factors",
    )(saved, swapped_saved)


def slot_weights(notes, wide):
    return jnp.concatenate([notes.astype(f32)] * (wide // extra), axis=1)


def product_with(rows, weight):
    return lax.dot_general(
        rows, weight, (((1,), (1,)), ((), ())), preferred_element_type=f32
    )


def store_grads(out, raw, weights, gate, up, order):
    slots = raw.shape[0] // 16
    grad = weights * raw
    for part, factor in enumerate((gate, up)):
        value = (grad * factor).astype(bf16)
        for chunk in range(16):
            at = pl.ds(pl.multiple_of(order[chunk] * slots, slots), slots)
            out[part, at, :] = value[chunk * slots : (chunk + 1) * slots]


def raw_kernel(rows, mine, other, factors, grads, dots):
    count = rows.shape[0]
    width = rows.shape[1] - extra
    slots = count // 16
    order = token_blocks(*position())
    raw_other = product_with(rows[:, :width], other[...])
    raw = product_with(rows[:, :width], mine[...])
    dot = jnp.sum(factors[0] * raw_other + factors[1] * raw, axis=1, keepdims=True)
    lane = lax.broadcasted_iota(jnp.int32, (count, 128), 1)
    row = lax.broadcasted_iota(jnp.int32, (count, 128), 0)
    spread = jnp.where(lane == (row & 15), dot, 0.0)
    for chunk in range(16):
        line = jnp.sum(spread[chunk * slots : (chunk + 1) * slots], axis=0, keepdims=True)
        for target in range(2):
            dots[pl.ds(order[chunk] * 2 + target, 1), :] = line
    weights = slot_weights(rows[:, width:], raw.shape[1])
    store_grads(grads, raw, weights, factors[2], factors[3], order)


def raw_grads(rows, mine, other, factors):
    return pl.pallas_call(
        raw_kernel,
        out_shape=(
            jax.ShapeDtypeStruct((2,) + factors.shape[1:], bf16),
            jax.ShapeDtypeStruct((32, 128), f32),
        ),
        in_specs=[whole] * 4,
        out_specs=(whole,) * 2,
        compiler_params=params,
        name="raw_grads",
    )(rows, mine, other, factors)


def finish_kernel(
    rows, notes, rows_other, notes_other, mine, hidden, later, grads, *refs
):
    tables, (pair_grads, weight_grad), passed = refs[:3], refs[3:5], refs[5:8]
    scaled, raw = refs[8:]
    count, wide = hidden.shape[1:]
    step = pl.program_id(0)
    span, near, far = position()

    @pl.when(step == 0)
    def _():
        pair_grads[span] = grads[...]
        for table, out in zip(tables, passed, strict=True):
            out[...] = table[...]
        for index, ref in enumerate((notes, notes_other)):
            value = slot_weights(ref[...], wide) * hidden[index].astype(f32)
            scaled[:, index * count : (index + 1) * count] = value.T.astype(bf16)
        raw[...] = jnp.zeros_like(raw)

    total = jnp.dot(scaled[:, :count], rows[...], preferred_element_type=f32)
    total = total + jnp.dot(scaled[:, count:], rows_other[...], preferred_element_type=f32)
    weight_grad[...] = total.astype(bf16)
    columns = rows.shape[1]
    here = pl.ds(pl.multiple_of(step * columns, 128), columns)
    raw[...] += product_with(rows_other[...], mine[:, here])

    @pl.when(step == pl.num_programs(0) - 1)
    def _():
        store_grads(
            pair_grads.at[1 - span],
            raw[...],
            slot_weights(notes_other[...], wide),
            later[0],
            later[1],
            token_blocks(1 - span, far, near),
        )


def finished(rows, rows_other, mine, hidden, later, grads, tables):
    count, wide = hidden.shape[1:]
    width = rows.shape[1] - extra
    step = width // 2 if width % 256 == 0 else width

    def kept(value):
        return pl.BlockSpec(value.shape, lambda i: (0,) * len(value.shape))

    block = pl.BlockSpec((count, step), lambda i: (0, i))
    note = pl.BlockSpec((count, extra), lambda i: (0, width // extra))
    weight = pl.BlockSpec((wide, step), lambda i: (0, i))
    shapes = (
        jax.ShapeDtypeStruct((2,) + grads.shape, bf16),
        jax.ShapeDtypeStruct((wide, width), bf16),
        *(jax.ShapeDtypeStruct(table.shape, table.dtype) for table in tables),
    )
    inputs = (hidden, later, grads, *tables)
    return pl.pallas_call(
        finish_kernel,
        grid=(width // step,),
        out_shape=shapes,
        in_specs=[block, note, block, note, whole, *(kept(value) for value in inputs)],
        out_specs=(kept(shapes[0]), weight, *(kept(value) for value in shapes[2:])),
        scratch_shapes=[
            pltpu.VMEM((wide, 2 * count), bf16),
            pltpu.VMEM((count, wide), f32),
        ],
        compiler_params=params,
        name="finished",
    )(rows, rows, rows_other, rows_other, mine, *inputs)


def logit_kernel(returned, experts, places, scores, out):
    tokens = scores.shape[1]
    spread = lax.dot_general(
        returned[...],
        experts[...],
        (((0,), (0,)), ((), ())),
        preferred_element_type=f32,
        precision=lax.Precision.HIGHEST,
    )
    route = jnp.sum(spread * places[...], axis=0, keepdims=True)
    for span in range(2):
        first, second = 2 * span, 2 * span + 1
        route0 = route[:, first * tokens : (first + 1) * tokens]
        route1 = route[:, second * tokens : (second + 1) * tokens]
        score0, score1 = scores[first : first + 1], scores[second : second + 1]
        total = score0 + score1
        mean = (route0 * score0 + route1 * score1) / total
        scale = route_scale / total
        out[first : first + 1] = scale * (route0 - mean) * score0 * (1.0 - score0)
        out[second : second + 1] = scale * (route1 - mean) * score1 * (1.0 - score1)


def note_kernel(ids, logits, notes, core, experts, places, scores):
    tokens = ids.shape[1]
    score = jax.nn.sigmoid(logits[...])
    scores[...] = score
    number = ids[...]
    line = jnp.concatenate([number[row : row + 1] for row in range(4)], axis=1)
    lane = lax.broadcasted_iota(jnp.int32, (1, 4 * tokens), 1)
    source = lax.broadcasted_iota(jnp.int32, (32, 4 * tokens), 0)
    span = lane >> 6
    experts[...] = jnp.where(((source >> 2) == line) & ((source & 1) == span), 1.0, 0.0)
    expert = lax.broadcasted_iota(jnp.int32, (8, 4 * tokens), 0)
    marked = jnp.where(expert == line, 1.0, 0.0)
    i = lax.broadcasted_iota(jnp.int32, (4 * tokens, 4 * tokens), 0)
    j = lax.broadcasted_iota(jnp.int32, (4 * tokens, 4 * tokens), 1)
    earlier = jnp.where(((i >> 6) == (j >> 6)) & ((i & 31) < (j & 31)), 1.0, 0.0)
    before = jnp.dot(marked.astype(bf16), earlier.astype(bf16), preferred_element_type=f32)
    place = jnp.sum(before * marked, axis=0, keepdims=True)
    slot = lax.broadcasted_iota(jnp.int32, (128, 4 * tokens), 0).astype(f32)
    places[...] = jnp.where(slot == place, 1.0, 0.0)
    core[...] = jnp.broadcast_to(lax.axis_index("dp"), core.shape)
    first = lax.axis_index("dp") == 0
    pair = jnp.where(first, score[0:2], score[2:4])
    lines = [
        jnp.where(first, number[0:2], number[2:4]).astype(f32),
        route_scale * pair / (pair[0:1] + pair[1:2]),
        jnp.zeros((extra - 4, tokens), f32),
    ]
    table = jnp.concatenate(lines, axis=0)
    table = jnp.concatenate([table, jnp.zeros((extra, extra - tokens), f32)], axis=1)
    notes[...] = table.T[:tokens].astype(bf16)


def slot_notes(ids, logits):
    tokens = ids.shape[1]
    return pl.pallas_call(
        note_kernel,
        out_shape=(
            jax.ShapeDtypeStruct((tokens, extra), bf16),
            jax.ShapeDtypeStruct((tokens, 1), jnp.int32),
            jax.ShapeDtypeStruct((32, 4 * tokens), f32),
            jax.ShapeDtypeStruct((128, 4 * tokens), f32),
            jax.ShapeDtypeStruct((4, tokens), f32),
        ),
        in_specs=[whole] * 2,
        out_specs=(whole,) * 5,
        compiler_params=params,
        name="slot_notes",
    )(ids, logits)


def local(sent_down, sent_up, expert_ids, router_logits, saved_gate_up, down_weight):
    saved = saved_gate_up[:, 0, 0]
    mine = down_weight[0, 0]
    slots = saved.shape[2] // 16
    tokens, top = expert_ids.shape[2:]

    def by_slot(value):
        return jnp.swapaxes(value[:, 0], 1, 2).reshape(2 * top, tokens)

    count = lax.axis_size("pipe")
    from_above = lax.ppermute(
        sent_down[0], ("pipe", "dp"), [(2 * z, 2 * z - 2) for z in range(1, count)]
    )
    from_below = lax.ppermute(
        sent_up[0], ("pipe", "dp"), [(2 * z + 1, 2 * z + 3) for z in range(count - 1)]
    )
    notes, core, experts, places, scores = slot_notes(
        by_slot(expert_ids), by_slot(router_logits)
    )
    notes, held = lax.optimization_barrier((notes, mine))
    other = swapped(held)
    incoming = jnp.where(core == 0, from_above, from_below)
    block = jnp.concatenate([incoming, notes], axis=1)
    block, swapped_saved = lax.optimization_barrier((block, swapped(saved)))

    def sent(pieces):
        return [pieces[0]] + [
            plane_shift(piece, step, False)
            for piece, step in zip(pieces[1:], shifts, strict=True)
        ]

    blocks = [plane_shift(block, step, True) for step in shifts]
    block, other = lax.optimization_barrier((block, other))
    picked = select_rows([block], slots)
    own = sent(picked)
    blocks[2], own[1] = lax.optimization_barrier((blocks[2], own[1]))
    rest = sent(select_rows(blocks, slots))
    own[1], saved, swapped_saved = lax.optimization_barrier((own[1], saved, swapped_saved))
    factors, later, hidden = saved_factors(saved, swapped_saved)
    rest[1], factors, later, hidden = lax.optimization_barrier((rest[1], factors, later, hidden))
    rows = jnp.zeros((16 * slots, block.shape[1]), bf16)
    for index in range(4):
        rows = lax.dynamic_update_slice(rows, own[index], (index * 4 * slots, 0))
        rows = lax.dynamic_update_slice(rows, rest[index], ((index * 4 + 1) * slots, 0))
    grads, dots = raw_grads(rows, mine, other, factors)
    returned = lax.all_to_all(dots, ("expert", "dp"), split_axis=0, concat_axis=0, tiled=True)
    pair_grads, weight_grad, experts, places, scores = finished(
        rows, swapped(rows), mine, hidden, later, grads, (experts, places, scores)
    )
    returned, pair_grads, weight_grad = lax.optimization_barrier(
        (returned, pair_grads, weight_grad)
    )
    logit_grads = pl.pallas_call(
        logit_kernel,
        out_shape=jax.ShapeDtypeStruct((2 * top, tokens), f32),
        in_specs=[whole] * 4,
        out_specs=whole,
        compiler_params=params,
        name="logit_grads",
    )(returned, experts, places, scores)
    return (
        pair_grads[:, None, None],
        weight_grad[None, None],
        jnp.swapaxes(logit_grads.reshape(2, 1, top, tokens), 2, 3),
    )


def solution(mesh):
    placed = (
        P("pipe", "expert", None),
        P("pipe", "expert", None),
        P(None, "pipe", "expert", None),
        P(None, "pipe", "expert", None),
        P(None, "pipe", "expert", None, None, "dp"),
        P("pipe", "expert", "dp", None),
    )
    return jax.shard_map(
        local,
        mesh=mesh,
        in_specs=placed,
        out_specs=(
            P(None, "pipe", "expert", None, None, "dp"),
            P("pipe", "expert", "dp", None),
            P(None, "pipe", "expert", None),
        ),
        check_vma=False,
    )
```

```python
import jax
import jax.numpy as jnp
from jax import lax
from jax.experimental import pallas as pl
from jax.experimental.pallas import tpu as pltpu
from jax.sharding import PartitionSpec as P

route_scale = 2.5
side = 4
gather_steps, exchange_steps = (2, 1, 3), (2, 3, 1)
extra = 128
bf16, f32 = jnp.bfloat16, jnp.float32
params = pltpu.CompilerParams(vmem_limit_bytes=16 * 2**20)
whole = pl.BlockSpec(memory_space=pltpu.VMEM)


def moved(place, step, along_x):
    y, x = place // side, place % side
    return y * side + (x ^ step) if along_x else (y ^ step) * side + x


def plane_shift(value, step, first_along_x):
    pairs = [
        (place * 2 + core, moved(place, step, first_along_x == (core == 0)) * 2 + core)
        for place in range(side * side)
        for core in range(2)
    ]
    return lax.ppermute(value, ("expert", "dp"), pairs)


def swapped(value):
    return lax.ppermute(value, "dp", [(0, 1), (1, 0)])


def position():
    core, spot = lax.axis_index("dp"), lax.axis_index("expert")
    y, x = spot >> 2, spot & 3
    return core, jnp.where(core == 0, x, y), jnp.where(core == 0, y, x)


def token_blocks(core, far):
    places = [far ^ step for step in (0,) + exchange_steps]
    return [
        jnp.where(core == 0, place * 4 + chunk, chunk * 4 + place)
        for place in places
        for chunk in range(side)
    ]


def select_kernel(*refs):
    blocks, outs = refs[:4], refs[4:]
    core, near, far = position()
    held = [near ^ step for step in (0,) + gather_steps]
    targets = [far ^ step for step in (0,) + exchange_steps]
    wanted = [jnp.where(core == 0, t * 2 + (near >> 1), near * 2 + (t >> 1)) for t in targets]
    tokens, width = blocks[0].shape
    width -= extra
    slots = outs[0].shape[0] // 4
    rows, columns = 4 * outs[0].shape[0], 4 * tokens

    def pick(index, values):
        return jnp.where(
            index < 2,
            jnp.where(index == 0, values[0], values[1]),
            jnp.where(index == 2, values[2], values[3]),
        )

    notes = jnp.concatenate([ref[:, width:] for ref in blocks], axis=0).astype(f32).T
    row = lax.broadcasted_iota(jnp.int32, (rows, 1), 0)
    column = lax.broadcasted_iota(jnp.int32, (1, columns), 1)
    expert = pick(row >> 6, wanted).astype(f32)
    same = ((row >> 4) & 3) == pick(column >> 5, held)
    named0 = same & (notes[0:1] == expert)
    named = named0 | (same & (notes[1:2] == expert))
    i = lax.broadcasted_iota(jnp.int32, (columns, columns), 0)
    j = lax.broadcasted_iota(jnp.int32, (columns, columns), 1)
    earlier = jnp.where((i < j) & ((i >> 5) == (j >> 5)), 1.0, 0.0).astype(bf16)
    marked = jnp.where(named, 1.0, 0.0).astype(bf16)
    place = jnp.dot(marked, earlier, preferred_element_type=f32)
    taken = jnp.where(named & (place == (row & 15).astype(f32)), 1.0, 0.0)
    weight = jnp.sum(
        taken * jnp.where(named0, notes[2:3], notes[3:4]), axis=1, keepdims=True
    )
    taken = taken.astype(bf16)

    def put(start, size, value):
        for index, out in enumerate(outs):
            out[:, start : start + size] = value[index * 4 * slots : (index + 1) * 4 * slots]

    put(width, extra, jnp.broadcast_to(weight, (rows, extra)).astype(bf16))
    step = 512 if width % 512 == 0 else width
    for start in range(0, width, step):
        chunk = jnp.concatenate([ref[:, start : start + step] for ref in blocks], axis=0)
        put(start, step, jnp.dot(taken, chunk, preferred_element_type=f32).astype(bf16))


def select_rows(blocks, slots):
    shape = jax.ShapeDtypeStruct((4 * slots, blocks[0].shape[1]), bf16)
    return pl.pallas_call(
        select_kernel,
        out_shape=(shape,) * 4,
        in_specs=[whole] * 4,
        out_specs=(whole,) * 4,
        compiler_params=params,
        name="select_rows",
    )(*blocks)


def factor_kernel(saved, swapped_saved, factors, later, hidden):
    slots = saved.shape[2] // 16
    span, near, far = position()
    order, order_other = token_blocks(span, far), token_blocks(1 - span, near)

    def loaded(ref, which, block):
        at = pl.ds(pl.multiple_of(block * slots, slots), slots)
        gate, up = ref[which, 0, at, :].astype(f32), ref[which, 1, at, :].astype(f32)
        sigma = jax.nn.sigmoid(gate)
        silu = gate * sigma
        return up * sigma * (1.0 + gate * (1.0 - sigma)), silu, (silu * up).astype(bf16)

    for chunk in range(16):
        here = slice(chunk * slots, (chunk + 1) * slots)
        factors[0, here, :] = loaded(swapped_saved, span, order[chunk])[2].astype(f32)
        gate, up, product = loaded(saved, span, order[chunk])
        factors[1, here, :] = product.astype(f32)
        factors[2, here, :] = gate
        factors[3, here, :] = up
        hidden[0, here, :] = product
        later[0, here, :], later[1, here, :], hidden[1, here, :] = loaded(
            saved, 1 - span, order_other[chunk]
        )


def saved_factors(saved, swapped_saved):
    shape = saved.shape[2:]
    return pl.pallas_call(
        factor_kernel,
        out_shape=(
            jax.ShapeDtypeStruct((4,) + shape, f32),
            jax.ShapeDtypeStruct((2,) + shape, f32),
            jax.ShapeDtypeStruct((2,) + shape, bf16),
        ),
        in_specs=[whole] * 2,
        out_specs=(whole,) * 3,
        compiler_params=params,
        name="saved_factors",
    )(saved, swapped_saved)


def slot_weights(notes, wide):
    return jnp.concatenate([notes.astype(f32)] * (wide // extra), axis=1)


def product_with(rows, weight):
    return lax.dot_general(
        rows, weight, (((1,), (1,)), ((), ())), preferred_element_type=f32
    )


def store_grads(out, raw, weights, gate, up, order):
    slots = raw.shape[0] // 16
    grad = weights * raw
    for part, factor in enumerate((gate, up)):
        value = (grad * factor).astype(bf16)
        for chunk in range(16):
            at = pl.ds(pl.multiple_of(order[chunk] * slots, slots), slots)
            out[part, at, :] = value[chunk * slots : (chunk + 1) * slots]


def raw_kernel(rows, mine, other, factors, grads, dots):
    count = rows.shape[0]
    width = rows.shape[1] - extra
    slots = count // 16
    core, _, far = position()
    order = token_blocks(core, far)
    raw_other = product_with(rows[:, :width], other[...])
    raw = product_with(rows[:, :width], mine[...])
    dot = jnp.sum(factors[0] * raw_other + factors[1] * raw, axis=1, keepdims=True)
    lane = lax.broadcasted_iota(jnp.int32, (count, 128), 1)
    row = lax.broadcasted_iota(jnp.int32, (count, 128), 0)
    spread = jnp.where(lane == (row & 15), dot, 0.0)
    for chunk in range(16):
        line = jnp.sum(spread[chunk * slots : (chunk + 1) * slots], axis=0, keepdims=True)
        for target in range(2):
            dots[pl.ds(order[chunk] * 2 + target, 1), :] = line
    weights = slot_weights(rows[:, width:], raw.shape[1])
    store_grads(grads, raw, weights, factors[2], factors[3], order)


def raw_grads(rows, mine, other, factors):
    return pl.pallas_call(
        raw_kernel,
        out_shape=(
            jax.ShapeDtypeStruct((2,) + factors.shape[1:], bf16),
            jax.ShapeDtypeStruct((32, 128), f32),
        ),
        in_specs=[whole] * 4,
        out_specs=(whole,) * 2,
        compiler_params=params,
        name="raw_grads",
    )(rows, mine, other, factors)


def finish_kernel(
    rows, notes, rows_other, notes_other, mine, hidden, later, grads, *refs
):
    tables, (pair_grads, weight_grad), passed = refs[:3], refs[3:5], refs[5:8]
    scaled, raw = refs[8:]
    count, wide = hidden.shape[1:]
    step = pl.program_id(0)
    span, near, _ = position()

    @pl.when(step == 0)
    def _():
        pair_grads[span] = grads[...]
        for table, out in zip(tables, passed, strict=True):
            out[...] = table[...]
        for index, ref in enumerate((notes, notes_other)):
            value = slot_weights(ref[...], wide) * hidden[index].astype(f32)
            scaled[:, index * count : (index + 1) * count] = value.T.astype(bf16)
        raw[...] = jnp.zeros_like(raw)

    total = jnp.dot(scaled[:, :count], rows[...], preferred_element_type=f32)
    total = total + jnp.dot(scaled[:, count:], rows_other[...], preferred_element_type=f32)
    weight_grad[...] = total.astype(bf16)
    columns = rows.shape[1]
    here = pl.ds(pl.multiple_of(step * columns, 128), columns)
    raw[...] += product_with(rows_other[...], mine[:, here])

    @pl.when(step == pl.num_programs(0) - 1)
    def _():
        store_grads(
            pair_grads.at[1 - span],
            raw[...],
            slot_weights(notes_other[...], wide),
            later[0],
            later[1],
            token_blocks(1 - span, near),
        )


def finished(rows, rows_other, mine, hidden, later, grads, tables):
    count, wide = hidden.shape[1:]
    width = rows.shape[1] - extra
    step = width // 2 if width % 256 == 0 else width

    def kept(value):
        return pl.BlockSpec(value.shape, lambda i: (0,) * len(value.shape))

    block = pl.BlockSpec((count, step), lambda i: (0, i))
    note = pl.BlockSpec((count, extra), lambda i: (0, width // extra))
    weight = pl.BlockSpec((wide, step), lambda i: (0, i))
    shapes = (
        jax.ShapeDtypeStruct((2,) + grads.shape, bf16),
        jax.ShapeDtypeStruct((wide, width), bf16),
        *(jax.ShapeDtypeStruct(table.shape, table.dtype) for table in tables),
    )
    inputs = (hidden, later, grads, *tables)
    return pl.pallas_call(
        finish_kernel,
        grid=(width // step,),
        out_shape=shapes,
        in_specs=[block, note, block, note, whole, *(kept(value) for value in inputs)],
        out_specs=(kept(shapes[0]), weight, *(kept(value) for value in shapes[2:])),
        scratch_shapes=[
            pltpu.VMEM((wide, 2 * count), bf16),
            pltpu.VMEM((count, wide), f32),
        ],
        compiler_params=params,
        name="finished",
    )(rows, rows, rows_other, rows_other, mine, *inputs)


def logit_kernel(returned, experts, places, scores, out):
    tokens = scores.shape[1]
    left, parts = returned[...], []
    for _ in range(3):
        parts.append(left.astype(bf16))
        left = left - parts[-1].astype(f32)
    spread = lax.dot_general(
        jnp.concatenate(parts, axis=0),
        experts[...],
        (((0,), (0,)), ((), ())),
        preferred_element_type=f32,
    )
    slots = places.shape[0]
    route = jnp.sum(spread[:slots] * places[...], axis=0, keepdims=True)
    for span in range(2):
        first, second = 2 * span, 2 * span + 1
        route0 = route[:, first * tokens : (first + 1) * tokens]
        route1 = route[:, second * tokens : (second + 1) * tokens]
        score0, score1 = scores[first : first + 1], scores[second : second + 1]
        total = score0 + score1
        mean = (route0 * score0 + route1 * score1) / total
        scale = route_scale / total
        out[first : first + 1] = scale * (route0 - mean) * score0 * (1.0 - score0)
        out[second : second + 1] = scale * (route1 - mean) * score1 * (1.0 - score1)


def note_kernel(ids, logits, notes, core, experts, places, scores):
    tokens = ids.shape[1]
    score = jax.nn.sigmoid(logits[...])
    scores[...] = score
    number = ids[...]
    line = jnp.concatenate([number[row : row + 1] for row in range(4)], axis=1)
    lane = lax.broadcasted_iota(jnp.int32, (1, 4 * tokens), 1)
    source = lax.broadcasted_iota(jnp.int32, (32, 4 * tokens), 0)
    span = lane >> 6
    table = jnp.where(((source >> 2) == line) & ((source & 1) == span), 1.0, 0.0)
    experts[...] = jnp.concatenate([table] * 3, axis=0).astype(bf16)
    expert = lax.broadcasted_iota(jnp.int32, (8, 4 * tokens), 0)
    marked = jnp.where(expert == line, 1.0, 0.0)
    i = lax.broadcasted_iota(jnp.int32, (4 * tokens, 4 * tokens), 0)
    j = lax.broadcasted_iota(jnp.int32, (4 * tokens, 4 * tokens), 1)
    earlier = jnp.where(((i >> 6) == (j >> 6)) & ((i & 31) < (j & 31)), 1.0, 0.0)
    before = jnp.dot(marked.astype(bf16), earlier.astype(bf16), preferred_element_type=f32)
    place = jnp.sum(before * marked, axis=0, keepdims=True)
    slot = lax.broadcasted_iota(jnp.int32, places.shape, 0).astype(f32)
    places[...] = jnp.where(slot == place, 1.0, 0.0)
    core[...] = jnp.broadcast_to(lax.axis_index("dp"), core.shape)
    first = lax.axis_index("dp") == 0
    pair = jnp.where(first, score[0:2], score[2:4])
    lines = [
        jnp.where(first, number[0:2], number[2:4]).astype(f32),
        route_scale * pair / (pair[0:1] + pair[1:2]),
        jnp.zeros((extra - 4, tokens), f32),
    ]
    table = jnp.concatenate(lines, axis=0)
    table = jnp.concatenate([table, jnp.zeros((extra, extra - tokens), f32)], axis=1)
    notes[...] = table.T[:tokens].astype(bf16)


def slot_notes(ids, logits):
    tokens = ids.shape[1]
    return pl.pallas_call(
        note_kernel,
        out_shape=(
            jax.ShapeDtypeStruct((tokens, extra), bf16),
            jax.ShapeDtypeStruct((tokens, 1), jnp.int32),
            jax.ShapeDtypeStruct((96, 4 * tokens), bf16),
            jax.ShapeDtypeStruct((16, 4 * tokens), f32),
            jax.ShapeDtypeStruct((4, tokens), f32),
        ),
        in_specs=[whole] * 2,
        out_specs=(whole,) * 5,
        compiler_params=params,
        name="slot_notes",
    )(ids, logits)


def local(sent_down, sent_up, expert_ids, router_logits, saved_gate_up, down_weight):
    saved = saved_gate_up[:, 0, 0]
    mine = down_weight[0, 0]
    slots = saved.shape[2] // 16
    tokens, top = expert_ids.shape[2:]

    def by_slot(value):
        return jnp.swapaxes(value[:, 0], 1, 2).reshape(2 * top, tokens)

    count = lax.axis_size("pipe")
    from_above = lax.ppermute(
        sent_down[0], ("pipe", "dp"), [(2 * z, 2 * z - 2) for z in range(1, count)]
    )
    from_below = lax.ppermute(
        sent_up[0], ("pipe", "dp"), [(2 * z + 1, 2 * z + 3) for z in range(count - 1)]
    )
    notes, core, experts, places, scores = slot_notes(
        by_slot(expert_ids), by_slot(router_logits)
    )
    notes, held = lax.optimization_barrier((notes, mine))
    other = swapped(held)
    incoming = jnp.where(core == 0, from_above, from_below)
    block = jnp.concatenate([incoming, notes], axis=1)
    block, swapped_saved = lax.optimization_barrier((block, swapped(saved)))

    blocks = [block] + [plane_shift(block, step, True) for step in gather_steps]
    factors, later, hidden = saved_factors(saved, swapped_saved)
    blocks[1], factors, later, hidden = lax.optimization_barrier(
        (blocks[1], factors, later, hidden)
    )
    pieces = select_rows(blocks, slots)
    pieces = [pieces[0]] + [
        plane_shift(piece, step, False)
        for piece, step in zip(pieces[1:], exchange_steps, strict=True)
    ]
    pieces[1], other = lax.optimization_barrier((pieces[1], other))
    rows = jnp.zeros((16 * slots, pieces[0].shape[1]), bf16)
    for index, piece in enumerate(pieces):
        rows = lax.dynamic_update_slice(rows, piece, (index * 4 * slots, 0))
    grads, dots = raw_grads(rows, mine, other, factors)
    returned = lax.all_to_all(dots, ("expert", "dp"), split_axis=0, concat_axis=0, tiled=True)
    pair_grads, weight_grad, experts, places, scores = finished(
        rows, swapped(rows), mine, hidden, later, grads, (experts, places, scores)
    )
    returned, pair_grads, weight_grad = lax.optimization_barrier(
        (returned, pair_grads, weight_grad)
    )
    logit_grads = pl.pallas_call(
        logit_kernel,
        out_shape=jax.ShapeDtypeStruct((2 * top, tokens), f32),
        in_specs=[whole] * 4,
        out_specs=whole,
        compiler_params=params,
        name="logit_grads",
    )(returned, experts, places, scores)
    return (
        pair_grads[:, None, None],
        weight_grad[None, None],
        jnp.swapaxes(logit_grads.reshape(2, 1, top, tokens), 2, 3),
    )


def solution(mesh):
    placed = (
        P("pipe", "expert", None),
        P("pipe", "expert", None),
        P(None, "pipe", "expert", None),
        P(None, "pipe", "expert", None),
        P(None, "pipe", "expert", None, None, "dp"),
        P("pipe", "expert", "dp", None),
    )
    return jax.shard_map(
        local,
        mesh=mesh,
        in_specs=placed,
        out_specs=(
            P(None, "pipe", "expert", None, None, "dp"),
            P("pipe", "expert", "dp", None),
            P(None, "pipe", "expert", None),
        ),
        check_vma=False,
    )
```

```python
import jax
import jax.numpy as jnp
from jax import lax
from jax.experimental import pallas as pl
from jax.experimental.pallas import tpu as pltpu
from jax.sharding import PartitionSpec as P

route_scale = 2.5
side = 4
gather_steps, exchange_steps = (2, 1, 3), (2, 3, 1)
extra = 128
bf16, f32 = jnp.bfloat16, jnp.float32
params = pltpu.CompilerParams(vmem_limit_bytes=16 * 2**20)
whole = pl.BlockSpec(memory_space=pltpu.VMEM)


def moved(place, step, along_x):
    y, x = place // side, place % side
    return y * side + (x ^ step) if along_x else (y ^ step) * side + x


def plane_shift(value, step, first_along_x):
    pairs = [
        (place * 2 + core, moved(place, step, first_along_x == (core == 0)) * 2 + core)
        for place in range(side * side)
        for core in range(2)
    ]
    return lax.ppermute(value, ("expert", "dp"), pairs)


def swapped(value):
    return lax.ppermute(value, "dp", [(0, 1), (1, 0)])


def position():
    core, spot = lax.axis_index("dp"), lax.axis_index("expert")
    y, x = spot >> 2, spot & 3
    return core, jnp.where(core == 0, x, y), jnp.where(core == 0, y, x)


def token_blocks(core, far):
    places = [far ^ step for step in (0,) + exchange_steps]
    return [
        jnp.where(core == 0, place * 4 + chunk, chunk * 4 + place)
        for place in places
        for chunk in range(side)
    ]


def select_kernel(*refs):
    blocks, outs = refs[:4], refs[4:]
    core, near, far = position()
    held = [near ^ step for step in (0,) + gather_steps]
    targets = [far ^ step for step in (0,) + exchange_steps]
    wanted = [jnp.where(core == 0, t * 2 + (near >> 1), near * 2 + (t >> 1)) for t in targets]
    tokens, width = blocks[0].shape
    width -= extra
    slots = outs[0].shape[0] // 4
    rows, columns = 4 * outs[0].shape[0], 4 * tokens

    def pick(index, values):
        return jnp.where(
            index < 2,
            jnp.where(index == 0, values[0], values[1]),
            jnp.where(index == 2, values[2], values[3]),
        )

    notes = jnp.concatenate([ref[:, width:] for ref in blocks], axis=0).astype(f32).T
    row = lax.broadcasted_iota(jnp.int32, (rows, 1), 0)
    column = lax.broadcasted_iota(jnp.int32, (1, columns), 1)
    expert = pick(row >> 6, wanted).astype(f32)
    same = ((row >> 4) & 3) == pick(column >> 5, held)
    named0 = same & (notes[0:1] == expert)
    named = named0 | (same & (notes[1:2] == expert))
    i = lax.broadcasted_iota(jnp.int32, (columns, columns), 0)
    j = lax.broadcasted_iota(jnp.int32, (columns, columns), 1)
    earlier = jnp.where((i < j) & ((i >> 5) == (j >> 5)), 1.0, 0.0).astype(bf16)
    marked = jnp.where(named, 1.0, 0.0).astype(bf16)
    place = jnp.dot(marked, earlier, preferred_element_type=f32)
    taken = jnp.where(named & (place == (row & 15).astype(f32)), 1.0, 0.0)
    weight = jnp.sum(
        taken * jnp.where(named0, notes[2:3], notes[3:4]), axis=1, keepdims=True
    )
    taken = taken.astype(bf16)

    def put(start, size, value):
        for index, out in enumerate(outs):
            out[:, start : start + size] = value[index * 4 * slots : (index + 1) * 4 * slots]

    put(width, extra, jnp.broadcast_to(weight, (rows, extra)).astype(bf16))
    step = 512 if width % 512 == 0 else width
    for start in range(0, width, step):
        chunk = jnp.concatenate([ref[:, start : start + step] for ref in blocks], axis=0)
        put(start, step, jnp.dot(taken, chunk, preferred_element_type=f32).astype(bf16))


def select_rows(blocks, slots):
    shape = jax.ShapeDtypeStruct((4 * slots, blocks[0].shape[1]), bf16)
    return pl.pallas_call(
        select_kernel,
        out_shape=(shape,) * 4,
        in_specs=[whole] * 4,
        out_specs=(whole,) * 4,
        compiler_params=params,
        name="select_rows",
    )(*blocks)


def factor_kernel(saved, swapped_saved, factors, hidden):
    slots = saved.shape[2] // 16
    span, near, far = position()
    order, order_other = token_blocks(span, far), token_blocks(1 - span, near)

    def loaded(ref, which, block):
        at = pl.ds(pl.multiple_of(block * slots, slots), slots)
        gate, up = ref[which, 0, at, :].astype(f32), ref[which, 1, at, :].astype(f32)
        sigma = jax.nn.sigmoid(gate)
        silu = gate * sigma
        return (silu * up).astype(bf16), up * sigma * (1.0 + gate * (1.0 - sigma)), silu

    for chunk in range(16):
        here = slice(chunk * slots, (chunk + 1) * slots)
        for base, ref in ((0, swapped_saved), (3, saved)):
            product, gate, up = loaded(ref, span, order[chunk])
            factors[base, here, :] = product.astype(f32)
            factors[base + 1, here, :] = gate
            factors[base + 2, here, :] = up
        hidden[0, here, :] = product
        hidden[1, here, :] = loaded(saved, 1 - span, order_other[chunk])[0]


def saved_factors(saved, swapped_saved):
    shape = saved.shape[2:]
    return pl.pallas_call(
        factor_kernel,
        out_shape=(
            jax.ShapeDtypeStruct((6,) + shape, f32),
            jax.ShapeDtypeStruct((2,) + shape, bf16),
        ),
        in_specs=[whole] * 2,
        out_specs=(whole,) * 2,
        compiler_params=params,
        name="saved_factors",
    )(saved, swapped_saved)


def slot_weights(notes, wide):
    return jnp.concatenate([notes.astype(f32)] * (wide // extra), axis=1)


def product_with(rows, weight):
    return lax.dot_general(
        rows, weight, (((1,), (1,)), ((), ())), preferred_element_type=f32
    )


def store_grads(out, raw, weights, gate, up, order):
    slots = raw.shape[0] // 16
    grad = weights * raw
    for part, factor in enumerate((gate, up)):
        value = (grad * factor).astype(bf16)
        for chunk in range(16):
            at = pl.ds(pl.multiple_of(order[chunk] * slots, slots), slots)
            out[part, at, :] = value[chunk * slots : (chunk + 1) * slots]


def raw_kernel(rows, mine, other, factors, g_mine, g_other, dots):
    count = rows.shape[0]
    width = rows.shape[1] - extra
    slots = count // 16
    core, _, far = position()
    order = token_blocks(core, far)
    raw_other = product_with(rows[:, :width], other[...])
    raw = product_with(rows[:, :width], mine[...])
    dot = jnp.sum(factors[0] * raw_other + factors[3] * raw, axis=1, keepdims=True)
    lane = lax.broadcasted_iota(jnp.int32, (count, 128), 1)
    row = lax.broadcasted_iota(jnp.int32, (count, 128), 0)
    spread = jnp.where(lane == (row & 15), dot, 0.0)
    for chunk in range(16):
        line = jnp.sum(spread[chunk * slots : (chunk + 1) * slots], axis=0, keepdims=True)
        for target in range(2):
            dots[pl.ds(order[chunk] * 2 + target, 1), :] = line
    weights = slot_weights(rows[:, width:], raw.shape[1])
    store_grads(g_other, raw_other, weights, factors[1], factors[2], order)
    store_grads(g_mine, raw, weights, factors[4], factors[5], order)


def raw_grads(rows, mine, other, factors):
    grads = jax.ShapeDtypeStruct((2,) + factors.shape[1:], bf16)
    return pl.pallas_call(
        raw_kernel,
        out_shape=(grads, grads, jax.ShapeDtypeStruct((32, 128), f32)),
        in_specs=[whole] * 4,
        out_specs=(whole,) * 3,
        compiler_params=params,
        name="raw_grads",
    )(rows, mine, other, factors)


def finish_kernel(
    rows, notes, rows_other, notes_other, hidden, g_mine, g_other, *refs
):
    tables, (pair_grads, weight_grad), passed, scaled = refs[:3], refs[3:5], refs[5:8], refs[8]
    count, wide = hidden.shape[1:]

    @pl.when(pl.program_id(0) == 0)
    def _():
        span = lax.axis_index("dp")
        pair_grads[span] = g_mine[...]
        pair_grads[1 - span] = g_other[...]
        for table, out in zip(tables, passed, strict=True):
            out[...] = table[...]
        for index, ref in enumerate((notes, notes_other)):
            value = slot_weights(ref[...], wide) * hidden[index].astype(f32)
            scaled[:, index * count : (index + 1) * count] = value.T.astype(bf16)

    total = jnp.dot(scaled[:, :count], rows[...], preferred_element_type=f32)
    total = total + jnp.dot(scaled[:, count:], rows_other[...], preferred_element_type=f32)
    weight_grad[...] = total.astype(bf16)


def finished(rows, rows_other, hidden, g_mine, g_other, tables):
    count, wide = hidden.shape[1:]
    width = rows.shape[1] - extra
    step = width // 2 if width % 256 == 0 else width

    def kept(value):
        return pl.BlockSpec(value.shape, lambda i: (0,) * len(value.shape))

    block = pl.BlockSpec((count, step), lambda i: (0, i))
    note = pl.BlockSpec((count, extra), lambda i: (0, width // extra))
    shapes = (
        jax.ShapeDtypeStruct((2,) + g_mine.shape, bf16),
        jax.ShapeDtypeStruct((wide, width), bf16),
        *(jax.ShapeDtypeStruct(table.shape, table.dtype) for table in tables),
    )
    inputs = (hidden, g_mine, g_other, *tables)
    return pl.pallas_call(
        finish_kernel,
        grid=(width // step,),
        out_shape=shapes,
        in_specs=[block, note, block, note, *(kept(value) for value in inputs)],
        out_specs=(
            kept(shapes[0]),
            pl.BlockSpec((wide, step), lambda i: (0, i)),
            *(kept(value) for value in shapes[2:]),
        ),
        scratch_shapes=[pltpu.VMEM((wide, 2 * count), bf16)],
        compiler_params=params,
        name="finished",
    )(rows, rows, rows_other, rows_other, *inputs)


def logit_kernel(returned, experts, places, scores, out):
    tokens = scores.shape[1]
    left, parts = returned[...], []
    for _ in range(3):
        parts.append(left.astype(bf16))
        left = left - parts[-1].astype(f32)
    spread = lax.dot_general(
        jnp.concatenate(parts, axis=0),
        experts[...],
        (((0,), (0,)), ((), ())),
        preferred_element_type=f32,
    )
    slots = places.shape[0]
    route = jnp.sum(spread[:slots] * places[...], axis=0, keepdims=True)
    for span in range(2):
        first, second = 2 * span, 2 * span + 1
        route0 = route[:, first * tokens : (first + 1) * tokens]
        route1 = route[:, second * tokens : (second + 1) * tokens]
        score0, score1 = scores[first : first + 1], scores[second : second + 1]
        total = score0 + score1
        mean = (route0 * score0 + route1 * score1) / total
        scale = route_scale / total
        out[first : first + 1] = scale * (route0 - mean) * score0 * (1.0 - score0)
        out[second : second + 1] = scale * (route1 - mean) * score1 * (1.0 - score1)


def note_kernel(ids, logits, notes, core, experts, places, scores):
    tokens = ids.shape[1]
    score = jax.nn.sigmoid(logits[...])
    scores[...] = score
    number = ids[...]
    line = jnp.concatenate([number[row : row + 1] for row in range(4)], axis=1)
    lane = lax.broadcasted_iota(jnp.int32, (1, 4 * tokens), 1)
    source = lax.broadcasted_iota(jnp.int32, (32, 4 * tokens), 0)
    span = lane >> 6
    table = jnp.where(((source >> 2) == line) & ((source & 1) == span), 1.0, 0.0)
    experts[...] = jnp.concatenate([table] * 3, axis=0).astype(bf16)
    expert = lax.broadcasted_iota(jnp.int32, (8, 4 * tokens), 0)
    marked = jnp.where(expert == line, 1.0, 0.0)
    i = lax.broadcasted_iota(jnp.int32, (4 * tokens, 4 * tokens), 0)
    j = lax.broadcasted_iota(jnp.int32, (4 * tokens, 4 * tokens), 1)
    earlier = jnp.where(((i >> 6) == (j >> 6)) & ((i & 31) < (j & 31)), 1.0, 0.0)
    before = jnp.dot(marked.astype(bf16), earlier.astype(bf16), preferred_element_type=f32)
    place = jnp.sum(before * marked, axis=0, keepdims=True)
    slot = lax.broadcasted_iota(jnp.int32, places.shape, 0).astype(f32)
    places[...] = jnp.where(slot == place, 1.0, 0.0)
    core[...] = jnp.broadcast_to(lax.axis_index("dp"), core.shape)
    first = lax.axis_index("dp") == 0
    pair = jnp.where(first, score[0:2], score[2:4])
    lines = [
        jnp.where(first, number[0:2], number[2:4]).astype(f32),
        route_scale * pair / (pair[0:1] + pair[1:2]),
        jnp.zeros((extra - 4, tokens), f32),
    ]
    table = jnp.concatenate(lines, axis=0)
    table = jnp.concatenate([table, jnp.zeros((extra, extra - tokens), f32)], axis=1)
    notes[...] = table.T[:tokens].astype(bf16)


def slot_notes(ids, logits):
    tokens = ids.shape[1]
    return pl.pallas_call(
        note_kernel,
        out_shape=(
            jax.ShapeDtypeStruct((tokens, extra), bf16),
            jax.ShapeDtypeStruct((tokens, 1), jnp.int32),
            jax.ShapeDtypeStruct((96, 4 * tokens), bf16),
            jax.ShapeDtypeStruct((16, 4 * tokens), f32),
            jax.ShapeDtypeStruct((4, tokens), f32),
        ),
        in_specs=[whole] * 2,
        out_specs=(whole,) * 5,
        compiler_params=params,
        name="slot_notes",
    )(ids, logits)


def local(sent_down, sent_up, expert_ids, router_logits, saved_gate_up, down_weight):
    saved = saved_gate_up[:, 0, 0]
    mine = down_weight[0, 0]
    slots = saved.shape[2] // 16
    tokens, top = expert_ids.shape[2:]

    def by_slot(value):
        return jnp.swapaxes(value[:, 0], 1, 2).reshape(2 * top, tokens)

    count = lax.axis_size("pipe")
    from_above = lax.ppermute(
        sent_down[0], ("pipe", "dp"), [(2 * z, 2 * z - 2) for z in range(1, count)]
    )
    from_below = lax.ppermute(
        sent_up[0], ("pipe", "dp"), [(2 * z + 1, 2 * z + 3) for z in range(count - 1)]
    )
    notes, core, experts, places, scores = slot_notes(
        by_slot(expert_ids), by_slot(router_logits)
    )
    notes, held = lax.optimization_barrier((notes, mine))
    other = swapped(held)
    incoming = jnp.where(core == 0, from_above, from_below)
    block = jnp.concatenate([incoming, notes], axis=1)
    block, swapped_saved = lax.optimization_barrier((block, swapped(saved)))

    blocks = [block] + [plane_shift(block, step, True) for step in gather_steps]
    factors, hidden = saved_factors(saved, swapped_saved)
    blocks[1], factors, hidden = lax.optimization_barrier((blocks[1], factors, hidden))
    pieces = select_rows(blocks, slots)
    pieces = [pieces[0]] + [
        plane_shift(piece, step, False)
        for piece, step in zip(pieces[1:], exchange_steps, strict=True)
    ]
    pieces[1], other = lax.optimization_barrier((pieces[1], other))
    rows = jnp.zeros((16 * slots, pieces[0].shape[1]), bf16)
    for index, piece in enumerate(pieces):
        rows = lax.dynamic_update_slice(rows, piece, (index * 4 * slots, 0))
    g_mine, g_other, dots = raw_grads(rows, mine, other, factors)
    rows, g_other = lax.optimization_barrier((rows, g_other))
    returned = lax.all_to_all(dots, ("expert", "dp"), split_axis=0, concat_axis=0, tiled=True)
    pair_grads, weight_grad, experts, places, scores = finished(
        rows, swapped(rows), hidden, g_mine, swapped(g_other), (experts, places, scores)
    )
    returned, pair_grads, weight_grad = lax.optimization_barrier(
        (returned, pair_grads, weight_grad)
    )
    logit_grads = pl.pallas_call(
        logit_kernel,
        out_shape=jax.ShapeDtypeStruct((2 * top, tokens), f32),
        in_specs=[whole] * 4,
        out_specs=whole,
        compiler_params=params,
        name="logit_grads",
    )(returned, experts, places, scores)
    return (
        pair_grads[:, None, None],
        weight_grad[None, None],
        jnp.swapaxes(logit_grads.reshape(2, 1, top, tokens), 2, 3),
    )


def solution(mesh):
    placed = (
        P("pipe", "expert", None),
        P("pipe", "expert", None),
        P(None, "pipe", "expert", None),
        P(None, "pipe", "expert", None),
        P(None, "pipe", "expert", None, None, "dp"),
        P("pipe", "expert", "dp", None),
    )
    return jax.shard_map(
        local,
        mesh=mesh,
        in_specs=placed,
        out_specs=(
            P(None, "pipe", "expert", None, None, "dp"),
            P("pipe", "expert", "dp", None),
            P(None, "pipe", "expert", None),
        ),
        check_vma=False,
    )
```

```python
import jax
import jax.numpy as jnp
from jax import lax
from jax.experimental import pallas as pl
from jax.experimental.pallas import tpu as pltpu
from jax.sharding import PartitionSpec as P

route_scale = 2.5
side = 4
gather_steps, exchange_steps = (2, 1, 3), (2, 3, 1)
extra = 128
bf16, f32 = jnp.bfloat16, jnp.float32
params = pltpu.CompilerParams(vmem_limit_bytes=16 * 2**20)
whole = pl.BlockSpec(memory_space=pltpu.VMEM)


def moved(place, step, along_x):
    y, x = place // side, place % side
    return y * side + (x ^ step) if along_x else (y ^ step) * side + x


def plane_shift(value, step, first_along_x):
    pairs = [
        (place * 2 + core, moved(place, step, first_along_x == (core == 0)) * 2 + core)
        for place in range(side * side)
        for core in range(2)
    ]
    return lax.ppermute(value, ("expert", "dp"), pairs)


def swapped(value):
    return lax.ppermute(value, "dp", [(0, 1), (1, 0)])


def position():
    core, spot = lax.axis_index("dp"), lax.axis_index("expert")
    y, x = spot >> 2, spot & 3
    return core, jnp.where(core == 0, x, y), jnp.where(core == 0, y, x)


def token_blocks(core, far):
    places = [far ^ step for step in (0,) + exchange_steps]
    return [
        jnp.where(core == 0, place * 4 + chunk, chunk * 4 + place)
        for place in places
        for chunk in range(side)
    ]


def select_kernel(*refs):
    blocks, outs = refs[:4], refs[4:]
    core, near, far = position()
    held = [near ^ step for step in (0,) + gather_steps]
    targets = [far ^ step for step in (0,) + exchange_steps]
    wanted = [jnp.where(core == 0, t * 2 + (near >> 1), near * 2 + (t >> 1)) for t in targets]
    tokens, width = blocks[0].shape
    width -= extra
    slots = outs[0].shape[0] // 4
    rows, columns = 4 * outs[0].shape[0], 4 * tokens

    def pick(index, values):
        return jnp.where(
            index < 2,
            jnp.where(index == 0, values[0], values[1]),
            jnp.where(index == 2, values[2], values[3]),
        )

    notes = jnp.concatenate([ref[:, width:] for ref in blocks], axis=0).astype(f32).T
    row = lax.broadcasted_iota(jnp.int32, (rows, 1), 0)
    column = lax.broadcasted_iota(jnp.int32, (1, columns), 1)
    expert = pick(row >> 6, wanted).astype(f32)
    same = ((row >> 4) & 3) == pick(column >> 5, held)
    named0 = same & (notes[0:1] == expert)
    named = named0 | (same & (notes[1:2] == expert))
    i = lax.broadcasted_iota(jnp.int32, (columns, columns), 0)
    j = lax.broadcasted_iota(jnp.int32, (columns, columns), 1)
    earlier = jnp.where((i < j) & ((i >> 5) == (j >> 5)), 1.0, 0.0).astype(bf16)
    marked = jnp.where(named, 1.0, 0.0).astype(bf16)
    place = jnp.dot(marked, earlier, preferred_element_type=f32)
    taken = jnp.where(named & (place == (row & 15).astype(f32)), 1.0, 0.0)
    weight = jnp.sum(
        taken * jnp.where(named0, notes[2:3], notes[3:4]), axis=1, keepdims=True
    )
    taken = taken.astype(bf16)

    def put(start, size, value):
        for index, out in enumerate(outs):
            out[:, start : start + size] = value[index * 4 * slots : (index + 1) * 4 * slots]

    put(width, extra, jnp.broadcast_to(weight, (rows, extra)).astype(bf16))
    step = 512 if width % 512 == 0 else width
    for start in range(0, width, step):
        chunk = jnp.concatenate([ref[:, start : start + step] for ref in blocks], axis=0)
        put(start, step, jnp.dot(taken, chunk, preferred_element_type=f32).astype(bf16))


def select_rows(blocks, slots):
    shape = jax.ShapeDtypeStruct((4 * slots, blocks[0].shape[1]), bf16)
    return pl.pallas_call(
        select_kernel,
        out_shape=(shape,) * 4,
        in_specs=[whole] * 4,
        out_specs=(whole,) * 4,
        compiler_params=params,
        name="select_rows",
    )(*blocks)


def factor_kernel(saved, swapped_saved, factors, later, hidden):
    slots = saved.shape[2] // 16
    span, near, far = position()
    order, order_other = token_blocks(span, far), token_blocks(1 - span, near)

    def loaded(ref, which, block):
        at = pl.ds(pl.multiple_of(block * slots, slots), slots)
        gate, up = ref[which, 0, at, :].astype(f32), ref[which, 1, at, :].astype(f32)
        sigma = jax.nn.sigmoid(gate)
        silu = gate * sigma
        return up * sigma * (1.0 + gate * (1.0 - sigma)), silu, (silu * up).astype(bf16)

    for chunk in range(16):
        here = slice(chunk * slots, (chunk + 1) * slots)
        factors[0, here, :] = loaded(swapped_saved, span, order[chunk])[2].astype(f32)
        gate, up, product = loaded(saved, span, order[chunk])
        factors[1, here, :] = product.astype(f32)
        factors[2, here, :] = gate
        factors[3, here, :] = up
        hidden[0, here, :] = product
        later[0, here, :], later[1, here, :], hidden[1, here, :] = loaded(
            saved, 1 - span, order_other[chunk]
        )


def saved_factors(saved, swapped_saved):
    shape = saved.shape[2:]
    return pl.pallas_call(
        factor_kernel,
        out_shape=(
            jax.ShapeDtypeStruct((4,) + shape, f32),
            jax.ShapeDtypeStruct((2,) + shape, f32),
            jax.ShapeDtypeStruct((2,) + shape, bf16),
        ),
        in_specs=[whole] * 2,
        out_specs=(whole,) * 3,
        compiler_params=params,
        name="saved_factors",
    )(saved, swapped_saved)


def slot_weights(notes, wide):
    return jnp.concatenate([notes.astype(f32)] * (wide // extra), axis=1)


def product_with(rows, weight):
    return lax.dot_general(
        rows, weight, (((1,), (1,)), ((), ())), preferred_element_type=f32
    )


def store_grads(out, raw, weights, gate, up, order):
    slots = raw.shape[0] // 16
    grad = weights * raw
    for part, factor in enumerate((gate, up)):
        value = (grad * factor).astype(bf16)
        for chunk in range(16):
            at = pl.ds(pl.multiple_of(order[chunk] * slots, slots), slots)
            out[part, at, :] = value[chunk * slots : (chunk + 1) * slots]


def raw_kernel(rows, mine, other, factors, grads, dots, table, left):
    count = rows.shape[0]
    width = rows.shape[1] - extra
    slots = count // 16
    core, _, far = position()
    order = token_blocks(core, far)
    raw_other = product_with(rows[:, :width], other[...])
    raw = product_with(rows[:, :width], mine[...])
    dot = jnp.sum(factors[0] * raw_other + factors[1] * raw, axis=1, keepdims=True)
    lane = lax.broadcasted_iota(jnp.int32, (count, 128), 1)
    row = lax.broadcasted_iota(jnp.int32, (count, 128), 0)
    spread = jnp.where(lane == (row & 15), dot, 0.0)
    for chunk in range(16):
        line = jnp.sum(spread[chunk * slots : (chunk + 1) * slots], axis=0, keepdims=True)
        for target in range(2):
            table[pl.ds(order[chunk] * 2 + target, 1), :] = line
    leaving = pltpu.make_async_copy(table, dots, left)
    leaving.start()
    weights = slot_weights(rows[:, width:], raw.shape[1])
    store_grads(grads, raw, weights, factors[2], factors[3], order)
    leaving.wait()


def raw_grads(rows, mine, other, factors):
    return pl.pallas_call(
        raw_kernel,
        out_shape=(
            jax.ShapeDtypeStruct((2,) + factors.shape[1:], bf16),
            jax.ShapeDtypeStruct((32, 128), f32),
        ),
        in_specs=[whole] * 4,
        out_specs=(whole, pl.BlockSpec(memory_space=pl.ANY)),
        scratch_shapes=[pltpu.VMEM((32, 128), f32), pltpu.SemaphoreType.DMA],
        compiler_params=params,
        name="raw_grads",
    )(rows, mine, other, factors)


def finish_kernel(
    rows, notes, rows_other, notes_other, mine, hidden, later, grads, *refs
):
    tables, (pair_grads, weight_grad), passed = refs[:3], refs[3:5], refs[5:8]
    scaled, raw = refs[8:]
    count, wide = hidden.shape[1:]
    step = pl.program_id(0)
    span, near, _ = position()

    @pl.when(step == 0)
    def _():
        pair_grads[span] = grads[...]
        for table, out in zip(tables, passed, strict=True):
            out[...] = table[...]
        for index, ref in enumerate((notes, notes_other)):
            value = slot_weights(ref[...], wide) * hidden[index].astype(f32)
            scaled[:, index * count : (index + 1) * count] = value.T.astype(bf16)
        raw[...] = jnp.zeros_like(raw)

    total = jnp.dot(scaled[:, :count], rows[...], preferred_element_type=f32)
    total = total + jnp.dot(scaled[:, count:], rows_other[...], preferred_element_type=f32)
    weight_grad[...] = total.astype(bf16)
    columns = rows.shape[1]
    here = pl.ds(pl.multiple_of(step * columns, 128), columns)
    raw[...] += product_with(rows_other[...], mine[:, here])

    @pl.when(step == pl.num_programs(0) - 1)
    def _():
        store_grads(
            pair_grads.at[1 - span],
            raw[...],
            slot_weights(notes_other[...], wide),
            later[0],
            later[1],
            token_blocks(1 - span, near),
        )


def finished(rows, rows_other, mine, hidden, later, grads, tables):
    count, wide = hidden.shape[1:]
    width = rows.shape[1] - extra
    step = width // 2 if width % 256 == 0 else width

    def kept(value):
        return pl.BlockSpec(value.shape, lambda i: (0,) * len(value.shape))

    block = pl.BlockSpec((count, step), lambda i: (0, i))
    note = pl.BlockSpec((count, extra), lambda i: (0, width // extra))
    weight = pl.BlockSpec((wide, step), lambda i: (0, i))
    shapes = (
        jax.ShapeDtypeStruct((2,) + grads.shape, bf16),
        jax.ShapeDtypeStruct((wide, width), bf16),
        *(jax.ShapeDtypeStruct(table.shape, table.dtype) for table in tables),
    )
    inputs = (hidden, later, grads, *tables)
    return pl.pallas_call(
        finish_kernel,
        grid=(width // step,),
        out_shape=shapes,
        in_specs=[block, note, block, note, whole, *(kept(value) for value in inputs)],
        out_specs=(kept(shapes[0]), weight, *(kept(value) for value in shapes[2:])),
        scratch_shapes=[
            pltpu.VMEM((wide, 2 * count), bf16),
            pltpu.VMEM((count, wide), f32),
        ],
        compiler_params=params,
        name="finished",
    )(rows, rows, rows_other, rows_other, mine, *inputs)


def logit_kernel(returned, experts, places, scores, out):
    tokens = scores.shape[1]
    left, parts = returned[...], []
    for _ in range(3):
        parts.append(left.astype(bf16))
        left = left - parts[-1].astype(f32)
    spread = lax.dot_general(
        jnp.concatenate(parts, axis=0),
        experts[...],
        (((0,), (0,)), ((), ())),
        preferred_element_type=f32,
    )
    slots = places.shape[0]
    route = jnp.sum(spread[:slots] * places[...], axis=0, keepdims=True)
    for span in range(2):
        first, second = 2 * span, 2 * span + 1
        route0 = route[:, first * tokens : (first + 1) * tokens]
        route1 = route[:, second * tokens : (second + 1) * tokens]
        score0, score1 = scores[first : first + 1], scores[second : second + 1]
        total = score0 + score1
        mean = (route0 * score0 + route1 * score1) / total
        scale = route_scale / total
        out[first : first + 1] = scale * (route0 - mean) * score0 * (1.0 - score0)
        out[second : second + 1] = scale * (route1 - mean) * score1 * (1.0 - score1)


def note_kernel(ids, logits, notes, core, experts, places, scores):
    tokens = ids.shape[1]
    score = jax.nn.sigmoid(logits[...])
    scores[...] = score
    number = ids[...]
    line = jnp.concatenate([number[row : row + 1] for row in range(4)], axis=1)
    lane = lax.broadcasted_iota(jnp.int32, (1, 4 * tokens), 1)
    source = lax.broadcasted_iota(jnp.int32, (32, 4 * tokens), 0)
    span = lane >> 6
    table = jnp.where(((source >> 2) == line) & ((source & 1) == span), 1.0, 0.0)
    experts[...] = jnp.concatenate([table] * 3, axis=0).astype(bf16)
    expert = lax.broadcasted_iota(jnp.int32, (8, 4 * tokens), 0)
    marked = jnp.where(expert == line, 1.0, 0.0)
    i = lax.broadcasted_iota(jnp.int32, (4 * tokens, 4 * tokens), 0)
    j = lax.broadcasted_iota(jnp.int32, (4 * tokens, 4 * tokens), 1)
    earlier = jnp.where(((i >> 6) == (j >> 6)) & ((i & 31) < (j & 31)), 1.0, 0.0)
    before = jnp.dot(marked.astype(bf16), earlier.astype(bf16), preferred_element_type=f32)
    place = jnp.sum(before * marked, axis=0, keepdims=True)
    slot = lax.broadcasted_iota(jnp.int32, places.shape, 0).astype(f32)
    places[...] = jnp.where(slot == place, 1.0, 0.0)
    core[...] = jnp.broadcast_to(lax.axis_index("dp"), core.shape)
    first = lax.axis_index("dp") == 0
    pair = jnp.where(first, score[0:2], score[2:4])
    lines = [
        jnp.where(first, number[0:2], number[2:4]).astype(f32),
        route_scale * pair / (pair[0:1] + pair[1:2]),
        jnp.zeros((extra - 4, tokens), f32),
    ]
    table = jnp.concatenate(lines, axis=0)
    table = jnp.concatenate([table, jnp.zeros((extra, extra - tokens), f32)], axis=1)
    notes[...] = table.T[:tokens].astype(bf16)


def slot_notes(ids, logits):
    tokens = ids.shape[1]
    return pl.pallas_call(
        note_kernel,
        out_shape=(
            jax.ShapeDtypeStruct((tokens, extra), bf16),
            jax.ShapeDtypeStruct((tokens, 1), jnp.int32),
            jax.ShapeDtypeStruct((96, 4 * tokens), bf16),
            jax.ShapeDtypeStruct((16, 4 * tokens), f32),
            jax.ShapeDtypeStruct((4, tokens), f32),
        ),
        in_specs=[whole] * 2,
        out_specs=(whole,) * 5,
        compiler_params=params,
        name="slot_notes",
    )(ids, logits)


def local(sent_down, sent_up, expert_ids, router_logits, saved_gate_up, down_weight):
    saved = saved_gate_up[:, 0, 0]
    mine = down_weight[0, 0]
    slots = saved.shape[2] // 16
    tokens, top = expert_ids.shape[2:]

    def by_slot(value):
        return jnp.swapaxes(value[:, 0], 1, 2).reshape(2 * top, tokens)

    count = lax.axis_size("pipe")
    from_above = lax.ppermute(
        sent_down[0], ("pipe", "dp"), [(2 * z, 2 * z - 2) for z in range(1, count)]
    )
    from_below = lax.ppermute(
        sent_up[0], ("pipe", "dp"), [(2 * z + 1, 2 * z + 3) for z in range(count - 1)]
    )
    notes, core, experts, places, scores = slot_notes(
        by_slot(expert_ids), by_slot(router_logits)
    )
    notes, held = lax.optimization_barrier((notes, mine))
    other = swapped(held)
    incoming = jnp.where(core == 0, from_above, from_below)
    block = jnp.concatenate([incoming, notes], axis=1)
    block, swapped_saved = lax.optimization_barrier((block, swapped(saved)))

    blocks = [block] + [plane_shift(block, step, True) for step in gather_steps]
    factors, later, hidden = saved_factors(saved, swapped_saved)
    blocks[1], factors, later, hidden = lax.optimization_barrier(
        (blocks[1], factors, later, hidden)
    )
    pieces = select_rows(blocks, slots)
    pieces = [pieces[0]] + [
        plane_shift(piece, step, False)
        for piece, step in zip(pieces[1:], exchange_steps, strict=True)
    ]
    pieces[1], other = lax.optimization_barrier((pieces[1], other))
    rows = jnp.zeros((16 * slots, pieces[0].shape[1]), bf16)
    for index, piece in enumerate(pieces):
        rows = lax.dynamic_update_slice(rows, piece, (index * 4 * slots, 0))
    grads, dots = raw_grads(rows, mine, other, factors)
    returned = lax.all_to_all(dots, ("expert", "dp"), split_axis=0, concat_axis=0, tiled=True)
    pair_grads, weight_grad, experts, places, scores = finished(
        rows, swapped(rows), mine, hidden, later, grads, (experts, places, scores)
    )
    returned, pair_grads, weight_grad = lax.optimization_barrier(
        (returned, pair_grads, weight_grad)
    )
    logit_grads = pl.pallas_call(
        logit_kernel,
        out_shape=jax.ShapeDtypeStruct((2 * top, tokens), f32),
        in_specs=[whole] * 4,
        out_specs=whole,
        compiler_params=params,
        name="logit_grads",
    )(returned, experts, places, scores)
    return (
        pair_grads[:, None, None],
        weight_grad[None, None],
        jnp.swapaxes(logit_grads.reshape(2, 1, top, tokens), 2, 3),
    )


def solution(mesh):
    placed = (
        P("pipe", "expert", None),
        P("pipe", "expert", None),
        P(None, "pipe", "expert", None),
        P(None, "pipe", "expert", None),
        P(None, "pipe", "expert", None, None, "dp"),
        P("pipe", "expert", "dp", None),
    )
    return jax.shard_map(
        local,
        mesh=mesh,
        in_specs=placed,
        out_specs=(
            P(None, "pipe", "expert", None, None, "dp"),
            P("pipe", "expert", "dp", None),
            P(None, "pipe", "expert", None),
        ),
        check_vma=False,
    )
```

```python
import jax
import jax.numpy as jnp
from jax import lax
from jax.experimental import pallas as pl
from jax.experimental.pallas import tpu as pltpu
from jax.sharding import PartitionSpec as P

route_scale = 2.5
side = 4
gather_steps, exchange_steps = (2, 1, 3), (2, 3, 1)
extra = 128
bf16, f32 = jnp.bfloat16, jnp.float32
params = pltpu.CompilerParams(vmem_limit_bytes=16 * 2**20)
whole = pl.BlockSpec(memory_space=pltpu.VMEM)


def moved(place, step, along_x):
    y, x = place // side, place % side
    return y * side + (x ^ step) if along_x else (y ^ step) * side + x


def plane_shift(value, step, first_along_x):
    pairs = [
        (place * 2 + core, moved(place, step, first_along_x == (core == 0)) * 2 + core)
        for place in range(side * side)
        for core in range(2)
    ]
    return lax.ppermute(value, ("expert", "dp"), pairs)


def swapped(value):
    return lax.ppermute(value, "dp", [(0, 1), (1, 0)])


def position():
    core, spot = lax.axis_index("dp"), lax.axis_index("expert")
    y, x = spot >> 2, spot & 3
    return core, jnp.where(core == 0, x, y), jnp.where(core == 0, y, x)


def token_blocks(core, far):
    places = [far ^ step for step in (0,) + exchange_steps]
    return [
        jnp.where(core == 0, place * 4 + chunk, chunk * 4 + place)
        for place in places
        for chunk in range(side)
    ]


def select_kernel(*refs):
    blocks, outs = refs[:4], refs[4:]
    core, near, far = position()
    held = [near ^ step for step in (0,) + gather_steps]
    targets = [far ^ step for step in (0,) + exchange_steps]
    wanted = [jnp.where(core == 0, t * 2 + (near >> 1), near * 2 + (t >> 1)) for t in targets]
    tokens, width = blocks[0].shape
    width -= extra
    slots = outs[0].shape[0] // 4
    rows, columns = 4 * outs[0].shape[0], 4 * tokens

    def pick(index, values):
        return jnp.where(
            index < 2,
            jnp.where(index == 0, values[0], values[1]),
            jnp.where(index == 2, values[2], values[3]),
        )

    notes = jnp.concatenate([ref[:, width:] for ref in blocks], axis=0).astype(f32).T
    row = lax.broadcasted_iota(jnp.int32, (rows, 1), 0)
    column = lax.broadcasted_iota(jnp.int32, (1, columns), 1)
    expert = pick(row >> 6, wanted).astype(f32)
    same = ((row >> 4) & 3) == pick(column >> 5, held)
    named0 = same & (notes[0:1] == expert)
    named = named0 | (same & (notes[1:2] == expert))
    i = lax.broadcasted_iota(jnp.int32, (columns, columns), 0)
    j = lax.broadcasted_iota(jnp.int32, (columns, columns), 1)
    earlier = jnp.where((i < j) & ((i >> 5) == (j >> 5)), 1.0, 0.0).astype(bf16)
    marked = jnp.where(named, 1.0, 0.0).astype(bf16)
    place = jnp.dot(marked, earlier, preferred_element_type=f32)
    taken = jnp.where(named & (place == (row & 15).astype(f32)), 1.0, 0.0)
    weight = jnp.sum(
        taken * jnp.where(named0, notes[2:3], notes[3:4]), axis=1, keepdims=True
    )
    taken = taken.astype(bf16)

    def put(start, size, value):
        for index, out in enumerate(outs):
            out[:, start : start + size] = value[index * 4 * slots : (index + 1) * 4 * slots]

    put(width, extra, jnp.broadcast_to(weight, (rows, extra)).astype(bf16))
    step = 512 if width % 512 == 0 else width
    for start in range(0, width, step):
        chunk = jnp.concatenate([ref[:, start : start + step] for ref in blocks], axis=0)
        put(start, step, jnp.dot(taken, chunk, preferred_element_type=f32).astype(bf16))


def select_rows(blocks, slots):
    shape = jax.ShapeDtypeStruct((4 * slots, blocks[0].shape[1]), bf16)
    return pl.pallas_call(
        select_kernel,
        out_shape=(shape,) * 4,
        in_specs=[whole] * 4,
        out_specs=(whole,) * 4,
        compiler_params=params,
        name="select_rows",
    )(*blocks)


def factor_kernel(saved, swapped_saved, factors, later, hidden):
    slots = saved.shape[2] // 16
    span, near, far = position()
    order, order_other = token_blocks(span, far), token_blocks(1 - span, near)

    def loaded(ref, which, block):
        at = pl.ds(pl.multiple_of(block * slots, slots), slots)
        gate, up = ref[which, 0, at, :].astype(f32), ref[which, 1, at, :].astype(f32)
        sigma = jax.nn.sigmoid(gate)
        silu = gate * sigma
        return up * sigma * (1.0 + gate * (1.0 - sigma)), silu, (silu * up).astype(bf16)

    for chunk in range(16):
        here = slice(chunk * slots, (chunk + 1) * slots)
        factors[0, here, :] = loaded(swapped_saved, span, order[chunk])[2].astype(f32)
        gate, up, product = loaded(saved, span, order[chunk])
        factors[1, here, :] = product.astype(f32)
        factors[2, here, :] = gate
        factors[3, here, :] = up
        hidden[0, here, :] = product
        later[0, here, :], later[1, here, :], hidden[1, here, :] = loaded(
            saved, 1 - span, order_other[chunk]
        )


def saved_factors(saved, swapped_saved):
    shape = saved.shape[2:]
    return pl.pallas_call(
        factor_kernel,
        out_shape=(
            jax.ShapeDtypeStruct((4,) + shape, f32),
            jax.ShapeDtypeStruct((2,) + shape, f32),
            jax.ShapeDtypeStruct((2,) + shape, bf16),
        ),
        in_specs=[whole] * 2,
        out_specs=(whole,) * 3,
        compiler_params=params,
        name="saved_factors",
    )(saved, swapped_saved)


def slot_weights(notes, wide):
    return jnp.concatenate([notes.astype(f32)] * (wide // extra), axis=1)


def product_with(rows, weight):
    return lax.dot_general(
        rows, weight, (((1,), (1,)), ((), ())), preferred_element_type=f32
    )


def store_grads(out, raw, weights, gate, up, order):
    slots = raw.shape[0] // 16
    grad = weights * raw
    for part, factor in enumerate((gate, up)):
        value = (grad * factor).astype(bf16)
        for chunk in range(16):
            at = pl.ds(pl.multiple_of(order[chunk] * slots, slots), slots)
            out[part, at, :] = value[chunk * slots : (chunk + 1) * slots]


def raw_kernel(rows, mine, other, factors, grads, dots):
    count = rows.shape[0]
    width = rows.shape[1] - extra
    slots = count // 16
    core, _, far = position()
    order = token_blocks(core, far)
    raw_other = product_with(rows[:, :width], other[...])
    raw = product_with(rows[:, :width], mine[...])
    dot = jnp.sum(factors[0] * raw_other + factors[1] * raw, axis=1, keepdims=True)
    lane = lax.broadcasted_iota(jnp.int32, (count, 128), 1)
    row = lax.broadcasted_iota(jnp.int32, (count, 128), 0)
    spread = jnp.where(lane == (row & 15), dot, 0.0)
    for chunk in range(16):
        line = jnp.sum(spread[chunk * slots : (chunk + 1) * slots], axis=0, keepdims=True)
        for target in range(2):
            dots[pl.ds(order[chunk] * 2 + target, 1), :] = line
    weights = slot_weights(rows[:, width:], raw.shape[1])
    store_grads(grads, raw, weights, factors[2], factors[3], order)


def raw_grads(rows, mine, other, factors):
    return pl.pallas_call(
        raw_kernel,
        out_shape=(
            jax.ShapeDtypeStruct((2,) + factors.shape[1:], bf16),
            jax.ShapeDtypeStruct((32, 128), f32),
        ),
        in_specs=[whole] * 4,
        out_specs=(whole,) * 2,
        compiler_params=params,
        name="raw_grads",
    )(rows, mine, other, factors)


def finish_kernel(
    rows, notes, rows_other, notes_other, mine, hidden, later, grads, *refs
):
    tables, (pair_grads, weight_grad), passed = refs[:3], refs[3:5], refs[5:8]
    scaled, raw = refs[8:]
    count, wide = hidden.shape[1:]
    step = pl.program_id(0)
    span, near, _ = position()

    @pl.when(step == 0)
    def _():
        pair_grads[span] = grads[...]
        for table, out in zip(tables, passed, strict=True):
            out[...] = table[...]
        for index, ref in enumerate((notes, notes_other)):
            value = slot_weights(ref[...], wide) * hidden[index].astype(f32)
            scaled[:, index * count : (index + 1) * count] = value.T.astype(bf16)
        raw[...] = jnp.zeros_like(raw)

    total = jnp.dot(scaled[:, :count], rows[...], preferred_element_type=f32)
    total = total + jnp.dot(scaled[:, count:], rows_other[...], preferred_element_type=f32)
    weight_grad[...] = total.astype(bf16)
    columns = rows.shape[1]
    here = pl.ds(pl.multiple_of(step * columns, 128), columns)
    raw[...] += product_with(rows_other[...], mine[:, here])

    @pl.when(step == pl.num_programs(0) - 1)
    def _():
        store_grads(
            pair_grads.at[1 - span],
            raw[...],
            slot_weights(notes_other[...], wide),
            later[0],
            later[1],
            token_blocks(1 - span, near),
        )


def finished(rows, rows_other, mine, hidden, later, grads, tables):
    count, wide = hidden.shape[1:]
    width = rows.shape[1] - extra
    step = width // 2 if width % 256 == 0 else width

    def kept(value):
        return pl.BlockSpec(value.shape, lambda i: (0,) * len(value.shape))

    block = pl.BlockSpec((count, step), lambda i: (0, i))
    note = pl.BlockSpec((count, extra), lambda i: (0, width // extra))
    weight = pl.BlockSpec((wide, step), lambda i: (0, i))
    shapes = (
        jax.ShapeDtypeStruct((2,) + grads.shape, bf16),
        jax.ShapeDtypeStruct((wide, width), bf16),
        *(jax.ShapeDtypeStruct(table.shape, table.dtype) for table in tables),
    )
    inputs = (hidden, later, grads, *tables)
    return pl.pallas_call(
        finish_kernel,
        grid=(width // step,),
        out_shape=shapes,
        in_specs=[block, note, block, note, whole, *(kept(value) for value in inputs)],
        out_specs=(kept(shapes[0]), weight, *(kept(value) for value in shapes[2:])),
        scratch_shapes=[
            pltpu.VMEM((wide, 2 * count), bf16),
            pltpu.VMEM((count, wide), f32),
        ],
        compiler_params=params,
        name="finished",
    )(rows, rows, rows_other, rows_other, mine, *inputs)


def logit_kernel(returned, experts, places, scores, out):
    tokens = scores.shape[1]
    left, parts = returned[...], []
    for _ in range(3):
        parts.append(left.astype(bf16))
        left = left - parts[-1].astype(f32)
    spread = lax.dot_general(
        jnp.concatenate(parts, axis=0),
        experts[...],
        (((0,), (0,)), ((), ())),
        preferred_element_type=f32,
    )
    slots = places.shape[0]
    route = jnp.sum(spread[:slots] * places[...], axis=0, keepdims=True)
    for span in range(2):
        first, second = 2 * span, 2 * span + 1
        route0 = route[:, first * tokens : (first + 1) * tokens]
        route1 = route[:, second * tokens : (second + 1) * tokens]
        score0, score1 = scores[first : first + 1], scores[second : second + 1]
        total = score0 + score1
        mean = (route0 * score0 + route1 * score1) / total
        scale = route_scale / total
        out[first : first + 1] = scale * (route0 - mean) * score0 * (1.0 - score0)
        out[second : second + 1] = scale * (route1 - mean) * score1 * (1.0 - score1)


def note_kernel(ids, logits, notes, core, experts, places, scores):
    tokens = ids.shape[1]
    score = jax.nn.sigmoid(logits[...])
    scores[...] = score
    number = ids[...]
    line = jnp.concatenate([number[row : row + 1] for row in range(4)], axis=1)
    lane = lax.broadcasted_iota(jnp.int32, (1, 4 * tokens), 1)
    source = lax.broadcasted_iota(jnp.int32, (32, 4 * tokens), 0)
    span = lane >> 6
    table = jnp.where(((source >> 2) == line) & ((source & 1) == span), 1.0, 0.0)
    experts[...] = jnp.concatenate([table] * 3, axis=0).astype(bf16)
    expert = lax.broadcasted_iota(jnp.int32, (8, 4 * tokens), 0)
    marked = jnp.where(expert == line, 1.0, 0.0)
    i = lax.broadcasted_iota(jnp.int32, (4 * tokens, 4 * tokens), 0)
    j = lax.broadcasted_iota(jnp.int32, (4 * tokens, 4 * tokens), 1)
    earlier = jnp.where(((i >> 6) == (j >> 6)) & ((i & 31) < (j & 31)), 1.0, 0.0)
    before = jnp.dot(marked.astype(bf16), earlier.astype(bf16), preferred_element_type=f32)
    place = jnp.sum(before * marked, axis=0, keepdims=True)
    slot = lax.broadcasted_iota(jnp.int32, places.shape, 0).astype(f32)
    places[...] = jnp.where(slot == place, 1.0, 0.0)
    core[...] = jnp.broadcast_to(lax.axis_index("dp"), core.shape)
    first = lax.axis_index("dp") == 0
    pair = jnp.where(first, score[0:2], score[2:4])
    lines = [
        jnp.where(first, number[0:2], number[2:4]).astype(f32),
        route_scale * pair / (pair[0:1] + pair[1:2]),
        jnp.zeros((extra - 4, tokens), f32),
    ]
    table = jnp.concatenate(lines, axis=0)
    table = jnp.concatenate([table, jnp.zeros((extra, extra - tokens), f32)], axis=1)
    notes[...] = table.T[:tokens].astype(bf16)


def slot_notes(ids, logits):
    tokens = ids.shape[1]
    return pl.pallas_call(
        note_kernel,
        out_shape=(
            jax.ShapeDtypeStruct((tokens, extra), bf16),
            jax.ShapeDtypeStruct((tokens, 1), jnp.int32),
            jax.ShapeDtypeStruct((96, 4 * tokens), bf16),
            jax.ShapeDtypeStruct((16, 4 * tokens), f32),
            jax.ShapeDtypeStruct((4, tokens), f32),
        ),
        in_specs=[whole] * 2,
        out_specs=(whole,) * 5,
        compiler_params=params,
        name="slot_notes",
    )(ids, logits)


def local(sent_down, sent_up, expert_ids, router_logits, saved_gate_up, down_weight):
    saved = saved_gate_up[:, 0, 0]
    mine = down_weight[0, 0]
    slots = saved.shape[2] // 16
    tokens, top = expert_ids.shape[2:]

    def by_slot(value):
        return jnp.swapaxes(value[:, 0], 1, 2).reshape(2 * top, tokens)

    count = lax.axis_size("pipe")
    from_above = lax.ppermute(
        sent_down[0], ("pipe", "dp"), [(2 * z, 2 * z - 2) for z in range(1, count)]
    )
    from_below = lax.ppermute(
        sent_up[0], ("pipe", "dp"), [(2 * z + 1, 2 * z + 3) for z in range(count - 1)]
    )
    notes, core, experts, places, scores = slot_notes(
        by_slot(expert_ids), by_slot(router_logits)
    )
    notes, held = lax.optimization_barrier((notes, mine))
    other = swapped(held)
    incoming = jnp.where(core == 0, from_above, from_below)
    block = jnp.concatenate([incoming, notes], axis=1)
    block, swapped_saved = lax.optimization_barrier((block, swapped(saved)))

    blocks = [block] + [plane_shift(block, step, True) for step in gather_steps]
    factors, later, hidden = saved_factors(saved, swapped_saved)
    blocks[1], factors, later, hidden = lax.optimization_barrier(
        (blocks[1], factors, later, hidden)
    )
    pieces = select_rows(blocks, slots)
    pieces = [pieces[0]] + [
        plane_shift(piece, step, False)
        for piece, step in zip(pieces[1:], exchange_steps, strict=True)
    ]
    pieces[1], other = lax.optimization_barrier((pieces[1], other))
    rows = jnp.zeros((16 * slots, pieces[0].shape[1]), bf16)
    for index, piece in enumerate(pieces):
        rows = lax.dynamic_update_slice(rows, piece, (index * 4 * slots, 0))
    grads, dots = raw_grads(rows, mine, other, factors)
    rows, grads = lax.optimization_barrier((rows, grads))
    returned = lax.all_to_all(dots, ("expert", "dp"), split_axis=0, concat_axis=0, tiled=True)
    pair_grads, weight_grad, experts, places, scores = finished(
        rows, swapped(rows), mine, hidden, later, grads, (experts, places, scores)
    )
    returned, pair_grads, weight_grad = lax.optimization_barrier(
        (returned, pair_grads, weight_grad)
    )
    logit_grads = pl.pallas_call(
        logit_kernel,
        out_shape=jax.ShapeDtypeStruct((2 * top, tokens), f32),
        in_specs=[whole] * 4,
        out_specs=whole,
        compiler_params=params,
        name="logit_grads",
    )(returned, experts, places, scores)
    return (
        pair_grads[:, None, None],
        weight_grad[None, None],
        jnp.swapaxes(logit_grads.reshape(2, 1, top, tokens), 2, 3),
    )


def solution(mesh):
    placed = (
        P("pipe", "expert", None),
        P("pipe", "expert", None),
        P(None, "pipe", "expert", None),
        P(None, "pipe", "expert", None),
        P(None, "pipe", "expert", None, None, "dp"),
        P("pipe", "expert", "dp", None),
    )
    return jax.shard_map(
        local,
        mesh=mesh,
        in_specs=placed,
        out_specs=(
            P(None, "pipe", "expert", None, None, "dp"),
            P("pipe", "expert", "dp", None),
            P(None, "pipe", "expert", None),
        ),
        check_vma=False,
    )
```

```python
import jax
import jax.numpy as jnp
from jax import lax
from jax.experimental import pallas as pl
from jax.experimental.pallas import tpu as pltpu
from jax.sharding import PartitionSpec as P

route_scale = 2.5
side = 4
gather_steps, exchange_steps = (3, 1, 2), (3, 2, 1)
extra = 128
bf16, f32 = jnp.bfloat16, jnp.float32
params = pltpu.CompilerParams(vmem_limit_bytes=16 * 2**20)
whole = pl.BlockSpec(memory_space=pltpu.VMEM)


def moved(place, step, along_x):
    y, x = place // side, place % side
    return y * side + (x ^ step) if along_x else (y ^ step) * side + x


def plane_shift(value, step, first_along_x):
    pairs = [
        (place * 2 + core, moved(place, step, first_along_x == (core == 0)) * 2 + core)
        for place in range(side * side)
        for core in range(2)
    ]
    return lax.ppermute(value, ("expert", "dp"), pairs)


def swapped(value):
    return lax.ppermute(value, "dp", [(0, 1), (1, 0)])


def position():
    core, spot = lax.axis_index("dp"), lax.axis_index("expert")
    y, x = spot >> 2, spot & 3
    return core, jnp.where(core == 0, x, y), jnp.where(core == 0, y, x)


def token_blocks(core, far):
    places = [far ^ step for step in (0,) + exchange_steps]
    return [
        jnp.where(core == 0, place * 4 + chunk, chunk * 4 + place)
        for place in places
        for chunk in range(side)
    ]


def select_kernel(*refs):
    blocks, outs = refs[:4], refs[4:]
    core, near, far = position()
    held = [near ^ step for step in (0,) + gather_steps]
    targets = [far ^ step for step in (0,) + exchange_steps]
    wanted = [jnp.where(core == 0, t * 2 + (near >> 1), near * 2 + (t >> 1)) for t in targets]
    tokens, width = blocks[0].shape
    width -= extra
    slots = outs[0].shape[0] // 4
    rows, columns = 4 * outs[0].shape[0], 4 * tokens

    def pick(index, values):
        return jnp.where(
            index < 2,
            jnp.where(index == 0, values[0], values[1]),
            jnp.where(index == 2, values[2], values[3]),
        )

    notes = jnp.concatenate([ref[:, width:] for ref in blocks], axis=0).astype(f32).T
    row = lax.broadcasted_iota(jnp.int32, (rows, 1), 0)
    column = lax.broadcasted_iota(jnp.int32, (1, columns), 1)
    expert = pick(row >> 6, wanted).astype(f32)
    same = ((row >> 4) & 3) == pick(column >> 5, held)
    named0 = same & (notes[0:1] == expert)
    named = named0 | (same & (notes[1:2] == expert))
    i = lax.broadcasted_iota(jnp.int32, (columns, columns), 0)
    j = lax.broadcasted_iota(jnp.int32, (columns, columns), 1)
    earlier = jnp.where((i < j) & ((i >> 5) == (j >> 5)), 1.0, 0.0).astype(bf16)
    marked = jnp.where(named, 1.0, 0.0).astype(bf16)
    place = jnp.dot(marked, earlier, preferred_element_type=f32)
    taken = jnp.where(named & (place == (row & 15).astype(f32)), 1.0, 0.0)
    weight = jnp.sum(
        taken * jnp.where(named0, notes[2:3], notes[3:4]), axis=1, keepdims=True
    )
    taken = taken.astype(bf16)

    def put(start, size, value):
        for index, out in enumerate(outs):
            out[:, start : start + size] = value[index * 4 * slots : (index + 1) * 4 * slots]

    put(width, extra, jnp.broadcast_to(weight, (rows, extra)).astype(bf16))
    step = 512 if width % 512 == 0 else width
    for start in range(0, width, step):
        chunk = jnp.concatenate([ref[:, start : start + step] for ref in blocks], axis=0)
        put(start, step, jnp.dot(taken, chunk, preferred_element_type=f32).astype(bf16))


def select_rows(blocks, slots):
    shape = jax.ShapeDtypeStruct((4 * slots, blocks[0].shape[1]), bf16)
    return pl.pallas_call(
        select_kernel,
        out_shape=(shape,) * 4,
        in_specs=[whole] * 4,
        out_specs=(whole,) * 4,
        compiler_params=params,
        name="select_rows",
    )(*blocks)


def factor_kernel(saved, swapped_saved, factors, later, hidden):
    slots = saved.shape[2] // 16
    span, near, far = position()
    order, order_other = token_blocks(span, far), token_blocks(1 - span, near)

    def loaded(ref, which, block):
        at = pl.ds(pl.multiple_of(block * slots, slots), slots)
        gate, up = ref[which, 0, at, :].astype(f32), ref[which, 1, at, :].astype(f32)
        sigma = jax.nn.sigmoid(gate)
        silu = gate * sigma
        return up * sigma * (1.0 + gate * (1.0 - sigma)), silu, (silu * up).astype(bf16)

    for chunk in range(16):
        here = slice(chunk * slots, (chunk + 1) * slots)
        factors[0, here, :] = loaded(swapped_saved, span, order[chunk])[2].astype(f32)
        gate, up, product = loaded(saved, span, order[chunk])
        factors[1, here, :] = product.astype(f32)
        factors[2, here, :] = gate
        factors[3, here, :] = up
        hidden[0, here, :] = product
        later[0, here, :], later[1, here, :], hidden[1, here, :] = loaded(
            saved, 1 - span, order_other[chunk]
        )


def saved_factors(saved, swapped_saved):
    shape = saved.shape[2:]
    return pl.pallas_call(
        factor_kernel,
        out_shape=(
            jax.ShapeDtypeStruct((4,) + shape, f32),
            jax.ShapeDtypeStruct((2,) + shape, f32),
            jax.ShapeDtypeStruct((2,) + shape, bf16),
        ),
        in_specs=[whole] * 2,
        out_specs=(whole,) * 3,
        compiler_params=params,
        name="saved_factors",
    )(saved, swapped_saved)


def slot_weights(notes, wide):
    return jnp.concatenate([notes.astype(f32)] * (wide // extra), axis=1)


def product_with(rows, weight):
    return lax.dot_general(
        rows, weight, (((1,), (1,)), ((), ())), preferred_element_type=f32
    )


def store_grads(out, raw, weights, gate, up, order):
    slots = raw.shape[0] // 16
    grad = weights * raw
    for part, factor in enumerate((gate, up)):
        value = (grad * factor).astype(bf16)
        for chunk in range(16):
            at = pl.ds(pl.multiple_of(order[chunk] * slots, slots), slots)
            out[part, at, :] = value[chunk * slots : (chunk + 1) * slots]


def raw_kernel(rows, mine, other, factors, grads, dots):
    count = rows.shape[0]
    width = rows.shape[1] - extra
    slots = count // 16
    core, _, far = position()
    order = token_blocks(core, far)
    raw_other = product_with(rows[:, :width], other[...])
    raw = product_with(rows[:, :width], mine[...])
    dot = jnp.sum(factors[0] * raw_other + factors[1] * raw, axis=1, keepdims=True)
    lane = lax.broadcasted_iota(jnp.int32, (count, 128), 1)
    row = lax.broadcasted_iota(jnp.int32, (count, 128), 0)
    spread = jnp.where(lane == (row & 15), dot, 0.0)
    for chunk in range(16):
        line = jnp.sum(spread[chunk * slots : (chunk + 1) * slots], axis=0, keepdims=True)
        for target in range(2):
            dots[pl.ds(order[chunk] * 2 + target, 1), :] = line
    weights = slot_weights(rows[:, width:], raw.shape[1])
    store_grads(grads, raw, weights, factors[2], factors[3], order)


def raw_grads(rows, mine, other, factors):
    return pl.pallas_call(
        raw_kernel,
        out_shape=(
            jax.ShapeDtypeStruct((2,) + factors.shape[1:], bf16),
            jax.ShapeDtypeStruct((32, 128), f32),
        ),
        in_specs=[whole] * 4,
        out_specs=(whole,) * 2,
        compiler_params=params,
        name="raw_grads",
    )(rows, mine, other, factors)


def finish_kernel(
    rows, notes, rows_other, notes_other, mine, hidden, later, grads, *refs
):
    tables, (pair_grads, weight_grad), passed = refs[:3], refs[3:5], refs[5:8]
    scaled, raw = refs[8:]
    count, wide = hidden.shape[1:]
    step = pl.program_id(0)
    span, near, _ = position()

    @pl.when(step == 0)
    def _():
        pair_grads[span] = grads[...]
        for table, out in zip(tables, passed, strict=True):
            out[...] = table[...]
        for index, ref in enumerate((notes, notes_other)):
            value = slot_weights(ref[...], wide) * hidden[index].astype(f32)
            scaled[:, index * count : (index + 1) * count] = value.T.astype(bf16)
        raw[...] = jnp.zeros_like(raw)

    total = jnp.dot(scaled[:, :count], rows[...], preferred_element_type=f32)
    total = total + jnp.dot(scaled[:, count:], rows_other[...], preferred_element_type=f32)
    weight_grad[...] = total.astype(bf16)
    columns = rows.shape[1]
    here = pl.ds(pl.multiple_of(step * columns, 128), columns)
    raw[...] += product_with(rows_other[...], mine[:, here])

    @pl.when(step == pl.num_programs(0) - 1)
    def _():
        store_grads(
            pair_grads.at[1 - span],
            raw[...],
            slot_weights(notes_other[...], wide),
            later[0],
            later[1],
            token_blocks(1 - span, near),
        )


def finished(rows, rows_other, mine, hidden, later, grads, tables):
    count, wide = hidden.shape[1:]
    width = rows.shape[1] - extra
    step = width // 2 if width % 256 == 0 else width

    def kept(value):
        return pl.BlockSpec(value.shape, lambda i: (0,) * len(value.shape))

    block = pl.BlockSpec((count, step), lambda i: (0, i))
    note = pl.BlockSpec((count, extra), lambda i: (0, width // extra))
    weight = pl.BlockSpec((wide, step), lambda i: (0, i))
    shapes = (
        jax.ShapeDtypeStruct((2,) + grads.shape, bf16),
        jax.ShapeDtypeStruct((wide, width), bf16),
        *(jax.ShapeDtypeStruct(table.shape, table.dtype) for table in tables),
    )
    inputs = (hidden, later, grads, *tables)
    return pl.pallas_call(
        finish_kernel,
        grid=(width // step,),
        out_shape=shapes,
        in_specs=[block, note, block, note, whole, *(kept(value) for value in inputs)],
        out_specs=(kept(shapes[0]), weight, *(kept(value) for value in shapes[2:])),
        scratch_shapes=[
            pltpu.VMEM((wide, 2 * count), bf16),
            pltpu.VMEM((count, wide), f32),
        ],
        compiler_params=params,
        name="finished",
    )(rows, rows, rows_other, rows_other, mine, *inputs)


def logit_kernel(returned, experts, places, scores, out):
    tokens = scores.shape[1]
    left, parts = returned[...], []
    for _ in range(3):
        parts.append(left.astype(bf16))
        left = left - parts[-1].astype(f32)
    spread = lax.dot_general(
        jnp.concatenate(parts, axis=0),
        experts[...],
        (((0,), (0,)), ((), ())),
        preferred_element_type=f32,
    )
    slots = places.shape[0]
    route = jnp.sum(spread[:slots] * places[...], axis=0, keepdims=True)
    for span in range(2):
        first, second = 2 * span, 2 * span + 1
        route0 = route[:, first * tokens : (first + 1) * tokens]
        route1 = route[:, second * tokens : (second + 1) * tokens]
        score0, score1 = scores[first : first + 1], scores[second : second + 1]
        total = score0 + score1
        mean = (route0 * score0 + route1 * score1) / total
        scale = route_scale / total
        out[first : first + 1] = scale * (route0 - mean) * score0 * (1.0 - score0)
        out[second : second + 1] = scale * (route1 - mean) * score1 * (1.0 - score1)


def note_kernel(ids, logits, notes, core, experts, places, scores):
    tokens = ids.shape[1]
    score = jax.nn.sigmoid(logits[...])
    scores[...] = score
    number = ids[...]
    line = jnp.concatenate([number[row : row + 1] for row in range(4)], axis=1)
    lane = lax.broadcasted_iota(jnp.int32, (1, 4 * tokens), 1)
    source = lax.broadcasted_iota(jnp.int32, (32, 4 * tokens), 0)
    span = lane >> 6
    table = jnp.where(((source >> 2) == line) & ((source & 1) == span), 1.0, 0.0)
    experts[...] = jnp.concatenate([table] * 3, axis=0).astype(bf16)
    expert = lax.broadcasted_iota(jnp.int32, (8, 4 * tokens), 0)
    marked = jnp.where(expert == line, 1.0, 0.0)
    i = lax.broadcasted_iota(jnp.int32, (4 * tokens, 4 * tokens), 0)
    j = lax.broadcasted_iota(jnp.int32, (4 * tokens, 4 * tokens), 1)
    earlier = jnp.where(((i >> 6) == (j >> 6)) & ((i & 31) < (j & 31)), 1.0, 0.0)
    before = jnp.dot(marked.astype(bf16), earlier.astype(bf16), preferred_element_type=f32)
    place = jnp.sum(before * marked, axis=0, keepdims=True)
    slot = lax.broadcasted_iota(jnp.int32, places.shape, 0).astype(f32)
    places[...] = jnp.where(slot == place, 1.0, 0.0)
    core[...] = jnp.broadcast_to(lax.axis_index("dp"), core.shape)
    first = lax.axis_index("dp") == 0
    pair = jnp.where(first, score[0:2], score[2:4])
    lines = [
        jnp.where(first, number[0:2], number[2:4]).astype(f32),
        route_scale * pair / (pair[0:1] + pair[1:2]),
        jnp.zeros((extra - 4, tokens), f32),
    ]
    table = jnp.concatenate(lines, axis=0)
    table = jnp.concatenate([table, jnp.zeros((extra, extra - tokens), f32)], axis=1)
    notes[...] = table.T[:tokens].astype(bf16)


def slot_notes(ids, logits):
    tokens = ids.shape[1]
    return pl.pallas_call(
        note_kernel,
        out_shape=(
            jax.ShapeDtypeStruct((tokens, extra), bf16),
            jax.ShapeDtypeStruct((tokens, 1), jnp.int32),
            jax.ShapeDtypeStruct((96, 4 * tokens), bf16),
            jax.ShapeDtypeStruct((16, 4 * tokens), f32),
            jax.ShapeDtypeStruct((4, tokens), f32),
        ),
        in_specs=[whole] * 2,
        out_specs=(whole,) * 5,
        compiler_params=params,
        name="slot_notes",
    )(ids, logits)


def local(sent_down, sent_up, expert_ids, router_logits, saved_gate_up, down_weight):
    saved = saved_gate_up[:, 0, 0]
    mine = down_weight[0, 0]
    slots = saved.shape[2] // 16
    tokens, top = expert_ids.shape[2:]

    def by_slot(value):
        return jnp.swapaxes(value[:, 0], 1, 2).reshape(2 * top, tokens)

    count = lax.axis_size("pipe")
    from_above = lax.ppermute(
        sent_down[0], ("pipe", "dp"), [(2 * z, 2 * z - 2) for z in range(1, count)]
    )
    from_below = lax.ppermute(
        sent_up[0], ("pipe", "dp"), [(2 * z + 1, 2 * z + 3) for z in range(count - 1)]
    )
    notes, core, experts, places, scores = slot_notes(
        by_slot(expert_ids), by_slot(router_logits)
    )
    notes, held = lax.optimization_barrier((notes, mine))
    other = swapped(held)
    incoming = jnp.where(core == 0, from_above, from_below)
    block = jnp.concatenate([incoming, notes], axis=1)
    block, swapped_saved = lax.optimization_barrier((block, swapped(saved)))

    blocks = [block] + [plane_shift(block, step, True) for step in gather_steps]
    factors, later, hidden = saved_factors(saved, swapped_saved)
    blocks[1], factors, later, hidden = lax.optimization_barrier(
        (blocks[1], factors, later, hidden)
    )
    pieces = select_rows(blocks, slots)
    pieces = [pieces[0]] + [
        plane_shift(piece, step, False)
        for piece, step in zip(pieces[1:], exchange_steps, strict=True)
    ]
    pieces[1], other = lax.optimization_barrier((pieces[1], other))
    rows = jnp.zeros((16 * slots, pieces[0].shape[1]), bf16)
    for index, piece in enumerate(pieces):
        rows = lax.dynamic_update_slice(rows, piece, (index * 4 * slots, 0))
    grads, dots = raw_grads(rows, mine, other, factors)
    returned = lax.all_to_all(dots, ("expert", "dp"), split_axis=0, concat_axis=0, tiled=True)
    pair_grads, weight_grad, experts, places, scores = finished(
        rows, swapped(rows), mine, hidden, later, grads, (experts, places, scores)
    )
    returned, pair_grads, weight_grad = lax.optimization_barrier(
        (returned, pair_grads, weight_grad)
    )
    logit_grads = pl.pallas_call(
        logit_kernel,
        out_shape=jax.ShapeDtypeStruct((2 * top, tokens), f32),
        in_specs=[whole] * 4,
        out_specs=whole,
        compiler_params=params,
        name="logit_grads",
    )(returned, experts, places, scores)
    return (
        pair_grads[:, None, None],
        weight_grad[None, None],
        jnp.swapaxes(logit_grads.reshape(2, 1, top, tokens), 2, 3),
    )


def solution(mesh):
    placed = (
        P("pipe", "expert", None),
        P("pipe", "expert", None),
        P(None, "pipe", "expert", None),
        P(None, "pipe", "expert", None),
        P(None, "pipe", "expert", None, None, "dp"),
        P("pipe", "expert", "dp", None),
    )
    return jax.shard_map(
        local,
        mesh=mesh,
        in_specs=placed,
        out_specs=(
            P(None, "pipe", "expert", None, None, "dp"),
            P("pipe", "expert", "dp", None),
            P(None, "pipe", "expert", None),
        ),
        check_vma=False,
    )
```

```python
import jax
import jax.numpy as jnp
from jax import lax
from jax.experimental import pallas as pl
from jax.experimental.pallas import tpu as pltpu
from jax.sharding import PartitionSpec as P

route_scale = 2.5
side = 4
gather_steps, exchange_steps = (2, 3, 1), (2, 3, 1)
extra = 128
bf16, f32 = jnp.bfloat16, jnp.float32
params = pltpu.CompilerParams(vmem_limit_bytes=16 * 2**20)
whole = pl.BlockSpec(memory_space=pltpu.VMEM)


def moved(place, step, along_x):
    y, x = place // side, place % side
    return y * side + (x ^ step) if along_x else (y ^ step) * side + x


def plane_shift(value, step, first_along_x):
    pairs = [
        (place * 2 + core, moved(place, step, first_along_x == (core == 0)) * 2 + core)
        for place in range(side * side)
        for core in range(2)
    ]
    return lax.ppermute(value, ("expert", "dp"), pairs)


def swapped(value):
    return lax.ppermute(value, "dp", [(0, 1), (1, 0)])


def position():
    core, spot = lax.axis_index("dp"), lax.axis_index("expert")
    y, x = spot >> 2, spot & 3
    return core, jnp.where(core == 0, x, y), jnp.where(core == 0, y, x)


def token_blocks(core, far):
    places = [far ^ step for step in (0,) + exchange_steps]
    return [
        jnp.where(core == 0, place * 4 + chunk, chunk * 4 + place)
        for place in places
        for chunk in range(side)
    ]


def select_kernel(*refs):
    blocks, outs = refs[:4], refs[4:]
    core, near, far = position()
    held = [near ^ step for step in (0,) + gather_steps]
    targets = [far ^ step for step in (0,) + exchange_steps]
    wanted = [jnp.where(core == 0, t * 2 + (near >> 1), near * 2 + (t >> 1)) for t in targets]
    tokens, width = blocks[0].shape
    width -= extra
    slots = outs[0].shape[0] // 4
    rows, columns = 4 * outs[0].shape[0], 4 * tokens

    def pick(index, values):
        return jnp.where(
            index < 2,
            jnp.where(index == 0, values[0], values[1]),
            jnp.where(index == 2, values[2], values[3]),
        )

    notes = jnp.concatenate([ref[:, width:] for ref in blocks], axis=0).astype(f32).T
    row = lax.broadcasted_iota(jnp.int32, (rows, 1), 0)
    column = lax.broadcasted_iota(jnp.int32, (1, columns), 1)
    expert = pick(row >> 6, wanted).astype(f32)
    same = ((row >> 4) & 3) == pick(column >> 5, held)
    named0 = same & (notes[0:1] == expert)
    named = named0 | (same & (notes[1:2] == expert))
    i = lax.broadcasted_iota(jnp.int32, (columns, columns), 0)
    j = lax.broadcasted_iota(jnp.int32, (columns, columns), 1)
    earlier = jnp.where((i < j) & ((i >> 5) == (j >> 5)), 1.0, 0.0).astype(bf16)
    marked = jnp.where(named, 1.0, 0.0).astype(bf16)
    place = jnp.dot(marked, earlier, preferred_element_type=f32)
    taken = jnp.where(named & (place == (row & 15).astype(f32)), 1.0, 0.0)
    weight = jnp.sum(
        taken * jnp.where(named0, notes[2:3], notes[3:4]), axis=1, keepdims=True
    )
    taken = taken.astype(bf16)

    def put(start, size, value):
        for index, out in enumerate(outs):
            out[:, start : start + size] = value[index * 4 * slots : (index + 1) * 4 * slots]

    put(width, extra, jnp.broadcast_to(weight, (rows, extra)).astype(bf16))
    step = 512 if width % 512 == 0 else width
    for start in range(0, width, step):
        chunk = jnp.concatenate([ref[:, start : start + step] for ref in blocks], axis=0)
        put(start, step, jnp.dot(taken, chunk, preferred_element_type=f32).astype(bf16))


def select_rows(blocks, slots):
    shape = jax.ShapeDtypeStruct((4 * slots, blocks[0].shape[1]), bf16)
    return pl.pallas_call(
        select_kernel,
        out_shape=(shape,) * 4,
        in_specs=[whole] * 4,
        out_specs=(whole,) * 4,
        compiler_params=params,
        name="select_rows",
    )(*blocks)


def factor_kernel(saved, swapped_saved, factors, later, hidden):
    slots = saved.shape[2] // 16
    span, near, far = position()
    order, order_other = token_blocks(span, far), token_blocks(1 - span, near)

    def loaded(ref, which, block):
        at = pl.ds(pl.multiple_of(block * slots, slots), slots)
        gate, up = ref[which, 0, at, :].astype(f32), ref[which, 1, at, :].astype(f32)
        sigma = jax.nn.sigmoid(gate)
        silu = gate * sigma
        return up * sigma * (1.0 + gate * (1.0 - sigma)), silu, (silu * up).astype(bf16)

    for chunk in range(16):
        here = slice(chunk * slots, (chunk + 1) * slots)
        factors[0, here, :] = loaded(swapped_saved, span, order[chunk])[2].astype(f32)
        gate, up, product = loaded(saved, span, order[chunk])
        factors[1, here, :] = product.astype(f32)
        factors[2, here, :] = gate
        factors[3, here, :] = up
        hidden[0, here, :] = product
        later[0, here, :], later[1, here, :], hidden[1, here, :] = loaded(
            saved, 1 - span, order_other[chunk]
        )


def saved_factors(saved, swapped_saved):
    shape = saved.shape[2:]
    return pl.pallas_call(
        factor_kernel,
        out_shape=(
            jax.ShapeDtypeStruct((4,) + shape, f32),
            jax.ShapeDtypeStruct((2,) + shape, f32),
            jax.ShapeDtypeStruct((2,) + shape, bf16),
        ),
        in_specs=[whole] * 2,
        out_specs=(whole,) * 3,
        compiler_params=params,
        name="saved_factors",
    )(saved, swapped_saved)


def slot_weights(notes, wide):
    return jnp.concatenate([notes.astype(f32)] * (wide // extra), axis=1)


def product_with(rows, weight):
    return lax.dot_general(
        rows, weight, (((1,), (1,)), ((), ())), preferred_element_type=f32
    )


def store_grads(out, raw, weights, gate, up, order):
    slots = raw.shape[0] // 16
    grad = weights * raw
    for part, factor in enumerate((gate, up)):
        value = (grad * factor).astype(bf16)
        for chunk in range(16):
            at = pl.ds(pl.multiple_of(order[chunk] * slots, slots), slots)
            out[part, at, :] = value[chunk * slots : (chunk + 1) * slots]


def raw_kernel(rows, mine, other, factors, grads, dots):
    count = rows.shape[0]
    width = rows.shape[1] - extra
    slots = count // 16
    core, _, far = position()
    order = token_blocks(core, far)
    raw_other = product_with(rows[:, :width], other[...])
    raw = product_with(rows[:, :width], mine[...])
    dot = jnp.sum(factors[0] * raw_other + factors[1] * raw, axis=1, keepdims=True)
    lane = lax.broadcasted_iota(jnp.int32, (count, 128), 1)
    row = lax.broadcasted_iota(jnp.int32, (count, 128), 0)
    spread = jnp.where(lane == (row & 15), dot, 0.0)
    for chunk in range(16):
        line = jnp.sum(spread[chunk * slots : (chunk + 1) * slots], axis=0, keepdims=True)
        for target in range(2):
            dots[pl.ds(order[chunk] * 2 + target, 1), :] = line
    weights = slot_weights(rows[:, width:], raw.shape[1])
    store_grads(grads, raw, weights, factors[2], factors[3], order)


def raw_grads(rows, mine, other, factors):
    return pl.pallas_call(
        raw_kernel,
        out_shape=(
            jax.ShapeDtypeStruct((2,) + factors.shape[1:], bf16),
            jax.ShapeDtypeStruct((32, 128), f32),
        ),
        in_specs=[whole] * 4,
        out_specs=(whole,) * 2,
        compiler_params=params,
        name="raw_grads",
    )(rows, mine, other, factors)


def finish_kernel(
    rows, notes, rows_other, notes_other, mine, hidden, later, grads, *refs
):
    tables, (pair_grads, weight_grad), passed = refs[:3], refs[3:5], refs[5:8]
    scaled, raw = refs[8:]
    count, wide = hidden.shape[1:]
    step = pl.program_id(0)
    span, near, _ = position()

    @pl.when(step == 0)
    def _():
        pair_grads[span] = grads[...]
        for table, out in zip(tables, passed, strict=True):
            out[...] = table[...]
        for index, ref in enumerate((notes, notes_other)):
            value = slot_weights(ref[...], wide) * hidden[index].astype(f32)
            scaled[:, index * count : (index + 1) * count] = value.T.astype(bf16)
        raw[...] = jnp.zeros_like(raw)

    total = jnp.dot(scaled[:, :count], rows[...], preferred_element_type=f32)
    total = total + jnp.dot(scaled[:, count:], rows_other[...], preferred_element_type=f32)
    weight_grad[...] = total.astype(bf16)
    columns = rows.shape[1]
    here = pl.ds(pl.multiple_of(step * columns, 128), columns)
    raw[...] += product_with(rows_other[...], mine[:, here])

    @pl.when(step == pl.num_programs(0) - 1)
    def _():
        store_grads(
            pair_grads.at[1 - span],
            raw[...],
            slot_weights(notes_other[...], wide),
            later[0],
            later[1],
            token_blocks(1 - span, near),
        )


def finished(rows, rows_other, mine, hidden, later, grads, tables):
    count, wide = hidden.shape[1:]
    width = rows.shape[1] - extra
    step = width // 2 if width % 256 == 0 else width

    def kept(value):
        return pl.BlockSpec(value.shape, lambda i: (0,) * len(value.shape))

    block = pl.BlockSpec((count, step), lambda i: (0, i))
    note = pl.BlockSpec((count, extra), lambda i: (0, width // extra))
    weight = pl.BlockSpec((wide, step), lambda i: (0, i))
    shapes = (
        jax.ShapeDtypeStruct((2,) + grads.shape, bf16),
        jax.ShapeDtypeStruct((wide, width), bf16),
        *(jax.ShapeDtypeStruct(table.shape, table.dtype) for table in tables),
    )
    inputs = (hidden, later, grads, *tables)
    return pl.pallas_call(
        finish_kernel,
        grid=(width // step,),
        out_shape=shapes,
        in_specs=[block, note, block, note, whole, *(kept(value) for value in inputs)],
        out_specs=(kept(shapes[0]), weight, *(kept(value) for value in shapes[2:])),
        scratch_shapes=[
            pltpu.VMEM((wide, 2 * count), bf16),
            pltpu.VMEM((count, wide), f32),
        ],
        compiler_params=params,
        name="finished",
    )(rows, rows, rows_other, rows_other, mine, *inputs)


def logit_kernel(returned, experts, places, scores, out):
    tokens = scores.shape[1]
    left, parts = returned[...], []
    for _ in range(3):
        parts.append(left.astype(bf16))
        left = left - parts[-1].astype(f32)
    spread = lax.dot_general(
        jnp.concatenate(parts, axis=0),
        experts[...],
        (((0,), (0,)), ((), ())),
        preferred_element_type=f32,
    )
    slots = places.shape[0]
    route = jnp.sum(spread[:slots] * places[...], axis=0, keepdims=True)
    for span in range(2):
        first, second = 2 * span, 2 * span + 1
        route0 = route[:, first * tokens : (first + 1) * tokens]
        route1 = route[:, second * tokens : (second + 1) * tokens]
        score0, score1 = scores[first : first + 1], scores[second : second + 1]
        total = score0 + score1
        mean = (route0 * score0 + route1 * score1) / total
        scale = route_scale / total
        out[first : first + 1] = scale * (route0 - mean) * score0 * (1.0 - score0)
        out[second : second + 1] = scale * (route1 - mean) * score1 * (1.0 - score1)


def note_kernel(ids, logits, notes, core, experts, places, scores):
    tokens = ids.shape[1]
    score = jax.nn.sigmoid(logits[...])
    scores[...] = score
    number = ids[...]
    line = jnp.concatenate([number[row : row + 1] for row in range(4)], axis=1)
    lane = lax.broadcasted_iota(jnp.int32, (1, 4 * tokens), 1)
    source = lax.broadcasted_iota(jnp.int32, (32, 4 * tokens), 0)
    span = lane >> 6
    table = jnp.where(((source >> 2) == line) & ((source & 1) == span), 1.0, 0.0)
    experts[...] = jnp.concatenate([table] * 3, axis=0).astype(bf16)
    expert = lax.broadcasted_iota(jnp.int32, (8, 4 * tokens), 0)
    marked = jnp.where(expert == line, 1.0, 0.0)
    i = lax.broadcasted_iota(jnp.int32, (4 * tokens, 4 * tokens), 0)
    j = lax.broadcasted_iota(jnp.int32, (4 * tokens, 4 * tokens), 1)
    earlier = jnp.where(((i >> 6) == (j >> 6)) & ((i & 31) < (j & 31)), 1.0, 0.0)
    before = jnp.dot(marked.astype(bf16), earlier.astype(bf16), preferred_element_type=f32)
    place = jnp.sum(before * marked, axis=0, keepdims=True)
    slot = lax.broadcasted_iota(jnp.int32, places.shape, 0).astype(f32)
    places[...] = jnp.where(slot == place, 1.0, 0.0)
    core[...] = jnp.broadcast_to(lax.axis_index("dp"), core.shape)
    first = lax.axis_index("dp") == 0
    pair = jnp.where(first, score[0:2], score[2:4])
    lines = [
        jnp.where(first, number[0:2], number[2:4]).astype(f32),
        route_scale * pair / (pair[0:1] + pair[1:2]),
        jnp.zeros((extra - 4, tokens), f32),
    ]
    table = jnp.concatenate(lines, axis=0)
    table = jnp.concatenate([table, jnp.zeros((extra, extra - tokens), f32)], axis=1)
    notes[...] = table.T[:tokens].astype(bf16)


def slot_notes(ids, logits):
    tokens = ids.shape[1]
    return pl.pallas_call(
        note_kernel,
        out_shape=(
            jax.ShapeDtypeStruct((tokens, extra), bf16),
            jax.ShapeDtypeStruct((tokens, 1), jnp.int32),
            jax.ShapeDtypeStruct((96, 4 * tokens), bf16),
            jax.ShapeDtypeStruct((16, 4 * tokens), f32),
            jax.ShapeDtypeStruct((4, tokens), f32),
        ),
        in_specs=[whole] * 2,
        out_specs=(whole,) * 5,
        compiler_params=params,
        name="slot_notes",
    )(ids, logits)


def local(sent_down, sent_up, expert_ids, router_logits, saved_gate_up, down_weight):
    saved = saved_gate_up[:, 0, 0]
    mine = down_weight[0, 0]
    slots = saved.shape[2] // 16
    tokens, top = expert_ids.shape[2:]

    def by_slot(value):
        return jnp.swapaxes(value[:, 0], 1, 2).reshape(2 * top, tokens)

    count = lax.axis_size("pipe")
    from_above = lax.ppermute(
        sent_down[0], ("pipe", "dp"), [(2 * z, 2 * z - 2) for z in range(1, count)]
    )
    from_below = lax.ppermute(
        sent_up[0], ("pipe", "dp"), [(2 * z + 1, 2 * z + 3) for z in range(count - 1)]
    )
    notes, core, experts, places, scores = slot_notes(
        by_slot(expert_ids), by_slot(router_logits)
    )
    notes, held = lax.optimization_barrier((notes, mine))
    other = swapped(held)
    incoming = jnp.where(core == 0, from_above, from_below)
    block = jnp.concatenate([incoming, notes], axis=1)
    block, swapped_saved = lax.optimization_barrier((block, swapped(saved)))

    blocks = [block] + [plane_shift(block, step, True) for step in gather_steps]
    factors, later, hidden = saved_factors(saved, swapped_saved)
    blocks[1], factors, later, hidden = lax.optimization_barrier(
        (blocks[1], factors, later, hidden)
    )
    pieces = select_rows(blocks, slots)
    pieces = [pieces[0]] + [
        plane_shift(piece, step, False)
        for piece, step in zip(pieces[1:], exchange_steps, strict=True)
    ]
    pieces[1], other = lax.optimization_barrier((pieces[1], other))
    rows = jnp.zeros((16 * slots, pieces[0].shape[1]), bf16)
    for index, piece in enumerate(pieces):
        rows = lax.dynamic_update_slice(rows, piece, (index * 4 * slots, 0))
    grads, dots = raw_grads(rows, mine, other, factors)
    returned = lax.all_to_all(dots, ("expert", "dp"), split_axis=0, concat_axis=0, tiled=True)
    pair_grads, weight_grad, experts, places, scores = finished(
        rows, swapped(rows), mine, hidden, later, grads, (experts, places, scores)
    )
    returned, pair_grads, weight_grad = lax.optimization_barrier(
        (returned, pair_grads, weight_grad)
    )
    logit_grads = pl.pallas_call(
        logit_kernel,
        out_shape=jax.ShapeDtypeStruct((2 * top, tokens), f32),
        in_specs=[whole] * 4,
        out_specs=whole,
        compiler_params=params,
        name="logit_grads",
    )(returned, experts, places, scores)
    return (
        pair_grads[:, None, None],
        weight_grad[None, None],
        jnp.swapaxes(logit_grads.reshape(2, 1, top, tokens), 2, 3),
    )


def solution(mesh):
    placed = (
        P("pipe", "expert", None),
        P("pipe", "expert", None),
        P(None, "pipe", "expert", None),
        P(None, "pipe", "expert", None),
        P(None, "pipe", "expert", None, None, "dp"),
        P("pipe", "expert", "dp", None),
    )
    return jax.shard_map(
        local,
        mesh=mesh,
        in_specs=placed,
        out_specs=(
            P(None, "pipe", "expert", None, None, "dp"),
            P("pipe", "expert", "dp", None),
            P(None, "pipe", "expert", None),
        ),
        check_vma=False,
    )
```

```python
import functools

import jax
import jax.numpy as jnp
from jax import lax
from jax.experimental import pallas as pl
from jax.experimental.pallas import tpu as pltpu
from jax.sharding import PartitionSpec as P

route_scale = 2.5
side = 4
gather_steps, exchange_steps = (2, 1, 3), (2, 3, 1)
extra = 128
bf16, f32 = jnp.bfloat16, jnp.float32
params = pltpu.CompilerParams(vmem_limit_bytes=16 * 2**20)
whole = pl.BlockSpec(memory_space=pltpu.VMEM)


def moved(place, step, along_x):
    y, x = place // side, place % side
    return y * side + (x ^ step) if along_x else (y ^ step) * side + x


def plane_shift(value, step, first_along_x):
    pairs = [
        (place * 2 + core, moved(place, step, first_along_x == (core == 0)) * 2 + core)
        for place in range(side * side)
        for core in range(2)
    ]
    return lax.ppermute(value, ("expert", "dp"), pairs)


def swapped(value):
    return lax.ppermute(value, "dp", [(0, 1), (1, 0)])


def position():
    core, spot = lax.axis_index("dp"), lax.axis_index("expert")
    y, x = spot >> 2, spot & 3
    return core, jnp.where(core == 0, x, y), jnp.where(core == 0, y, x)


def token_blocks(core, far):
    places = [far ^ step for step in (0,) + exchange_steps]
    return [
        jnp.where(core == 0, place * 4 + chunk, chunk * 4 + place)
        for place in places
        for chunk in range(side)
    ]


def select_kernel(steps, *refs):
    blocks, outs = refs[:4], refs[4:]
    core, near, far = position()
    held = [near ^ step for step in (0,) + gather_steps]
    targets = [far ^ step for step in (steps * 4)[:4]]
    wanted = [jnp.where(core == 0, t * 2 + (near >> 1), near * 2 + (t >> 1)) for t in targets]
    tokens, width = blocks[0].shape
    width -= extra
    slots = outs[0].shape[0] // 4
    rows, columns = len(steps) * outs[0].shape[0], 4 * tokens

    def pick(index, values):
        return jnp.where(
            index < 2,
            jnp.where(index == 0, values[0], values[1]),
            jnp.where(index == 2, values[2], values[3]),
        )

    notes = jnp.concatenate([ref[:, width:] for ref in blocks], axis=0).astype(f32).T
    row = lax.broadcasted_iota(jnp.int32, (rows, 1), 0)
    column = lax.broadcasted_iota(jnp.int32, (1, columns), 1)
    expert = pick(row >> 6, wanted).astype(f32)
    same = ((row >> 4) & 3) == pick(column >> 5, held)
    named0 = same & (notes[0:1] == expert)
    named = named0 | (same & (notes[1:2] == expert))
    i = lax.broadcasted_iota(jnp.int32, (columns, columns), 0)
    j = lax.broadcasted_iota(jnp.int32, (columns, columns), 1)
    earlier = jnp.where((i < j) & ((i >> 5) == (j >> 5)), 1.0, 0.0).astype(bf16)
    marked = jnp.where(named, 1.0, 0.0).astype(bf16)
    place = jnp.dot(marked, earlier, preferred_element_type=f32)
    taken = jnp.where(named & (place == (row & 15).astype(f32)), 1.0, 0.0)
    weight = jnp.sum(
        taken * jnp.where(named0, notes[2:3], notes[3:4]), axis=1, keepdims=True
    )
    taken = taken.astype(bf16)

    def put(start, size, value):
        for index, out in enumerate(outs):
            out[:, start : start + size] = value[index * 4 * slots : (index + 1) * 4 * slots]

    put(width, extra, jnp.broadcast_to(weight, (rows, extra)).astype(bf16))
    step = 512 if width % 512 == 0 else width
    for start in range(0, width, step):
        chunk = jnp.concatenate([ref[:, start : start + step] for ref in blocks], axis=0)
        put(start, step, jnp.dot(taken, chunk, preferred_element_type=f32).astype(bf16))


def select_rows(blocks, slots, steps):
    shape = jax.ShapeDtypeStruct((4 * slots, blocks[0].shape[1]), bf16)
    return pl.pallas_call(
        functools.partial(select_kernel, steps),
        out_shape=(shape,) * len(steps),
        in_specs=[whole] * 4,
        out_specs=(whole,) * len(steps),
        compiler_params=params,
        name="select_rows",
    )(*blocks)


def factor_kernel(saved, swapped_saved, factors, later, hidden):
    slots = saved.shape[2] // 16
    span, near, far = position()
    order, order_other = token_blocks(span, far), token_blocks(1 - span, near)

    def loaded(ref, which, block):
        at = pl.ds(pl.multiple_of(block * slots, slots), slots)
        gate, up = ref[which, 0, at, :].astype(f32), ref[which, 1, at, :].astype(f32)
        sigma = jax.nn.sigmoid(gate)
        silu = gate * sigma
        return up * sigma * (1.0 + gate * (1.0 - sigma)), silu, (silu * up).astype(bf16)

    for chunk in range(16):
        here = slice(chunk * slots, (chunk + 1) * slots)
        factors[0, here, :] = loaded(swapped_saved, span, order[chunk])[2].astype(f32)
        gate, up, product = loaded(saved, span, order[chunk])
        factors[1, here, :] = product.astype(f32)
        factors[2, here, :] = gate
        factors[3, here, :] = up
        hidden[0, here, :] = product
        later[0, here, :], later[1, here, :], hidden[1, here, :] = loaded(
            saved, 1 - span, order_other[chunk]
        )


def saved_factors(saved, swapped_saved):
    shape = saved.shape[2:]
    return pl.pallas_call(
        factor_kernel,
        out_shape=(
            jax.ShapeDtypeStruct((4,) + shape, f32),
            jax.ShapeDtypeStruct((2,) + shape, f32),
            jax.ShapeDtypeStruct((2,) + shape, bf16),
        ),
        in_specs=[whole] * 2,
        out_specs=(whole,) * 3,
        compiler_params=params,
        name="saved_factors",
    )(saved, swapped_saved)


def slot_weights(notes, wide):
    return jnp.concatenate([notes.astype(f32)] * (wide // extra), axis=1)


def product_with(rows, weight):
    return lax.dot_general(
        rows, weight, (((1,), (1,)), ((), ())), preferred_element_type=f32
    )


def store_grads(out, raw, weights, gate, up, order):
    slots = raw.shape[0] // 16
    grad = weights * raw
    for part, factor in enumerate((gate, up)):
        value = (grad * factor).astype(bf16)
        for chunk in range(16):
            at = pl.ds(pl.multiple_of(order[chunk] * slots, slots), slots)
            out[part, at, :] = value[chunk * slots : (chunk + 1) * slots]


def raw_kernel(rows, mine, other, factors, grads, dots):
    count = rows.shape[0]
    width = rows.shape[1] - extra
    slots = count // 16
    core, _, far = position()
    order = token_blocks(core, far)
    raw_other = product_with(rows[:, :width], other[...])
    raw = product_with(rows[:, :width], mine[...])
    dot = jnp.sum(factors[0] * raw_other + factors[1] * raw, axis=1, keepdims=True)
    lane = lax.broadcasted_iota(jnp.int32, (count, 128), 1)
    row = lax.broadcasted_iota(jnp.int32, (count, 128), 0)
    spread = jnp.where(lane == (row & 15), dot, 0.0)
    for chunk in range(16):
        line = jnp.sum(spread[chunk * slots : (chunk + 1) * slots], axis=0, keepdims=True)
        for target in range(2):
            dots[pl.ds(order[chunk] * 2 + target, 1), :] = line
    weights = slot_weights(rows[:, width:], raw.shape[1])
    store_grads(grads, raw, weights, factors[2], factors[3], order)


def raw_grads(rows, mine, other, factors):
    return pl.pallas_call(
        raw_kernel,
        out_shape=(
            jax.ShapeDtypeStruct((2,) + factors.shape[1:], bf16),
            jax.ShapeDtypeStruct((32, 128), f32),
        ),
        in_specs=[whole] * 4,
        out_specs=(whole,) * 2,
        compiler_params=params,
        name="raw_grads",
    )(rows, mine, other, factors)


def finish_kernel(
    rows, notes, rows_other, notes_other, mine, hidden, later, grads, *refs
):
    tables, (pair_grads, weight_grad), passed = refs[:3], refs[3:5], refs[5:8]
    scaled, raw = refs[8:]
    count, wide = hidden.shape[1:]
    step = pl.program_id(0)
    span, near, _ = position()

    @pl.when(step == 0)
    def _():
        pair_grads[span] = grads[...]
        for table, out in zip(tables, passed, strict=True):
            out[...] = table[...]
        for index, ref in enumerate((notes, notes_other)):
            value = slot_weights(ref[...], wide) * hidden[index].astype(f32)
            scaled[:, index * count : (index + 1) * count] = value.T.astype(bf16)
        raw[...] = jnp.zeros_like(raw)

    total = jnp.dot(scaled[:, :count], rows[...], preferred_element_type=f32)
    total = total + jnp.dot(scaled[:, count:], rows_other[...], preferred_element_type=f32)
    weight_grad[...] = total.astype(bf16)
    columns = rows.shape[1]
    here = pl.ds(pl.multiple_of(step * columns, 128), columns)
    raw[...] += product_with(rows_other[...], mine[:, here])

    @pl.when(step == pl.num_programs(0) - 1)
    def _():
        store_grads(
            pair_grads.at[1 - span],
            raw[...],
            slot_weights(notes_other[...], wide),
            later[0],
            later[1],
            token_blocks(1 - span, near),
        )


def finished(rows, rows_other, mine, hidden, later, grads, tables):
    count, wide = hidden.shape[1:]
    width = rows.shape[1] - extra
    step = width // 2 if width % 256 == 0 else width

    def kept(value):
        return pl.BlockSpec(value.shape, lambda i: (0,) * len(value.shape))

    block = pl.BlockSpec((count, step), lambda i: (0, i))
    note = pl.BlockSpec((count, extra), lambda i: (0, width // extra))
    weight = pl.BlockSpec((wide, step), lambda i: (0, i))
    shapes = (
        jax.ShapeDtypeStruct((2,) + grads.shape, bf16),
        jax.ShapeDtypeStruct((wide, width), bf16),
        *(jax.ShapeDtypeStruct(table.shape, table.dtype) for table in tables),
    )
    inputs = (hidden, later, grads, *tables)
    return pl.pallas_call(
        finish_kernel,
        grid=(width // step,),
        out_shape=shapes,
        in_specs=[block, note, block, note, whole, *(kept(value) for value in inputs)],
        out_specs=(kept(shapes[0]), weight, *(kept(value) for value in shapes[2:])),
        scratch_shapes=[
            pltpu.VMEM((wide, 2 * count), bf16),
            pltpu.VMEM((count, wide), f32),
        ],
        compiler_params=params,
        name="finished",
    )(rows, rows, rows_other, rows_other, mine, *inputs)


def logit_kernel(returned, experts, places, scores, out):
    tokens = scores.shape[1]
    left, parts = returned[...], []
    for _ in range(3):
        parts.append(left.astype(bf16))
        left = left - parts[-1].astype(f32)
    spread = lax.dot_general(
        jnp.concatenate(parts, axis=0),
        experts[...],
        (((0,), (0,)), ((), ())),
        preferred_element_type=f32,
    )
    slots = places.shape[0]
    route = jnp.sum(spread[:slots] * places[...], axis=0, keepdims=True)
    for span in range(2):
        first, second = 2 * span, 2 * span + 1
        route0 = route[:, first * tokens : (first + 1) * tokens]
        route1 = route[:, second * tokens : (second + 1) * tokens]
        score0, score1 = scores[first : first + 1], scores[second : second + 1]
        total = score0 + score1
        mean = (route0 * score0 + route1 * score1) / total
        scale = route_scale / total
        out[first : first + 1] = scale * (route0 - mean) * score0 * (1.0 - score0)
        out[second : second + 1] = scale * (route1 - mean) * score1 * (1.0 - score1)


def note_kernel(ids, logits, notes, core, experts, places, scores):
    tokens = ids.shape[1]
    score = jax.nn.sigmoid(logits[...])
    scores[...] = score
    number = ids[...]
    line = jnp.concatenate([number[row : row + 1] for row in range(4)], axis=1)
    lane = lax.broadcasted_iota(jnp.int32, (1, 4 * tokens), 1)
    source = lax.broadcasted_iota(jnp.int32, (32, 4 * tokens), 0)
    span = lane >> 6
    table = jnp.where(((source >> 2) == line) & ((source & 1) == span), 1.0, 0.0)
    experts[...] = jnp.concatenate([table] * 3, axis=0).astype(bf16)
    expert = lax.broadcasted_iota(jnp.int32, (8, 4 * tokens), 0)
    marked = jnp.where(expert == line, 1.0, 0.0)
    i = lax.broadcasted_iota(jnp.int32, (4 * tokens, 4 * tokens), 0)
    j = lax.broadcasted_iota(jnp.int32, (4 * tokens, 4 * tokens), 1)
    earlier = jnp.where(((i >> 6) == (j >> 6)) & ((i & 31) < (j & 31)), 1.0, 0.0)
    before = jnp.dot(marked.astype(bf16), earlier.astype(bf16), preferred_element_type=f32)
    place = jnp.sum(before * marked, axis=0, keepdims=True)
    slot = lax.broadcasted_iota(jnp.int32, places.shape, 0).astype(f32)
    places[...] = jnp.where(slot == place, 1.0, 0.0)
    core[...] = jnp.broadcast_to(lax.axis_index("dp"), core.shape)
    first = lax.axis_index("dp") == 0
    pair = jnp.where(first, score[0:2], score[2:4])
    lines = [
        jnp.where(first, number[0:2], number[2:4]).astype(f32),
        route_scale * pair / (pair[0:1] + pair[1:2]),
        jnp.zeros((extra - 4, tokens), f32),
    ]
    table = jnp.concatenate(lines, axis=0)
    table = jnp.concatenate([table, jnp.zeros((extra, extra - tokens), f32)], axis=1)
    notes[...] = table.T[:tokens].astype(bf16)


def slot_notes(ids, logits):
    tokens = ids.shape[1]
    return pl.pallas_call(
        note_kernel,
        out_shape=(
            jax.ShapeDtypeStruct((tokens, extra), bf16),
            jax.ShapeDtypeStruct((tokens, 1), jnp.int32),
            jax.ShapeDtypeStruct((96, 4 * tokens), bf16),
            jax.ShapeDtypeStruct((16, 4 * tokens), f32),
            jax.ShapeDtypeStruct((4, tokens), f32),
        ),
        in_specs=[whole] * 2,
        out_specs=(whole,) * 5,
        compiler_params=params,
        name="slot_notes",
    )(ids, logits)


def local(sent_down, sent_up, expert_ids, router_logits, saved_gate_up, down_weight):
    saved = saved_gate_up[:, 0, 0]
    mine = down_weight[0, 0]
    slots = saved.shape[2] // 16
    tokens, top = expert_ids.shape[2:]

    def by_slot(value):
        return jnp.swapaxes(value[:, 0], 1, 2).reshape(2 * top, tokens)

    count = lax.axis_size("pipe")
    from_above = lax.ppermute(
        sent_down[0], ("pipe", "dp"), [(2 * z, 2 * z - 2) for z in range(1, count)]
    )
    from_below = lax.ppermute(
        sent_up[0], ("pipe", "dp"), [(2 * z + 1, 2 * z + 3) for z in range(count - 1)]
    )
    notes, core, experts, places, scores = slot_notes(
        by_slot(expert_ids), by_slot(router_logits)
    )
    notes, held = lax.optimization_barrier((notes, mine))
    other = swapped(held)
    incoming = jnp.where(core == 0, from_above, from_below)
    block = jnp.concatenate([incoming, notes], axis=1)
    block, swapped_saved = lax.optimization_barrier((block, swapped(saved)))

    blocks = [block] + [plane_shift(block, step, True) for step in gather_steps]
    factors, later, hidden = saved_factors(saved, swapped_saved)
    blocks[1], factors, later, hidden = lax.optimization_barrier(
        (blocks[1], factors, later, hidden)
    )
    pieces = [
        plane_shift(piece, step, False)
        for piece, step in zip(
            select_rows(blocks, slots, exchange_steps), exchange_steps, strict=True
        )
    ]
    pieces[0], *blocks = lax.optimization_barrier((pieces[0], *blocks))
    pieces = [*select_rows(blocks, slots, (0,)), *pieces]
    pieces[1], other = lax.optimization_barrier((pieces[1], other))
    rows = jnp.zeros((16 * slots, pieces[0].shape[1]), bf16)
    for index, piece in enumerate(pieces):
        rows = lax.dynamic_update_slice(rows, piece, (index * 4 * slots, 0))
    grads, dots = raw_grads(rows, mine, other, factors)
    returned = lax.all_to_all(dots, ("expert", "dp"), split_axis=0, concat_axis=0, tiled=True)
    pair_grads, weight_grad, experts, places, scores = finished(
        rows, swapped(rows), mine, hidden, later, grads, (experts, places, scores)
    )
    returned, pair_grads, weight_grad = lax.optimization_barrier(
        (returned, pair_grads, weight_grad)
    )
    logit_grads = pl.pallas_call(
        logit_kernel,
        out_shape=jax.ShapeDtypeStruct((2 * top, tokens), f32),
        in_specs=[whole] * 4,
        out_specs=whole,
        compiler_params=params,
        name="logit_grads",
    )(returned, experts, places, scores)
    return (
        pair_grads[:, None, None],
        weight_grad[None, None],
        jnp.swapaxes(logit_grads.reshape(2, 1, top, tokens), 2, 3),
    )


def solution(mesh):
    placed = (
        P("pipe", "expert", None),
        P("pipe", "expert", None),
        P(None, "pipe", "expert", None),
        P(None, "pipe", "expert", None),
        P(None, "pipe", "expert", None, None, "dp"),
        P("pipe", "expert", "dp", None),
    )
    return jax.shard_map(
        local,
        mesh=mesh,
        in_specs=placed,
        out_specs=(
            P(None, "pipe", "expert", None, None, "dp"),
            P("pipe", "expert", "dp", None),
            P(None, "pipe", "expert", None),
        ),
        check_vma=False,
    )
```

```python
import functools

import jax
import jax.numpy as jnp
from jax import lax
from jax.experimental import pallas as pl
from jax.experimental.pallas import tpu as pltpu
from jax.sharding import PartitionSpec as P

route_scale = 2.5
side = 4
gather_steps, exchange_steps = (2, 1, 3), (2, 1, 3)
extra = 128
bf16, f32 = jnp.bfloat16, jnp.float32
params = pltpu.CompilerParams(vmem_limit_bytes=16 * 2**20)
whole = pl.BlockSpec(memory_space=pltpu.VMEM)


def moved(place, step, along_x):
    y, x = place // side, place % side
    return y * side + (x ^ step) if along_x else (y ^ step) * side + x


def plane_shift(value, step, first_along_x):
    pairs = [
        (place * 2 + core, moved(place, step, first_along_x == (core == 0)) * 2 + core)
        for place in range(side * side)
        for core in range(2)
    ]
    return lax.ppermute(value, ("expert", "dp"), pairs)


def swapped(value):
    return lax.ppermute(value, "dp", [(0, 1), (1, 0)])


def position():
    core, spot = lax.axis_index("dp"), lax.axis_index("expert")
    y, x = spot >> 2, spot & 3
    return core, jnp.where(core == 0, x, y), jnp.where(core == 0, y, x)


def token_blocks(core, far):
    places = [far ^ step for step in (0,) + exchange_steps]
    return [
        jnp.where(core == 0, place * 4 + chunk, chunk * 4 + place)
        for place in places
        for chunk in range(side)
    ]


def select_kernel(steps, *refs):
    blocks, outs = refs[:4], refs[4:]
    core, near, far = position()
    held = [near ^ step for step in (0,) + gather_steps]
    targets = [far ^ step for step in (steps * 4)[:4]]
    wanted = [jnp.where(core == 0, t * 2 + (near >> 1), near * 2 + (t >> 1)) for t in targets]
    tokens, width = blocks[0].shape
    width -= extra
    slots = outs[0].shape[0] // 4
    rows, columns = len(steps) * outs[0].shape[0], 4 * tokens

    def pick(index, values):
        return jnp.where(
            index < 2,
            jnp.where(index == 0, values[0], values[1]),
            jnp.where(index == 2, values[2], values[3]),
        )

    notes = jnp.concatenate([ref[:, width:] for ref in blocks], axis=0).astype(f32).T
    row = lax.broadcasted_iota(jnp.int32, (rows, 1), 0)
    column = lax.broadcasted_iota(jnp.int32, (1, columns), 1)
    expert = pick(row >> 6, wanted).astype(f32)
    same = ((row >> 4) & 3) == pick(column >> 5, held)
    named0 = same & (notes[0:1] == expert)
    named = named0 | (same & (notes[1:2] == expert))
    i = lax.broadcasted_iota(jnp.int32, (columns, columns), 0)
    j = lax.broadcasted_iota(jnp.int32, (columns, columns), 1)
    earlier = jnp.where((i < j) & ((i >> 5) == (j >> 5)), 1.0, 0.0).astype(bf16)
    marked = jnp.where(named, 1.0, 0.0).astype(bf16)
    place = jnp.dot(marked, earlier, preferred_element_type=f32)
    taken = jnp.where(named & (place == (row & 15).astype(f32)), 1.0, 0.0)
    weight = jnp.sum(
        taken * jnp.where(named0, notes[2:3], notes[3:4]), axis=1, keepdims=True
    )
    taken = taken.astype(bf16)

    def put(start, size, value):
        for index, out in enumerate(outs):
            out[:, start : start + size] = value[index * 4 * slots : (index + 1) * 4 * slots]

    put(width, extra, jnp.broadcast_to(weight, (rows, extra)).astype(bf16))
    step = 512 if width % 512 == 0 else width
    for start in range(0, width, step):
        chunk = jnp.concatenate([ref[:, start : start + step] for ref in blocks], axis=0)
        put(start, step, jnp.dot(taken, chunk, preferred_element_type=f32).astype(bf16))


def select_rows(blocks, slots, steps):
    shape = jax.ShapeDtypeStruct((4 * slots, blocks[0].shape[1]), bf16)
    return pl.pallas_call(
        functools.partial(select_kernel, steps),
        out_shape=(shape,) * len(steps),
        in_specs=[whole] * 4,
        out_specs=(whole,) * len(steps),
        compiler_params=params,
        name="select_rows",
    )(*blocks)


def factor_kernel(saved, swapped_saved, factors, later, hidden):
    slots = saved.shape[2] // 16
    span, near, far = position()
    order, order_other = token_blocks(span, far), token_blocks(1 - span, near)

    def loaded(ref, which, block):
        at = pl.ds(pl.multiple_of(block * slots, slots), slots)
        gate, up = ref[which, 0, at, :].astype(f32), ref[which, 1, at, :].astype(f32)
        sigma = jax.nn.sigmoid(gate)
        silu = gate * sigma
        return up * sigma * (1.0 + gate * (1.0 - sigma)), silu, (silu * up).astype(bf16)

    for chunk in range(16):
        here = slice(chunk * slots, (chunk + 1) * slots)
        factors[0, here, :] = loaded(swapped_saved, span, order[chunk])[2].astype(f32)
        gate, up, product = loaded(saved, span, order[chunk])
        factors[1, here, :] = product.astype(f32)
        factors[2, here, :] = gate
        factors[3, here, :] = up
        hidden[0, here, :] = product
        later[0, here, :], later[1, here, :], hidden[1, here, :] = loaded(
            saved, 1 - span, order_other[chunk]
        )


def saved_factors(saved, swapped_saved):
    shape = saved.shape[2:]
    return pl.pallas_call(
        factor_kernel,
        out_shape=(
            jax.ShapeDtypeStruct((4,) + shape, f32),
            jax.ShapeDtypeStruct((2,) + shape, f32),
            jax.ShapeDtypeStruct((2,) + shape, bf16),
        ),
        in_specs=[whole] * 2,
        out_specs=(whole,) * 3,
        compiler_params=params,
        name="saved_factors",
    )(saved, swapped_saved)


def slot_weights(notes, wide):
    return jnp.concatenate([notes.astype(f32)] * (wide // extra), axis=1)


def product_with(rows, weight):
    return lax.dot_general(
        rows, weight, (((1,), (1,)), ((), ())), preferred_element_type=f32
    )


def store_grads(out, raw, weights, gate, up, order):
    slots = raw.shape[0] // 16
    grad = weights * raw
    for part, factor in enumerate((gate, up)):
        value = (grad * factor).astype(bf16)
        for chunk in range(16):
            at = pl.ds(pl.multiple_of(order[chunk] * slots, slots), slots)
            out[part, at, :] = value[chunk * slots : (chunk + 1) * slots]


def raw_kernel(rows, mine, other, factors, grads, dots):
    count = rows.shape[0]
    width = rows.shape[1] - extra
    slots = count // 16
    core, _, far = position()
    order = token_blocks(core, far)
    raw_other = product_with(rows[:, :width], other[...])
    raw = product_with(rows[:, :width], mine[...])
    dot = jnp.sum(factors[0] * raw_other + factors[1] * raw, axis=1, keepdims=True)
    lane = lax.broadcasted_iota(jnp.int32, (count, 128), 1)
    row = lax.broadcasted_iota(jnp.int32, (count, 128), 0)
    spread = jnp.where(lane == (row & 15), dot, 0.0)
    for chunk in range(16):
        line = jnp.sum(spread[chunk * slots : (chunk + 1) * slots], axis=0, keepdims=True)
        for target in range(2):
            dots[pl.ds(order[chunk] * 2 + target, 1), :] = line
    weights = slot_weights(rows[:, width:], raw.shape[1])
    store_grads(grads, raw, weights, factors[2], factors[3], order)


def raw_grads(rows, mine, other, factors):
    return pl.pallas_call(
        raw_kernel,
        out_shape=(
            jax.ShapeDtypeStruct((2,) + factors.shape[1:], bf16),
            jax.ShapeDtypeStruct((32, 128), f32),
        ),
        in_specs=[whole] * 4,
        out_specs=(whole,) * 2,
        compiler_params=params,
        name="raw_grads",
    )(rows, mine, other, factors)


def finish_kernel(
    rows, notes, rows_other, notes_other, mine, hidden, later, grads, *refs
):
    tables, (pair_grads, weight_grad), passed = refs[:3], refs[3:5], refs[5:8]
    scaled, raw = refs[8:]
    count, wide = hidden.shape[1:]
    step = pl.program_id(0)
    span, near, _ = position()

    @pl.when(step == 0)
    def _():
        pair_grads[span] = grads[...]
        for table, out in zip(tables, passed, strict=True):
            out[...] = table[...]
        for index, ref in enumerate((notes, notes_other)):
            value = slot_weights(ref[...], wide) * hidden[index].astype(f32)
            scaled[:, index * count : (index + 1) * count] = value.T.astype(bf16)
        raw[...] = jnp.zeros_like(raw)

    total = jnp.dot(scaled[:, :count], rows[...], preferred_element_type=f32)
    total = total + jnp.dot(scaled[:, count:], rows_other[...], preferred_element_type=f32)
    weight_grad[...] = total.astype(bf16)
    columns = rows.shape[1]
    here = pl.ds(pl.multiple_of(step * columns, 128), columns)
    raw[...] += product_with(rows_other[...], mine[:, here])

    @pl.when(step == pl.num_programs(0) - 1)
    def _():
        store_grads(
            pair_grads.at[1 - span],
            raw[...],
            slot_weights(notes_other[...], wide),
            later[0],
            later[1],
            token_blocks(1 - span, near),
        )


def finished(rows, rows_other, mine, hidden, later, grads, tables):
    count, wide = hidden.shape[1:]
    width = rows.shape[1] - extra
    step = width // 2 if width % 256 == 0 else width

    def kept(value):
        return pl.BlockSpec(value.shape, lambda i: (0,) * len(value.shape))

    block = pl.BlockSpec((count, step), lambda i: (0, i))
    note = pl.BlockSpec((count, extra), lambda i: (0, width // extra))
    weight = pl.BlockSpec((wide, step), lambda i: (0, i))
    shapes = (
        jax.ShapeDtypeStruct((2,) + grads.shape, bf16),
        jax.ShapeDtypeStruct((wide, width), bf16),
        *(jax.ShapeDtypeStruct(table.shape, table.dtype) for table in tables),
    )
    inputs = (hidden, later, grads, *tables)
    return pl.pallas_call(
        finish_kernel,
        grid=(width // step,),
        out_shape=shapes,
        in_specs=[block, note, block, note, whole, *(kept(value) for value in inputs)],
        out_specs=(kept(shapes[0]), weight, *(kept(value) for value in shapes[2:])),
        scratch_shapes=[
            pltpu.VMEM((wide, 2 * count), bf16),
            pltpu.VMEM((count, wide), f32),
        ],
        compiler_params=params,
        name="finished",
    )(rows, rows, rows_other, rows_other, mine, *inputs)


def logit_kernel(returned, experts, places, scores, out):
    tokens = scores.shape[1]
    left, parts = returned[...], []
    for _ in range(3):
        parts.append(left.astype(bf16))
        left = left - parts[-1].astype(f32)
    spread = lax.dot_general(
        jnp.concatenate(parts, axis=0),
        experts[...],
        (((0,), (0,)), ((), ())),
        preferred_element_type=f32,
    )
    slots = places.shape[0]
    route = jnp.sum(spread[:slots] * places[...], axis=0, keepdims=True)
    for span in range(2):
        first, second = 2 * span, 2 * span + 1
        route0 = route[:, first * tokens : (first + 1) * tokens]
        route1 = route[:, second * tokens : (second + 1) * tokens]
        score0, score1 = scores[first : first + 1], scores[second : second + 1]
        total = score0 + score1
        mean = (route0 * score0 + route1 * score1) / total
        scale = route_scale / total
        out[first : first + 1] = scale * (route0 - mean) * score0 * (1.0 - score0)
        out[second : second + 1] = scale * (route1 - mean) * score1 * (1.0 - score1)


def note_kernel(ids, logits, notes, core, experts, places, scores):
    tokens = ids.shape[1]
    score = jax.nn.sigmoid(logits[...])
    scores[...] = score
    number = ids[...]
    line = jnp.concatenate([number[row : row + 1] for row in range(4)], axis=1)
    lane = lax.broadcasted_iota(jnp.int32, (1, 4 * tokens), 1)
    source = lax.broadcasted_iota(jnp.int32, (32, 4 * tokens), 0)
    span = lane >> 6
    table = jnp.where(((source >> 2) == line) & ((source & 1) == span), 1.0, 0.0)
    experts[...] = jnp.concatenate([table] * 3, axis=0).astype(bf16)
    expert = lax.broadcasted_iota(jnp.int32, (8, 4 * tokens), 0)
    marked = jnp.where(expert == line, 1.0, 0.0)
    i = lax.broadcasted_iota(jnp.int32, (4 * tokens, 4 * tokens), 0)
    j = lax.broadcasted_iota(jnp.int32, (4 * tokens, 4 * tokens), 1)
    earlier = jnp.where(((i >> 6) == (j >> 6)) & ((i & 31) < (j & 31)), 1.0, 0.0)
    before = jnp.dot(marked.astype(bf16), earlier.astype(bf16), preferred_element_type=f32)
    place = jnp.sum(before * marked, axis=0, keepdims=True)
    slot = lax.broadcasted_iota(jnp.int32, places.shape, 0).astype(f32)
    places[...] = jnp.where(slot == place, 1.0, 0.0)
    core[...] = jnp.broadcast_to(lax.axis_index("dp"), core.shape)
    first = lax.axis_index("dp") == 0
    pair = jnp.where(first, score[0:2], score[2:4])
    lines = [
        jnp.where(first, number[0:2], number[2:4]).astype(f32),
        route_scale * pair / (pair[0:1] + pair[1:2]),
        jnp.zeros((extra - 4, tokens), f32),
    ]
    table = jnp.concatenate(lines, axis=0)
    table = jnp.concatenate([table, jnp.zeros((extra, extra - tokens), f32)], axis=1)
    notes[...] = table.T[:tokens].astype(bf16)


def slot_notes(ids, logits):
    tokens = ids.shape[1]
    return pl.pallas_call(
        note_kernel,
        out_shape=(
            jax.ShapeDtypeStruct((tokens, extra), bf16),
            jax.ShapeDtypeStruct((tokens, 1), jnp.int32),
            jax.ShapeDtypeStruct((96, 4 * tokens), bf16),
            jax.ShapeDtypeStruct((16, 4 * tokens), f32),
            jax.ShapeDtypeStruct((4, tokens), f32),
        ),
        in_specs=[whole] * 2,
        out_specs=(whole,) * 5,
        compiler_params=params,
        name="slot_notes",
    )(ids, logits)


def local(sent_down, sent_up, expert_ids, router_logits, saved_gate_up, down_weight):
    saved = saved_gate_up[:, 0, 0]
    mine = down_weight[0, 0]
    slots = saved.shape[2] // 16
    tokens, top = expert_ids.shape[2:]

    def by_slot(value):
        return jnp.swapaxes(value[:, 0], 1, 2).reshape(2 * top, tokens)

    count = lax.axis_size("pipe")
    from_above = lax.ppermute(
        sent_down[0], ("pipe", "dp"), [(2 * z, 2 * z - 2) for z in range(1, count)]
    )
    from_below = lax.ppermute(
        sent_up[0], ("pipe", "dp"), [(2 * z + 1, 2 * z + 3) for z in range(count - 1)]
    )
    notes, core, experts, places, scores = slot_notes(
        by_slot(expert_ids), by_slot(router_logits)
    )
    notes, held = lax.optimization_barrier((notes, mine))
    other = swapped(held)
    incoming = jnp.where(core == 0, from_above, from_below)
    block = jnp.concatenate([incoming, notes], axis=1)
    block, swapped_saved = lax.optimization_barrier((block, swapped(saved)))

    blocks = [block] + [plane_shift(block, step, True) for step in gather_steps]
    factors, later, hidden = saved_factors(saved, swapped_saved)
    blocks[1], factors, later, hidden = lax.optimization_barrier(
        (blocks[1], factors, later, hidden)
    )
    pieces = [
        plane_shift(piece, step, False)
        for piece, step in zip(
            select_rows(blocks, slots, exchange_steps), exchange_steps, strict=True
        )
    ]
    pieces[0], *blocks = lax.optimization_barrier((pieces[0], *blocks))
    pieces = [*select_rows(blocks, slots, (0,)), *pieces]
    pieces[1], other = lax.optimization_barrier((pieces[1], other))
    rows = jnp.zeros((16 * slots, pieces[0].shape[1]), bf16)
    for index, piece in enumerate(pieces):
        rows = lax.dynamic_update_slice(rows, piece, (index * 4 * slots, 0))
    grads, dots = raw_grads(rows, mine, other, factors)
    returned = lax.all_to_all(dots, ("expert", "dp"), split_axis=0, concat_axis=0, tiled=True)
    pair_grads, weight_grad, experts, places, scores = finished(
        rows, swapped(rows), mine, hidden, later, grads, (experts, places, scores)
    )
    returned, pair_grads, weight_grad = lax.optimization_barrier(
        (returned, pair_grads, weight_grad)
    )
    logit_grads = pl.pallas_call(
        logit_kernel,
        out_shape=jax.ShapeDtypeStruct((2 * top, tokens), f32),
        in_specs=[whole] * 4,
        out_specs=whole,
        compiler_params=params,
        name="logit_grads",
    )(returned, experts, places, scores)
    return (
        pair_grads[:, None, None],
        weight_grad[None, None],
        jnp.swapaxes(logit_grads.reshape(2, 1, top, tokens), 2, 3),
    )


def solution(mesh):
    placed = (
        P("pipe", "expert", None),
        P("pipe", "expert", None),
        P(None, "pipe", "expert", None),
        P(None, "pipe", "expert", None),
        P(None, "pipe", "expert", None, None, "dp"),
        P("pipe", "expert", "dp", None),
    )
    return jax.shard_map(
        local,
        mesh=mesh,
        in_specs=placed,
        out_specs=(
            P(None, "pipe", "expert", None, None, "dp"),
            P("pipe", "expert", "dp", None),
            P(None, "pipe", "expert", None),
        ),
        check_vma=False,
    )
```
